32 devices in a mesh: tm: 2 (over x), space: 16 (over z, y, core).
Axes of the slice: x: 2, y: 2, z: 4, core: 2. Of those that a mesh axis runs over, the one named last changes fastest.
Arguments:
- panels_in: float32 [32, 8192], P(None, 'space'), may hold values from -120 to 120
- blocks: float32 [4, 128, 3, 4096], P('tm', 'space'), may hold values from -0.4375 to 0.4375
- block_mask: int32 [4, 128, 3], P('tm', 'space'), may hold values 0 or 1
- mixing: float32 [4, 4, 8, 8], P('tm'), may hold values from -0.6 to 0.6
Outputs:
- forward_states: float32 [2, 32, 8192], P('tm', None, 'space')
- adjoint_states: float32 [2, 32, 8192], P('tm', None, 'space')
The draws below stay inside these ranges and needn't reach their ends.
All inputs are finite; a program needn't handle non-finite values. No bound on the sum of `block_mask` on one device may be relied on, other than what follows from the above.
Results may differ from the reference program's by a relative error of at most 0.0003.
Values sent between devices are 32-bit elements; how exact they have to be, the bound alone decides.
No kernel may reach another device: no remote copies, remote signals or barrier semaphores. Data moves between devices by JAX's collectives and lax.ppermute only.
A program may use at most 64 MiB of HBM per device.

```python
import jax
import jax.numpy as jnp
from jax import lax

BLOCK = 64
COLS = 8
PANELS = 4
TRANSFER_RUN = 2
STEPS = 4
NBOX = 8192
NBLK = 128
N_TM = 2


def draw_panels_in(key, part):
    subkeys = jax.random.split(key, 3)
    row_count = NBOX
    width_all = PANELS * COLS
    position = jnp.arange(row_count, dtype=jnp.float32) / row_count
    rising = jnp.exp(jnp.log(3.0) * position)
    row_scale = jnp.exp(jnp.log(10.0) * (jax.random.uniform(subkeys[0], (row_count,), jnp.float32) - 0.5))
    col_scale = jnp.exp(jnp.log(10.0) * (jax.random.uniform(subkeys[1], (width_all, 1), jnp.float32) - 0.5))
    values_base = jax.random.truncated_normal(subkeys[2], -4.0, 4.0, (width_all, row_count), jnp.float32)
    return (values_base * row_scale[None, :] * col_scale * rising[None, :]).astype(jnp.float32)


def with_ends(drawn, stream_key, smallest, high):
    spot = [jax.random.randint(jax.random.fold_in(stream_key, axis), (), 0, length) for axis, length in enumerate(drawn.shape)]
    main_axis = drawn.shape.index(max(drawn.shape))
    neighbour = spot[:main_axis] + [(spot[main_axis] + 1) % drawn.shape[main_axis]] + spot[main_axis + 1:]
    return drawn.at[tuple(spot)].set(smallest).at[tuple(neighbour)].set(high)


def levels(rng, extent, cuts, least, high):
    def one(dim, parts):
        heights = jax.random.uniform(jax.random.fold_in(jax.random.fold_in(rng, 6), dim), (parts,), jnp.float32, least / len(cuts), high / len(cuts))
        return jnp.repeat(jnp.exp(heights), extent[dim] // parts).reshape((-1,) + (1,) * (len(extent) - dim - 1))

    level = one(*cuts[0])
    for cut in cuts[1:]:
        level = level * one(*cut)
    return level


def normal_values(key, shape, spread, most, cuts=(), kind=jnp.bfloat16):
    entries = jax.random.normal(key, shape, jnp.float32) * spread
    if len(cuts) > 0:
        entries = levels(key, shape, cuts, -0.22, 0.18) * entries
    return jnp.clip(entries, min=-most, max=most).astype(kind)


def setup_inputs(seed: int = 0) -> dict:
    key_list = jax.random.split(jax.random.key(seed), 5)
    return {
        "panels_in": draw_panels_in(jax.random.fold_in(key_list[4], 71), 0),
        "blocks": normal_values(key_list[1], (STEPS, NBLK, 3, BLOCK * BLOCK), (3 * BLOCK) ** -0.5, 0.4375, ((0, 2), (1, 16)), jnp.float32),
        "block_mask": with_ends((jax.random.randint(key_list[2], (STEPS, NBLK, 3), 0, 4) < 3).astype(jnp.int32), jax.random.fold_in(key_list[2], 1), 0, 1),
        "mixing": normal_values(key_list[3], (STEPS, PANELS, COLS, COLS), 0.15, 0.6, ((0, 2),), jnp.float32),
    }


def push_step(blocks_here, mask_here, current):
    count_blocks = current.shape[1] // BLOCK
    reshaped_block = current.reshape(current.shape[0], count_blocks, BLOCK)
    padded = jnp.pad(reshaped_block, ((0, 0), (1, 1), (0, 0)))
    mask_float = mask_here.astype(jnp.float32)
    pieces = jnp.stack([padded[:, offset:offset + count_blocks] for offset in range(3)], axis=2)
    pieces = pieces * mask_float[None, :, :, None]
    matrices = blocks_here.reshape(count_blocks, 3, BLOCK, BLOCK)
    result = jnp.einsum('bjik,cbjk->cbi', matrices, pieces, precision=lax.Precision.HIGHEST)
    return result.reshape(current.shape[0], count_blocks * BLOCK)

def pull_step(blocks_here, mask_here, current):
    count_blocks = current.shape[1] // BLOCK
    reshaped_block = current.reshape(current.shape[0], count_blocks, BLOCK)
    matrices = blocks_here.reshape(count_blocks, 3, BLOCK, BLOCK)
    products = jnp.einsum('bjik,cbi->cbjk', matrices, reshaped_block, precision=lax.Precision.HIGHEST)
    products = products * mask_here.astype(jnp.float32)[None, :, :, None]
    first_part = products[:, :, 0]
    middle_part = products[:, :, 1]
    last_part = products[:, :, 2]
    result = middle_part + jnp.pad(first_part[:, 1:], ((0, 0), (0, 1), (0, 0))) + jnp.pad(last_part[:, :-1], ((0, 0), (1, 0), (0, 0)))
    return result.reshape(current.shape[0], count_blocks * BLOCK)

def mix_columns(working, expansion_weights):
    panel_count = expansion_weights.shape[0]
    reshaped_block = working.reshape(panel_count, COLS, working.shape[1])
    blended_panel = jnp.einsum('yit,yif->ytf', expansion_weights, reshaped_block, precision=lax.Precision.HIGHEST)
    return working - blended_panel.reshape(working.shape)

def rescale(current):
    squares = lax.optimization_barrier(jnp.mean(current * current, axis=1, keepdims=True))
    return current / jnp.sqrt(squares + 1e-06)

def reference(panels_in, blocks, block_mask, mixing):
    current = panels_in
    forward_list = []
    for pair_index in range(N_TM):
        for offset in range(TRANSFER_RUN):
            step_index = pair_index * TRANSFER_RUN + offset
            current = mix_columns(push_step(blocks[step_index], block_mask[step_index], current), mixing[step_index])
        current = rescale(current)
        forward_list.append(current)
    adjoint_list = [None] * N_TM
    for pair_index in range(N_TM - 1, -1, -1):
        for offset in range(TRANSFER_RUN - 1, -1, -1):
            step_index = pair_index * TRANSFER_RUN + offset
            current = mix_columns(pull_step(blocks[step_index], block_mask[step_index], current), mixing[step_index])
        current = rescale(current)
        adjoint_list[pair_index] = current
    return (jnp.stack(forward_list), jnp.stack(adjoint_list))
```

```python
import functools

import jax
import jax.numpy as jnp
from jax import lax
from jax.experimental import pallas as pl
from jax.experimental.pallas import tpu as pltpu
from jax.sharding import PartitionSpec as P

BLOCK = 64
COLS = 8
PANELS = 4
ROWS = COLS * PANELS
RUN = 2
GROUP = 4
RIM_A = 5
RIM_B = 4
DOWN = 2.0**-16
BF = jnp.bfloat16
F32 = jnp.float32
HIGH = lax.Precision.HIGHEST
NT = (((1,), (1,)), ((), ()))
NN = (((1,), (0,)), ((), ()))
TN = (((0,), (0,)), ((), ()))
VM = pl.BlockSpec(memory_space=pltpu.VMEM)


def call(kernel, outs, args, scratch=(), flops=10**6):
    shapes = [jax.ShapeDtypeStruct(shape, dtype) for shape, dtype in outs]
    return pl.pallas_call(
        kernel,
        out_shape=shapes,
        in_specs=[VM] * len(args),
        out_specs=[VM] * len(outs),
        scratch_shapes=list(scratch),
        compiler_params=pltpu.CompilerParams(vmem_limit_bytes=12 << 20),
        cost_estimate=pl.CostEstimate(flops=flops, bytes_accessed=10**6, transcendentals=0),
    )(*args)


def inside():
    place, last = lax.axis_index("space"), lax.axis_size("space") - 1
    return jnp.where((place == 0) | (place == last), 0.0, 1.0).astype(F32)


def parity():
    return lax.rem(lax.axis_index("space"), 2)


def iota(shape, dim):
    return lax.broadcasted_iota(jnp.int32, shape, dim)


def edge_kernel(nb, blocks, mask, panels, to_a, to_b):
    width = panels.shape[1]

    def emit(dst, row, start, keep=1.0):
        for j in range(3):
            line = blocks[0, j, row : row + 1, :] * (mask[0, j, row : row + 1, 0:1] * keep)
            for r in range(32):
                dst[j * 32 + r : j * 32 + r + 1, :] = line[:, r * 128 : (r + 1) * 128]
        dst[96:128, :] = panels[:, start : start + 128]

    @pl.when(parity() == 0)
    def _():
        emit(to_a, nb - 1, width - 128)
        emit(to_b, 0, 0, inside())

    @pl.when(parity() == 1)
    def _():
        emit(to_a, 0, 0)
        emit(to_b, nb - 1, width - 128, inside())


def far_kernel(nb, blocks, mask, to_a, to_b):
    def emit(dst, row_a, row_b, keep=1.0):
        for j in range(3):
            for r in range(32):
                lanes = slice(r * 128, (r + 1) * 128)
                va = blocks[0, j, :, lanes] * (mask[0, j] * keep)
                vb = blocks[1, j, :, lanes] * (mask[1, j] * keep)
                dst[pl.ds(j * 32 + r, RIM_A - 1, stride=96), :] = va[row_a : row_a + RIM_A - 1]
                dst[pl.ds(96 * (RIM_A - 1) + j * 32 + r, RIM_B, stride=96), :] = vb[row_b : row_b + RIM_B]

    @pl.when(parity() == 0)
    def _():
        emit(to_a, nb - RIM_A, nb - RIM_B)
        emit(to_b, 1, 0, inside())

    @pl.when(parity() == 1)
    def _():
        emit(to_a, 1, 0)
        emit(to_b, nb - RIM_A, nb - RIM_B, inside())


def banded(y, p):
    low = iota(y[0].shape, 1) < BLOCK
    zero = jnp.zeros_like(y[0])
    turned = [pltpu.roll(v, BLOCK, 1) for v in y]
    at_low, at_high = (y, turned) if p == 0 else (turned, y)
    first = (jnp.where(low, at_low[0], at_high[1]), jnp.where(low, at_low[2], zero))
    second = (jnp.where(low, zero, at_high[0]), jnp.where(low, at_low[1], at_high[2]))
    return first, second


def split2(x):
    high = x.astype(BF)
    return high, (x - high.astype(F32)).astype(BF)


def split_halves(wide, at, hi, lo):
    for half in range(2):
        lanes = slice(half * 128, half * 128 + 128)
        hi[:, lanes], lo[:, lanes] = split2(wide[at + half])


def own_kernel(nb, blocks, mask, mixing, a_hi, a_lo, b_hi, b_lo, expand, wide):
    for t, hi, lo in ((0, a_hi, a_lo), (1, b_hi, b_lo)):
        is_first = lax.rem(iota((nb, 128), 0), 2) == (1 - t)
        for r in range(32):
            lanes = slice(r * 128, (r + 1) * 128)
            y = [blocks[t, j, :, lanes] * mask[t, j] for j in range(3)]
            for p in range(2):
                first, second = banded(y, p)
                for half in range(2):
                    wide[2 * t + half, pl.ds(2 * r + p, nb, stride=BLOCK), :] = jnp.where(
                        is_first, first[half], second[half]
                    )
        split_halves(wide, 2 * t, hi, lo)
    pick = (lax.rem(iota((COLS, 128), 1), COLS) == iota((COLS, 128), 0)).astype(F32)
    row, lane = iota((ROWS, 128), 0), lax.rem(iota((ROWS, 128), 1), ROWS)
    same = (row // COLS) == (lane // COLS)
    step = []
    for t in range(RUN):
        m = mixing[t].reshape(ROWS, COLS)
        spread = lax.dot_general(m, pick, NN, precision=HIGH, preferred_element_type=F32)
        step.append((row == lane).astype(F32) - jnp.where(same, spread, 0.0))
    for i, (x, y) in enumerate(((step[0], step[1]), (step[1], step[0]))):
        e = lax.dot_general(x[:, :ROWS], y, NN, precision=HIGH, preferred_element_type=F32)
        expand[i * COLS : (i + 1) * COLS, :] = (
            e[0:COLS] + e[COLS : 2 * COLS] + e[2 * COLS : 3 * COLS] + e[3 * COLS :]
        )


def rim_row(dst, index, first, from_a, from_b, base, left):
    use_b = (parity() == 0) == left
    y = []
    for j in range(3):
        rows = slice(base + j * 32, base + j * 32 + 32)
        y.append(jnp.where(use_b, from_b[rows, :], from_a[rows, :]))
    for p in range(2):
        tiles = banded(y, p)[0 if first else 1]
        for half in range(2):
            dst[half, pl.ds(index * BLOCK + p, 32, stride=2), :] = tiles[half]


def rim_kernel(near_a, near_b, far_a, far_b, a_hi, a_lo, b_hi, b_lo, wide_a, wide_b):
    for i in range(RIM_A - 1):
        rim_row(wide_a, i, (RIM_A - i) % 2 == 1, far_a, far_b, i * 96, True)
        rim_row(wide_a, RIM_A + 1 + i, i % 2 == 0, far_a, far_b, i * 96, False)
    rim_row(wide_a, RIM_A - 1, True, near_a, near_b, 0, True)
    rim_row(wide_a, RIM_A, False, near_a, near_b, 0, False)
    for i in range(RIM_B):
        base = (RIM_A - 1 + i) * 96
        rim_row(wide_b, i, (RIM_B - i) % 2 == 0, far_a, far_b, base, True)
        rim_row(wide_b, RIM_B + i, i % 2 == 0, far_a, far_b, base, False)
    split_halves(wide_a, 0, a_hi, a_lo)
    split_halves(wide_b, 0, b_hi, b_lo)


def pair_tile(own, rim, depth, nb, b):
    def row(k):
        if 0 <= k < nb:
            return own[k * BLOCK : (k + 1) * BLOCK, :]
        k = k + depth if k < 0 else depth + k - nb
        return rim[k * BLOCK : (k + 1) * BLOCK, :]

    return jnp.concatenate([row(b), row(b + 1)], axis=0)


def product(x, w, dims):
    o = lax.dot_general(x, w, dims, preferred_element_type=F32)
    return (o[ROWS:, 128:] + o[ROWS:, :128] + o[:ROWS, 128:]) + o[:ROWS, :128]


def push(v, tiles):
    x = jnp.concatenate(split2(v), axis=0)
    outs = []
    for i, (hi, lo) in enumerate(tiles):
        outs.append(product(x[:, i * 128 : i * 128 + 256], jnp.concatenate([hi, lo], axis=0), NT))
    return jnp.concatenate(outs, axis=1)


def pull(v, tiles):
    x = jnp.concatenate(split2(v), axis=0)
    outs = []
    for i in range(len(tiles) - 1):
        parts = [
            jnp.concatenate([tiles[i][s][:, 128:], tiles[i + 1][s][:, :128]], axis=0) for s in range(2)
        ]
        outs.append(product(x[:, i * 128 : i * 128 + 256], jnp.concatenate(parts, axis=1), NN))
    return jnp.concatenate(outs, axis=1)


def tiles_of(refs, depth, nb, first, last):
    own_hi, own_lo, rim_hi, rim_lo = refs
    return [
        (pair_tile(own_hi, rim_hi, depth, nb, b), pair_tile(own_lo, rim_lo, depth, nb, b))
        for b in range(first, last, 2)
    ]


def gram(u):
    u1, rest = u.astype(BF), u
    rest = rest - u1.astype(F32)
    u2 = rest.astype(BF)
    u3 = (rest - u2.astype(F32)).astype(BF)
    stack = jnp.concatenate([u3, u2, u1], axis=0)
    total = None
    for part in (u3, u2, u1):
        g = lax.dot_general(stack, jnp.concatenate([part] * 4, axis=0), NT, preferred_element_type=F32)
        g = (g[:ROWS] + g[ROWS : 2 * ROWS]) + g[2 * ROWS :]
        total = g if total is None else total + g
    panel = lax.rem(iota((COLS, 128), 1), ROWS) // COLS
    out = jnp.zeros((COLS, 128), F32)
    for p in range(PANELS):
        out = out + jnp.where(panel == p, total[p * COLS : (p + 1) * COLS], 0.0)
    return out


def noted(meta, slot, g, e):
    mine = (iota((COLS, 128), 1) // ROWS) == slot
    return jnp.concatenate(
        [jnp.where(mine, g, meta[:COLS]), jnp.where(mine, e, meta[COLS : 2 * COLS]), meta[2 * COLS :]], axis=0
    )


def by_side(e_a, e_b):
    even = parity() == 0
    return jnp.where(even, e_b, e_a), jnp.where(even, e_a, e_b)


def push_kernel(nb, owner, slot, reach, old, main, edge_a, edge_b, near_a, near_b, a_hi, a_lo, b_hi, b_lo, expand,
                out, out_a, out_b, meta, wide):
    own = nb * BLOCK

    @pl.when(lax.axis_index("tm") != owner)
    def _():
        meta[...] = old[...]

    @pl.when(lax.axis_index("tm") == owner)
    def _():
        rim_row(wide, 0, True, near_a, near_b, 0, True)
        rim_row(wide, 1, False, near_a, near_b, 0, False)
        rim_hi, rim_lo = split2(jnp.concatenate([wide[0], wide[1]], axis=1))
        w_edge = edge_a.shape[1]
        left, right = by_side(edge_a[...], edge_b[...])
        v = jnp.concatenate([left[:, w_edge - 128 :], main[:, :own], right[:, :128]], axis=1)
        w = push(v, tiles_of((a_hi, a_lo, rim_hi, rim_lo), 1, nb, -1, nb))
        u = push(w, tiles_of((b_hi, b_lo, None, None), 0, nb, 0, nb))
        known = old[...] if main.shape[1] == own else main[:, own:]
        now = noted(known, slot, gram(u), expand[:COLS])
        out[:, :own] = u
        out[:, own:] = now
        meta[...] = now
        low, high = u[:, :reach], u[:, own - reach :]
        out_b[...], out_a[...] = by_side(high, low)


def turn_kernel(nb, owner, slot, old, main, edge_a, edge_b, a_hi, a_lo, b_hi, b_lo, ra_hi, ra_lo, rb_hi, rb_lo,
                expand, first_out, out, meta):
    own = nb * BLOCK

    @pl.when(lax.axis_index("tm") != owner)
    def _():
        meta[...] = old[...]

    @pl.when(lax.axis_index("tm") == owner)
    def _():
        left, right = by_side(edge_a[...], edge_b[...])
        v = jnp.concatenate([left, main[:, :own], right], axis=1)
        tiles_a = tiles_of((a_hi, a_lo, ra_hi, ra_lo), RIM_A, nb, -RIM_A, nb + RIM_A)
        tiles_b = tiles_of((b_hi, b_lo, rb_hi, rb_lo), RIM_B, nb, -RIM_B, nb + RIM_B)
        u = push(push(v, tiles_a), tiles_b)
        u_own = u[:, 256 : 256 + own]
        first_out[...] = u_own
        back = pull(pull(u * DOWN, tiles_b), tiles_a[1:-1])
        now = noted(main[:, own:], slot, gram(u_own), expand[:COLS])
        now = noted(now, slot + 1, gram(back[:, 128 : 128 + own]), expand[COLS:] * (1.0 / DOWN))
        out[:, : own + 256] = back
        out[:, own + 256 :] = now
        meta[...] = now


def pull_kernel(nb, owner, slot, old, ext, a_hi, a_lo, b_hi, b_lo, ra_hi, ra_lo, rb_hi, rb_lo, expand, out, meta):
    own = nb * BLOCK

    @pl.when(lax.axis_index("tm") != owner)
    def _():
        meta[...] = old[...]

    @pl.when(lax.axis_index("tm") == owner)
    def _():
        y = pull(ext[:, : own + 256], tiles_of((b_hi, b_lo, rb_hi, rb_lo), RIM_B, nb, -2, nb + 2))
        u = pull(y, tiles_of((a_hi, a_lo, ra_hi, ra_lo), RIM_A, nb, -1, nb + 1))
        out[...] = u
        meta[...] = noted(ext[:, own + 256 :], slot, gram(u), expand[COLS:])


def scale_kernel(stages, boxes, offsets, grams, meta, *refs):
    panels, (out_f, out_a) = refs[: len(stages)], refs[len(stages) :]
    own = out_f.shape[1]
    total = grams[0]
    for i in range(1, grams.shape[0]):
        total = total + grams[i]
    total = total * (1.0 / boxes)
    growth = meta[COLS : 2 * COLS, :]
    row, lane = iota((ROWS, ROWS), 0), iota((ROWS, ROWS), 1)
    same = (row // COLS) == (lane // COLS)
    me = lax.axis_index("tm")

    def full(x, n):
        return jnp.where(same, jnp.concatenate([x[:, n * ROWS : (n + 1) * ROWS]] * PANELS, axis=0), 0.0)

    dot = functools.partial(lax.dot_general, precision=HIGH, preferred_element_type=F32)
    back = None
    for n, (owner, forward) in enumerate(stages):
        e = full(growth, n)
        h = e if back is None else dot(back, e, NN)
        square = jnp.sum(h * dot(full(total, n), h, NN), axis=0, keepdims=True)
        back = h / jnp.sqrt(jnp.maximum(square, 0.0) + 1e-06)

        @pl.when(me == owner)
        def _(n=n, back=back, out=out_f if forward else out_a):
            u = panels[n][:, offsets[n] : offsets[n] + own]
            out[...] = dot(back, u, TN)


def shards(panels_in, blocks, block_mask, mixing):
    owners, count = lax.axis_size("tm"), lax.axis_size("space")
    me, place = lax.axis_index("tm"), lax.axis_index("space")
    nb, own = blocks.shape[1], panels_in.shape[1]
    even = lax.rem(place, 2) == 0
    bf, f32 = (lambda *s: (s, BF)), (lambda *s: (s, F32))

    def partner_a(s):
        return s ^ 1

    def partner_b(s):
        t = s + 1 if s % 2 else s - 1
        return t if 0 <= t < count else s

    def beside(x, to):
        return lax.ppermute(x, "space", [(s, to(s)) for s in range(count)])

    def hop(x, shift, to):
        route = [
            (t * count + s, (t + shift) % owners * count + to(s)) for t in range(owners) for s in range(count)
        ]
        return lax.ppermute(x, ("tm", "space"), route)

    b, j = iota((RUN, nb, 3), 1), iota((RUN, nb, 3), 2)
    outside = ((place == 0) & (b == 0) & (j == 0)) | ((place == count - 1) & (b == nb - 1) & (j == 2))
    present = jnp.where(outside, 0, block_mask).astype(F32).transpose(0, 2, 1)
    mask = jnp.broadcast_to(present[..., None], (RUN, 3, nb, 128))
    rows = blocks.transpose(0, 2, 1, 3)

    near = call(functools.partial(edge_kernel, nb), [f32(128, 128)] * 2, (rows, mask, panels_in))
    near_a, near_b = beside(near[0], partner_a), beside(near[1], partner_b)
    far_rows = 96 * (RIM_A - 1 + RIM_B)
    far = call(functools.partial(far_kernel, nb), [f32(far_rows, 128)] * 2, (rows, mask))
    far_a, far_b = beside(far[0], partner_a), beside(far[1], partner_b)
    *own_tiles, expand = call(
        functools.partial(own_kernel, nb),
        [bf(own, 256)] * 4 + [f32(2 * COLS, 128)],
        (rows, mask, mixing),
        [pltpu.VMEM((2 * RUN, own, 128), F32)],
    )
    depth_a, depth_b = 2 * RIM_A * BLOCK, 2 * RIM_B * BLOCK
    rim_tiles = call(
        rim_kernel,
        [bf(depth_a, 256)] * 2 + [bf(depth_b, 256)] * 2,
        (near_a, near_b, far_a, far_b),
        [pltpu.VMEM((2, depth_a, 128), F32), pltpu.VMEM((2, depth_b, 128), F32)],
    )

    meta = jnp.zeros((ROWS, 128), F32)
    main, edge_a, edge_b = panels_in, near_a[96:], near_b[96:]
    ext = None
    stages = 2 * owners
    owner_of = [k if k < owners else stages - 1 - k for k in range(stages)]
    result = None
    kept, offsets = [], []
    k = 0
    while k < stages:
        turning = k == owners - 1 and (k + 1) % GROUP != 0
        owner, slot = owner_of[k], k % GROUP
        if turning:
            first, ext, meta = call(
                functools.partial(turn_kernel, nb, owner, slot),
                [f32(ROWS, own), f32(ROWS, own + 384), f32(ROWS, 128)],
                (meta, main, edge_a, edge_b, *own_tiles, *rim_tiles, expand),
            )
            kept += [first, ext]
            offsets += [0, 128]
            current = ext[:, 128 : 128 + own]
            k += 2
        elif k < owners:
            reach = 384 if k + 1 == owners - 1 and (k + 2) % GROUP != 0 else 128
            main, edge_a, edge_b, meta = call(
                functools.partial(push_kernel, nb, owner, slot, reach),
                [f32(ROWS, own + 128), f32(ROWS, reach), f32(ROWS, reach), f32(ROWS, 128)],
                (meta, main, edge_a, edge_b, near_a, near_b, *own_tiles, expand),
                [pltpu.VMEM((2, 2 * BLOCK, 128), F32)],
            )
            kept.append(main)
            offsets.append(0)
            current = main[:, :own]
            k += 1
        else:
            current, meta = call(
                functools.partial(pull_kernel, nb, owner, slot),
                [f32(ROWS, own), f32(ROWS, 128)],
                (meta, ext, *own_tiles, *rim_tiles, expand),
            )
            ext = None
            kept.append(current)
            offsets.append(0)
            k += 1

        fresh = False
        if k % GROUP == 0 or k == stages:
            start = k - len(kept)
            todo = [(owner_of[i], i < owners) for i in range(start, k)]
            every = jnp.broadcast_to(meta[None, :COLS], (count, COLS, 128))
            grams = lax.all_to_all(every, "space", 0, 0)
            pair = call(
                functools.partial(scale_kernel, todo, count * own, offsets),
                [f32(ROWS, own)] * 2,
                (grams, meta, *kept),
            )
            if result is None:
                result = pair
            else:
                live = [
                    functools.reduce(jnp.logical_or, [me == o for o, f in todo if f == way], jnp.bool_(False))
                    for way in (True, False)
                ]
                result = [jnp.where(c, new, old) for c, new, old in zip(live, pair, result)]
            current = pair[0 if k - 1 < owners else 1]
            meta, ext, fresh = jnp.zeros((ROWS, 128), F32), None, True
            kept, offsets = [], []
        if k == stages:
            break

        shift = owner_of[k] - owner_of[k - 1]
        if ext is not None:
            ext = hop(ext, shift, lambda s: s)
            continue
        turns_next = k == owners - 1 and (k + 1) % GROUP != 0
        reach = 384 if turns_next else 128
        if fresh or k > owners or main.shape[1] == own:
            main = jnp.concatenate([current, meta], axis=1)
            low, high = current[:, :reach], current[:, own - reach :]
            edge_a, edge_b = jnp.where(even, high, low), jnp.where(even, low, high)
        main = hop(main, shift, lambda s: s)
        edge_a, edge_b = hop(edge_a, shift, partner_a), hop(edge_b, shift, partner_b)
        if k >= owners:
            left, right = jnp.where(even, edge_b, edge_a), jnp.where(even, edge_a, edge_b)
            ext = jnp.concatenate([left, main[:, :own], right, main[:, own:]], axis=1)
    return result[0][None], result[1][None]


def solution(mesh):
    return jax.shard_map(
        shards,
        mesh=mesh,
        in_specs=(
            P(None, "space"),
            P("tm", "space", None, None),
            P("tm", "space", None),
            P("tm", None, None, None),
        ),
        out_specs=(P("tm", None, "space"), P("tm", None, "space")),
        check_vma=False,
    )
```

```python
import functools

import jax
import jax.numpy as jnp
from jax import lax
from jax.experimental import pallas as pl
from jax.experimental.pallas import tpu as pltpu
from jax.sharding import PartitionSpec as P

BLOCK = 64
COLS = 8
PANELS = 4
ROWS = COLS * PANELS
RUN = 2
GROUP = 4
RIM_A = 5
RIM_B = 4
DOWN = 2.0**-16
BF = jnp.bfloat16
F32 = jnp.float32
HIGH = lax.Precision.HIGHEST
NT = (((1,), (1,)), ((), ()))
NN = (((1,), (0,)), ((), ()))
TN = (((0,), (0,)), ((), ()))
VM = pl.BlockSpec(memory_space=pltpu.VMEM)


def call(kernel, outs, args, scratch=(), flops=10**6, far=0, limit=12):
    shapes = [jax.ShapeDtypeStruct(shape, dtype) for shape, dtype in outs]
    return pl.pallas_call(
        kernel,
        out_shape=shapes,
        in_specs=[pl.BlockSpec(memory_space=pltpu.HBM)] * far + [VM] * (len(args) - far),
        out_specs=[VM] * len(outs),
        scratch_shapes=list(scratch),
        compiler_params=pltpu.CompilerParams(vmem_limit_bytes=limit << 20),
        cost_estimate=pl.CostEstimate(flops=flops, bytes_accessed=10**5, transcendentals=0),
    )(*args)


def inside():
    place, last = lax.axis_index("space"), lax.axis_size("space") - 1
    return jnp.where((place == 0) | (place == last), 0.0, 1.0).astype(F32)


def parity():
    return lax.rem(lax.axis_index("space"), 2)


def iota(shape, dim):
    return lax.broadcasted_iota(jnp.int32, shape, dim)


def presence(mask, t, j, nb):
    place, last = lax.axis_index("space"), lax.axis_size("space") - 1
    here = jnp.broadcast_to(mask[j, t : t + 1, :], (nb, nb))
    diagonal = iota((nb, nb), 0) == iota((nb, nb), 1)
    column = jnp.sum(jnp.where(diagonal, here, 0), axis=1, keepdims=True).astype(F32)
    if j == 0:
        column = jnp.where((iota((nb, 1), 0) == 0) & (place == 0), 0.0, column)
    if j == 2:
        column = jnp.where((iota((nb, 1), 0) == nb - 1) & (place == last), 0.0, column)
    return column


def first_kernel(out):
    out[...] = jnp.zeros_like(out)


def edge_kernel(nb, turning, _, blocks, mask, panels, near_b, to_a, *far_b):
    width = panels.shape[1]
    turns = lax.axis_index("tm") == turning

    def near(dst, low_side, column, keep=1.0):
        edge = 0 if low_side else nb - 1
        inner = 1 if low_side else nb - 2
        rest = [(edge, 0), (edge, 1), (inner, 0)] if low_side else [(inner, 2), (edge, 1), (edge, 2)]
        slots = [(0, edge, j, j) for j in range(3)] + [(1, b, j, 4 + i) for i, (b, j) in enumerate(rest)]
        for t, b, j, slot in slots:
            line = blocks[t, j, b : b + 1, :] * (column[t][j][b : b + 1, :] * keep)
            for r in range(32):
                dst[slot * 32 + r : slot * 32 + r + 1, :] = line[:, r * 128 : (r + 1) * 128]
        dst[96:128, :] = panels[:, :128] if low_side else panels[:, width - 128 :]

    for side in range(2):

        @pl.when((parity() == side) & jnp.logical_not(turns))
        def _():
            column = [[presence(mask, t, j, nb) for j in range(3)] for t in range(RUN)]
            near(near_b, side == 0, column, inside())
            near(to_a, side == 1, column)

    if not far_b:
        return

    @pl.when(turns)
    def _():
        even = parity() == 0
        keep = inside()
        for t, rows, start in ((0, RIM_A, 0), (1, RIM_B, 96 * RIM_A)):
            column = [jnp.broadcast_to(presence(mask, t, j, nb), (nb, 128)) for j in range(3)]
            for r in range(32):
                for j in range(3):
                    y = blocks[t, j, :, r * 128 : (r + 1) * 128] * column[j]
                    to = pl.ds(start + j * 32 + r, rows, stride=96)
                    head, tail = y[:rows], y[nb - rows :]
                    to_a[to, :] = jnp.where(even, tail, head)
                    far_b[0][to, :] = jnp.where(even, head, tail) * keep


def banded(y, p):
    low = iota(y[0].shape, 1) < BLOCK
    zero = jnp.zeros_like(y[0])
    turned = [pltpu.roll(v, BLOCK, 1) for v in y]
    at_low, at_high = (y, turned) if p == 0 else (turned, y)
    first = (jnp.where(low, at_low[0], at_high[1]), jnp.where(low, at_low[2], zero))
    second = (jnp.where(low, zero, at_high[0]), jnp.where(low, at_low[1], at_high[2]))
    return first, second


def split2(x):
    high = x.astype(BF)
    return high, (x - high.astype(F32)).astype(BF)


def split3(x):
    first = x.astype(BF)
    x = x - first.astype(F32)
    second = x.astype(BF)
    return first, second, (x - second.astype(F32)).astype(BF)


def split_halves(wide, at, hi, lo):
    for half in range(2):
        lanes = slice(half * 128, half * 128 + 128)
        hi[:, lanes], lo[:, lanes] = split2(wide[at + half])


def own_kernel(nb, blocks, mask, mixing, a_hi, a_lo, b_hi, b_lo, expand, wide):
    for t, hi, lo in ((0, a_hi, a_lo), (1, b_hi, b_lo)):
        is_first = lax.rem(iota((nb, 128), 0), 2) == (1 - t)
        column = [jnp.broadcast_to(presence(mask, t, j, nb), (nb, 128)) for j in range(3)]
        for r in range(32):
            lanes = slice(r * 128, (r + 1) * 128)
            y = [blocks[t, j, :, lanes] * column[j] for j in range(3)]
            for p in range(2):
                first, second = banded(y, p)
                for half in range(2):
                    wide[2 * t + half, pl.ds(2 * r + p, nb, stride=BLOCK), :] = jnp.where(
                        is_first, first[half], second[half]
                    )
        split_halves(wide, 2 * t, hi, lo)
    pick = (lax.rem(iota((COLS, 128), 1), COLS) == iota((COLS, 128), 0)).astype(F32)
    row, lane = iota((ROWS, 128), 0), lax.rem(iota((ROWS, 128), 1), ROWS)
    same = (row // COLS) == (lane // COLS)
    step = []
    for t in range(RUN):
        m = mixing[t].reshape(ROWS, COLS)
        spread = lax.dot_general(m, pick, NN, precision=HIGH, preferred_element_type=F32)
        step.append((row == lane).astype(F32) - jnp.where(same, spread, 0.0))
    for i, (x, y) in enumerate(((step[0], step[1]), (step[1], step[0]))):
        e = lax.dot_general(x[:, :ROWS], y, NN, precision=HIGH, preferred_element_type=F32)
        expand[i * COLS : (i + 1) * COLS, :] = (
            e[0:COLS] + e[COLS : 2 * COLS] + e[2 * COLS : 3 * COLS] + e[3 * COLS :]
        )


def taken(from_a, from_b, left, start):
    use_b = (parity() == 0) == left
    return jnp.where(use_b, from_b[start : start + 32, :], from_a[start : start + 32, :])


def rim_row(dst, index, first, y):
    for p in range(2):
        tiles = banded(y, p)[0 if first else 1]
        for half in range(2):
            dst[half, pl.ds(index * BLOCK + p, 32, stride=2), :] = tiles[half]


def edge_rows(near_a, near_b, dst):
    for left in (True, False):
        rim_row(dst, 1 - left, left, [taken(near_a, near_b, left, j * 32) for j in range(3)])


def rim_kernel(turning, far_b, far_a, a_hi, a_lo, b_hi, b_lo, wide_a, wide_b):
    @pl.when(lax.axis_index("tm") == turning)
    def _():
        for dst, depth, start, odd in ((wide_a, RIM_A, 0, 1), (wide_b, RIM_B, 96 * RIM_A, 0)):
            for i in range(depth):
                for left in (True, False):
                    y = [taken(far_a, far_b, left, start + i * 96 + j * 32) for j in range(3)]
                    place = i - depth if left else i
                    rim_row(dst, i if left else depth + i, place % 2 == odd, y)
        split_halves(wide_a, 0, a_hi, a_lo)
        split_halves(wide_b, 0, b_hi, b_lo)


def pull_rim_kernel(near_a, near_b, a_hi, a_lo, b_hi, b_lo, wide_a, wide_b):
    edge_rows(near_a, near_b, wide_a)
    none = jnp.zeros((32, 128), F32)
    left = [taken(near_a, near_b, True, (4 + i) * 32) for i in range(3)]
    right = [taken(near_a, near_b, False, (4 + i) * 32) for i in range(3)]
    rim_row(wide_b, 0, True, [none, none, left[0]])
    rim_row(wide_b, 1, False, [none, left[1], left[2]])
    rim_row(wide_b, 2, True, [right[0], right[1], none])
    rim_row(wide_b, 3, False, [right[2], none, none])
    split_halves(wide_a, 0, a_hi, a_lo)
    split_halves(wide_b, 0, b_hi, b_lo)


def pair_tile(own, rim, depth, nb, b):
    def row(k):
        if 0 <= k < nb:
            return own[k * BLOCK : (k + 1) * BLOCK, :]
        k = k + depth if k < 0 else depth + k - nb
        return rim[k * BLOCK : (k + 1) * BLOCK, :]

    return jnp.concatenate([row(b), row(b + 1)], axis=0)


def product(x, w, dims):
    o = lax.dot_general(x, w, dims, preferred_element_type=F32)
    return (o[ROWS:, 128:] + o[ROWS:, :128] + o[:ROWS, 128:]) + o[:ROWS, :128]


def push(v, tiles):
    x = jnp.concatenate(split2(v), axis=0)
    outs = []
    for i, (hi, lo) in enumerate(tiles):
        outs.append(product(x[:, i * 128 : i * 128 + 256], jnp.concatenate([hi, lo], axis=0), NT))
    return jnp.concatenate(outs, axis=1)


def pull(v, tiles):
    x = jnp.concatenate(split2(v), axis=0)
    outs = []
    for i in range(len(tiles) - 1):
        parts = [
            jnp.concatenate([tiles[i][s][:, 128:], tiles[i + 1][s][:, :128]], axis=0) for s in range(2)
        ]
        outs.append(product(x[:, i * 128 : i * 128 + 256], jnp.concatenate(parts, axis=1), NN))
    return jnp.concatenate(outs, axis=1)


def tiles_of(refs, depth, nb, first, last):
    own_hi, own_lo, rim_hi, rim_lo = refs
    return [
        (pair_tile(own_hi, rim_hi, depth, nb, b), pair_tile(own_lo, rim_lo, depth, nb, b))
        for b in range(first, last, 2)
    ]


def gram(u):
    u1, u2, u3 = split3(u)
    stack = jnp.concatenate([u3, u2, u1], axis=0)
    total = None
    for part in (u3, u2, u1):
        g = lax.dot_general(stack, jnp.concatenate([part] * 4, axis=0), NT, preferred_element_type=F32)
        g = (g[:ROWS] + g[ROWS : 2 * ROWS]) + g[2 * ROWS :]
        total = g if total is None else total + g
    panel = lax.rem(iota((COLS, 128), 1), ROWS) // COLS
    out = jnp.zeros((COLS, 128), F32)
    for p in range(PANELS):
        out = out + jnp.where(panel == p, total[p * COLS : (p + 1) * COLS], 0.0)
    return out


def noted(meta, slot, g, e):
    mine = (iota((COLS, 128), 1) // ROWS) == slot
    return jnp.concatenate(
        [jnp.where(mine, g, meta[:COLS]), jnp.where(mine, e, meta[COLS : 2 * COLS]), meta[2 * COLS :]], axis=0
    )


def by_side(e_a, e_b):
    even = parity() == 0
    return jnp.where(even, e_b, e_a), jnp.where(even, e_a, e_b)


def push_kernel(nb, owner, slot, reach, old, edge_b, main, edge_a, near_b, near_a, a_hi, a_lo, b_hi, b_lo, expand,
                out, out_a, out_b, meta, wide):
    own = nb * BLOCK

    @pl.when(lax.axis_index("tm") != owner)
    def _():
        meta[...] = old[...]

    @pl.when(lax.axis_index("tm") == owner)
    def _():
        edge_rows(near_a, near_b, wide)
        rim_hi, rim_lo = split2(jnp.concatenate([wide[0], wide[1]], axis=1))
        w_edge = edge_a.shape[1]
        left, right = by_side(edge_a[...], edge_b[...])
        v = jnp.concatenate([left[:, w_edge - 128 :], main[:, :own], right[:, :128]], axis=1)
        w = push(v, tiles_of((a_hi, a_lo, rim_hi, rim_lo), 1, nb, -1, nb))
        u = push(w, tiles_of((b_hi, b_lo, None, None), 0, nb, 0, nb))
        known = old[...] if main.shape[1] == own else main[:, own:]
        now = noted(known, slot, gram(u), expand[:COLS])
        out[:, :own] = u
        out[:, own:] = now
        meta[...] = now
        low, high = u[:, :reach], u[:, own - reach :]
        out_b[...], out_a[...] = by_side(high, low)


def turn_kernel(nb, owner, slot, old, edge_b, main, edge_a, a_hi, a_lo, b_hi, b_lo, ra_hi, ra_lo, rb_hi, rb_lo,
                expand, first_out, out, meta):
    own = nb * BLOCK

    @pl.when(lax.axis_index("tm") != owner)
    def _():
        meta[...] = old[...]

    @pl.when(lax.axis_index("tm") == owner)
    def _():
        left, right = by_side(edge_a[...], edge_b[...])
        v = jnp.concatenate([left, main[:, :own], right], axis=1)
        tiles_a = tiles_of((a_hi, a_lo, ra_hi, ra_lo), RIM_A, nb, -RIM_A, nb + RIM_A)
        tiles_b = tiles_of((b_hi, b_lo, rb_hi, rb_lo), RIM_B, nb, -RIM_B, nb + RIM_B)
        u = push(push(v, tiles_a), tiles_b)
        u_own = u[:, 256 : 256 + own]
        first_out[...] = u_own
        back = pull(pull(u * DOWN, tiles_b), tiles_a[1:-1])
        now = noted(main[:, own:], slot, gram(u_own), expand[:COLS])
        now = noted(now, slot + 1, gram(back[:, 128 : 128 + own]), expand[COLS:] * (1.0 / DOWN))
        out[:, : own + 256] = back
        out[:, own + 256 :] = now
        meta[...] = now


def pull_kernel(nb, owner, slot, old, ext, a_hi, a_lo, b_hi, b_lo, ra_hi, ra_lo, rb_hi, rb_lo, expand, out, meta):
    own = nb * BLOCK

    @pl.when(lax.axis_index("tm") != owner)
    def _():
        meta[...] = old[...]

    @pl.when(lax.axis_index("tm") == owner)
    def _():
        y = pull(ext[:, : own + 256], tiles_of((b_hi, b_lo, rb_hi, rb_lo), 2, nb, -2, nb + 2))
        u = pull(y, tiles_of((a_hi, a_lo, ra_hi, ra_lo), 1, nb, -1, nb + 1))
        out[...] = u
        meta[...] = noted(ext[:, own + 256 :], slot, gram(u), expand[COLS:])


def exact(x, y):
    width = y.shape[1]
    xs, ys = split3(x), split3(y)
    o = lax.dot_general(
        jnp.concatenate(xs, axis=0), jnp.concatenate(ys, axis=1), NN, preferred_element_type=F32
    )
    piece = [[o[i * ROWS : (i + 1) * ROWS, j * width : (j + 1) * width] for j in range(3)] for i in range(3)]
    small = (piece[0][2] + piece[2][0]) + piece[1][1]
    return (small + (piece[0][1] + piece[1][0])) + piece[0][0]


def scale_kernel(stages, boxes, offsets, grams, meta, *refs):
    panels, (out_f, out_a) = refs[: len(stages)], refs[len(stages) :]
    own = out_f.shape[1]
    parts = [grams[i] for i in range(grams.shape[0])]
    while len(parts) > 1:
        parts = [a + b for a, b in zip(parts[::2], parts[1::2])] + parts[len(parts) // 2 * 2 :]
    total = parts[0] * (1.0 / boxes)
    growth = meta[COLS : 2 * COLS, :]
    row, lane = iota((ROWS, 128), 0), iota((ROWS, 128), 1)
    same = (row // COLS) == (lax.rem(lane, ROWS) // COLS)
    me = lax.axis_index("tm")

    def full(x, n):
        turns = [x if k == n else pltpu.roll(x, ((k - n) % 4) * ROWS, 1) for k in range(4)]
        group = lane[:COLS] // ROWS
        spread = turns[0]
        for k in range(1, 4):
            spread = jnp.where(group == k, turns[k], spread)
        return jnp.where(same, jnp.concatenate([spread] * PANELS, axis=0), 0.0)

    back, select = None, {True: None, False: None}
    for n, (owner, forward) in enumerate(stages):
        e = full(growth, n)
        h = e if back is None else exact(back[:, :ROWS], e)
        square = jnp.sum(h * exact(full(total, n)[:, :ROWS], h), axis=0, keepdims=True)
        back = h * lax.rsqrt(jnp.maximum(square, 0.0) + 1e-06)
        u = panels[n][:, offsets[n] : offsets[n] + own]
        old = select[forward]
        select[forward] = (back, u) if old is None else (
            jnp.where(me == owner, back, old[0]), jnp.where(me == owner, u, old[1])
        )
    for forward, out in ((True, out_f), (False, out_a)):
        if select[forward] is None:
            out[...] = jnp.zeros_like(out)
        else:
            b, u = select[forward]
            out[...] = exact(b[:, :ROWS].T, u)


def shards(panels_in, blocks, block_mask, mixing):
    owners, count = lax.axis_size("tm"), lax.axis_size("space")
    me, place = lax.axis_index("tm"), lax.axis_index("space")
    nb, own = blocks.shape[1], panels_in.shape[1]
    even = lax.rem(place, 2) == 0
    bf, f32 = (lambda *s: (s, BF)), (lambda *s: (s, F32))

    def partner_a(s):
        return s ^ 1

    def partner_b(s):
        t = s + 1 if s % 2 else s - 1
        return t if 0 <= t < count else s

    def beside(x, to, only=None):
        route = [(t * count + s, t * count + to(s)) for t in (only or range(owners)) for s in range(count)]
        return lax.ppermute(x, ("tm", "space"), route)

    def hop(x, shift, to):
        route = [
            (t * count + s, (t + shift) % owners * count + to(s)) for t in range(owners) for s in range(count)
        ]
        return lax.ppermute(x, ("tm", "space"), route)

    rows, mask = blocks.transpose(0, 2, 1, 3), block_mask.transpose(2, 0, 1)
    vm = lambda *s: pltpu.VMEM(s, F32)
    turn = owners % GROUP != 0
    turning = owners - 1 if turn else owners
    begin = call(first_kernel, [f32(8, 128)], (), flops=10**9)
    far_rows = 96 * (RIM_A + RIM_B)
    sizes = [224, far_rows, far_rows] if turn else [224, 224]
    edges = call(
        functools.partial(edge_kernel, nb, turning),
        [f32(n, 128) for n in sizes],
        (*begin, rows, mask, panels_in),
    )
    near_b, near_a = beside(edges[0], partner_b, range(turning)), beside(edges[1], partner_a)
    if turn:
        far_b = beside(edges[2], partner_b, [turning])
    rows, mask, mixing, _ = lax.optimization_barrier((rows, mask, mixing, edges))
    *own_tiles, expand = call(
        functools.partial(own_kernel, nb),
        [bf(own, 256)] * 4 + [f32(2 * COLS, 128)],
        (rows, mask, mixing),
        [vm(2 * RUN, own, 128)],
    )

    def rim_call(kernel, deep_a, deep_b, args):
        deep_a, deep_b = 2 * deep_a * BLOCK, 2 * deep_b * BLOCK
        outs, scratch = [bf(deep_a, 256)] * 2 + [bf(deep_b, 256)] * 2, [vm(2, deep_a, 128), vm(2, deep_b, 128)]
        return call(kernel, outs, args, scratch)

    pull_rims = rim_call(pull_rim_kernel, 1, 2, (near_a, near_b))
    if turn:
        turn_rims = rim_call(functools.partial(rim_kernel, turning), RIM_A, RIM_B, (far_b, near_a))

    meta = jnp.zeros((ROWS, 128), F32)
    main, edge_a, edge_b = panels_in, near_a[96:128], near_b[96:128]
    ext = None
    stages = 2 * owners
    owner_of = [k if k < owners else stages - 1 - k for k in range(stages)]
    result = None
    kept, offsets = [], []
    k = 0
    while k < stages:
        turning = k == owners - 1 and (k + 1) % GROUP != 0
        owner, slot = owner_of[k], k % GROUP
        if turning:
            first, ext, meta = call(
                functools.partial(turn_kernel, nb, owner, slot),
                [f32(ROWS, own), f32(ROWS, own + 384), f32(ROWS, 128)],
                (meta, edge_b, main, edge_a, *own_tiles, *turn_rims, expand),
            )
            kept += [first, ext]
            offsets += [0, 128]
            current = ext[:, 128 : 128 + own]
            k += 2
        elif k < owners:
            reach = 384 if k + 1 == owners - 1 and (k + 2) % GROUP != 0 else 128
            main, edge_a, edge_b, meta = call(
                functools.partial(push_kernel, nb, owner, slot, reach),
                [f32(ROWS, own + 128), f32(ROWS, reach), f32(ROWS, reach), f32(ROWS, 128)],
                (meta, edge_b, main, edge_a, near_b, near_a, *own_tiles, expand),
                [pltpu.VMEM((2, 2 * BLOCK, 128), F32)],
            )
            kept.append(main)
            offsets.append(0)
            current = main[:, :own]
            k += 1
        else:
            current, meta = call(
                functools.partial(pull_kernel, nb, owner, slot),
                [f32(ROWS, own), f32(ROWS, 128)],
                (meta, ext, *own_tiles, *pull_rims, expand),
            )
            ext = None
            kept.append(current)
            offsets.append(0)
            k += 1

        fresh = False
        if k % GROUP == 0 or k == stages:
            start = k - len(kept)
            todo = [(owner_of[i], i < owners) for i in range(start, k)]
            every = jnp.broadcast_to(meta[None, :COLS], (count, COLS, 128))
            grams = lax.all_to_all(every, "space", 0, 0)
            pair = call(
                functools.partial(scale_kernel, todo, count * own, offsets),
                [f32(ROWS, own)] * 2,
                (grams, meta, *kept),
            )
            if result is None:
                result = pair
            else:
                live = [
                    functools.reduce(jnp.logical_or, [me == o for o, f in todo if f == way], jnp.bool_(False))
                    for way in (True, False)
                ]
                result = [jnp.where(c, new, old) for c, new, old in zip(live, pair, result)]
            current = pair[0 if k - 1 < owners else 1]
            meta, ext, fresh = jnp.zeros((ROWS, 128), F32), None, True
            kept, offsets = [], []
        if k == stages:
            break

        shift = owner_of[k] - owner_of[k - 1]
        if ext is not None:
            ext = hop(ext, shift, lambda s: s)
            continue
        turns_next = k == owners - 1 and (k + 1) % GROUP != 0
        reach = 384 if turns_next else 128
        if fresh or k > owners or main.shape[1] == own:
            main = jnp.concatenate([current, meta], axis=1)
            low, high = current[:, :reach], current[:, own - reach :]
            edge_a, edge_b = jnp.where(even, high, low), jnp.where(even, low, high)
        main = hop(main, shift, lambda s: s)
        edge_a, edge_b = hop(edge_a, shift, partner_a), hop(edge_b, shift, partner_b)
        if k >= owners:
            left, right = jnp.where(even, edge_b, edge_a), jnp.where(even, edge_a, edge_b)
            ext = jnp.concatenate([left, main[:, :own], right, main[:, own:]], axis=1)
    return result[0][None], result[1][None]


def solution(mesh):
    return jax.shard_map(
        shards,
        mesh=mesh,
        in_specs=(
            P(None, "space"),
            P("tm", "space", None, None),
            P("tm", "space", None),
            P("tm", None, None, None),
        ),
        out_specs=(P("tm", None, "space"), P("tm", None, "space")),
        check_vma=False,
    )
```

```python
import functools

import jax
import jax.numpy as jnp
from jax import lax
from jax.experimental import pallas as pl
from jax.experimental.pallas import tpu as pltpu
from jax.sharding import PartitionSpec as P

BLOCK = 64
COLS = 8
PANELS = 4
ROWS = COLS * PANELS
RUN = 2
GROUP = 4
RIM_A, RIM_B = 5, 4
FAR_A, FAR_B = 3, 2
PUSH = 10**9
ASIDE_1, ASIDE_2 = 3 * 10**8, 5 * 10**8
DOWN = 2.0**-16
BF = jnp.bfloat16
F32 = jnp.float32
HIGH = lax.Precision.HIGHEST
NT = (((1,), (1,)), ((), ()))
NN = (((1,), (0,)), ((), ()))
TN = (((0,), (0,)), ((), ()))
VM = pl.BlockSpec(memory_space=pltpu.VMEM)


def call(kernel, outs, args, scratch=(), flops=10**6, far=0, limit=12):
    shapes = [jax.ShapeDtypeStruct(shape, dtype) for shape, dtype in outs]
    return pl.pallas_call(
        kernel,
        out_shape=shapes,
        in_specs=[pl.BlockSpec(memory_space=pltpu.HBM)] * far + [VM] * (len(args) - far),
        out_specs=[VM] * len(outs),
        scratch_shapes=list(scratch),
        compiler_params=pltpu.CompilerParams(vmem_limit_bytes=limit << 20),
        cost_estimate=pl.CostEstimate(flops=flops, bytes_accessed=10**5, transcendentals=0),
    )(*args)


def inside():
    place, last = lax.axis_index("space"), lax.axis_size("space") - 1
    return jnp.where((place == 0) | (place == last), 0.0, 1.0).astype(F32)


def parity():
    return lax.rem(lax.axis_index("space"), 2)


def iota(shape, dim):
    return lax.broadcasted_iota(jnp.int32, shape, dim)


def presence(mask, t, j, nb):
    place, last = lax.axis_index("space"), lax.axis_size("space") - 1
    here = jnp.broadcast_to(mask[j, t : t + 1, :], (nb, nb))
    diagonal = iota((nb, nb), 0) == iota((nb, nb), 1)
    column = jnp.sum(jnp.where(diagonal, here, 0), axis=1, keepdims=True).astype(F32)
    if j == 0:
        column = jnp.where((iota((nb, 1), 0) == 0) & (place == 0), 0.0, column)
    if j == 2:
        column = jnp.where((iota((nb, 1), 0) == nb - 1) & (place == last), 0.0, column)
    return column


def first_kernel(out):
    out[...] = jnp.zeros_like(out)


def edge_kernel(nb, turning, _, blocks, mask, panels, near_b, to_a, *far_b):
    width = panels.shape[1]
    turns = lax.axis_index("tm") == turning

    def near(dst, low_side, column, keep=1.0):
        edge = 0 if low_side else nb - 1
        inner = 1 if low_side else nb - 2
        rest = [(edge, 0), (edge, 1), (inner, 0)] if low_side else [(inner, 2), (edge, 1), (edge, 2)]
        slots = [(0, edge, j, j) for j in range(3)] + [(1, b, j, 4 + i) for i, (b, j) in enumerate(rest)]
        for t, b, j, slot in slots:
            line = blocks[t, j, b : b + 1, :] * (column[t][j][b : b + 1, :] * keep)
            for r in range(32):
                dst[slot * 32 + r : slot * 32 + r + 1, :] = line[:, r * 128 : (r + 1) * 128]
        dst[96:128, :] = panels[:, :128] if low_side else panels[:, width - 128 :]

    for side in range(2):

        @pl.when((parity() == side) & jnp.logical_not(turns))
        def _():
            column = [[presence(mask, t, j, nb) for j in range(3)] for t in range(RUN)]
            near(near_b, side == 0, column, inside())
            near(to_a, side == 1, column)

    if not far_b:
        return

    @pl.when(turns)
    def _():
        even, odd = parity() == 0, parity() == 1
        keep = inside()
        for t, deep, start_a, wide, start_b in ((0, RIM_A, 0, FAR_A, 0), (1, RIM_B, 96 * RIM_A, FAR_B, 96 * FAR_A)):
            column = [jnp.broadcast_to(presence(mask, t, j, nb), (nb, 128)) for j in range(3)]
            for r in range(32):
                for j in range(3):
                    y = blocks[t, j, :, r * 128 : (r + 1) * 128] * column[j]
                    for dst, rows, start, tail_if in ((to_a, deep, start_a, even), (far_b[0], wide, start_b, odd)):
                        to = pl.ds(start + j * 32 + r, rows, stride=96)
                        dst[to, :] = jnp.where(tail_if, y[nb - rows :], y[:rows])
        far_b[0][...] = far_b[0][...] * keep


def banded(y, p):
    low = iota(y[0].shape, 1) < BLOCK
    zero = jnp.zeros_like(y[0])
    turned = [pltpu.roll(v, BLOCK, 1) for v in y]
    at_low, at_high = (y, turned) if p == 0 else (turned, y)
    first = (jnp.where(low, at_low[0], at_high[1]), jnp.where(low, at_low[2], zero))
    second = (jnp.where(low, zero, at_high[0]), jnp.where(low, at_low[1], at_high[2]))
    return first, second


def split2(x):
    high = x.astype(BF)
    return high, (x - high.astype(F32)).astype(BF)


def split3(x):
    first = x.astype(BF)
    x = x - first.astype(F32)
    second = x.astype(BF)
    return first, second, (x - second.astype(F32)).astype(BF)


def split_halves(wide, at, hi, lo):
    for half in range(2):
        lanes = slice(half * 128, half * 128 + 128)
        hi[:, lanes], lo[:, lanes] = split2(wide[at + half])


def own_kernel(nb, blocks, mask, mixing, a_hi, a_lo, b_hi, b_lo, expand, wide):
    for t, hi, lo in ((0, a_hi, a_lo), (1, b_hi, b_lo)):
        is_first = lax.rem(iota((nb, 128), 0), 2) == (1 - t)
        column = [jnp.broadcast_to(presence(mask, t, j, nb), (nb, 128)) for j in range(3)]
        for r in range(32):
            lanes = slice(r * 128, (r + 1) * 128)
            y = [blocks[t, j, :, lanes] * column[j] for j in range(3)]
            for p in range(2):
                first, second = banded(y, p)
                for half in range(2):
                    wide[2 * t + half, pl.ds(2 * r + p, nb, stride=BLOCK), :] = jnp.where(
                        is_first, first[half], second[half]
                    )
        split_halves(wide, 2 * t, hi, lo)
    pick = (lax.rem(iota((COLS, 128), 1), COLS) == iota((COLS, 128), 0)).astype(F32)
    row, lane = iota((ROWS, 128), 0), lax.rem(iota((ROWS, 128), 1), ROWS)
    same = (row // COLS) == (lane // COLS)
    step = []
    for t in range(RUN):
        m = mixing[t].reshape(ROWS, COLS)
        spread = lax.dot_general(m, pick, NN, precision=HIGH, preferred_element_type=F32)
        step.append((row == lane).astype(F32) - jnp.where(same, spread, 0.0))
    for i, (x, y) in enumerate(((step[0], step[1]), (step[1], step[0]))):
        e = lax.dot_general(x[:, :ROWS], y, NN, precision=HIGH, preferred_element_type=F32)
        expand[i * COLS : (i + 1) * COLS, :] = (
            e[0:COLS] + e[COLS : 2 * COLS] + e[2 * COLS : 3 * COLS] + e[3 * COLS :]
        )


def taken(from_a, from_b, left, start):
    use_b = (parity() == 0) == left
    return jnp.where(use_b, from_b[start : start + 32, :], from_a[start : start + 32, :])


def rim_row(dst, index, first, y):
    for p in range(2):
        tiles = banded(y, p)[0 if first else 1]
        for half in range(2):
            dst[half, pl.ds(index * BLOCK + p, 32, stride=2), :] = tiles[half]


def edge_rows(near_a, near_b, dst):
    for left in (True, False):
        rim_row(dst, 1 - left, left, [taken(near_a, near_b, left, j * 32) for j in range(3)])


def rim_kernel(turning, far_b, far_a, a_hi, a_lo, b_hi, b_lo, wide_a, wide_b):
    none = jnp.zeros((32, 128), F32)

    @pl.when(lax.axis_index("tm") == turning)
    def _():
        for dst, deep, start_a, wide, start_b, odd in (
            (wide_a, RIM_A, 0, FAR_A, 0, 1),
            (wide_b, RIM_B, 96 * RIM_A, FAR_B, 96 * FAR_A, 0),
        ):
            for i in range(deep):
                for left in (True, False):
                    k = i - (deep - wide) if left else i
                    y = []
                    for j in range(3):
                        n, m = start_a + i * 96 + j * 32, start_b + k * 96 + j * 32
                        from_b = far_b[m : m + 32, :] if 0 <= k < wide else none
                        y.append(jnp.where((parity() == 0) == left, from_b, far_a[n : n + 32, :]))
                    place = i - deep if left else i
                    rim_row(dst, i if left else deep + i, place % 2 == odd, y)
        split_halves(wide_a, 0, a_hi, a_lo)
        split_halves(wide_b, 0, b_hi, b_lo)


def pull_rim_kernel(turning, near_a, near_b, a_hi, a_lo, b_hi, b_lo, wide_a, wide_b):
    @pl.when(lax.axis_index("tm") != turning)
    def _():
        edge_rows(near_a, near_b, wide_a)
        none = jnp.zeros((32, 128), F32)
        left = [taken(near_a, near_b, True, (4 + i) * 32) for i in range(3)]
        right = [taken(near_a, near_b, False, (4 + i) * 32) for i in range(3)]
        rim_row(wide_b, 0, True, [none, none, left[0]])
        rim_row(wide_b, 1, False, [none, left[1], left[2]])
        rim_row(wide_b, 2, True, [right[0], right[1], none])
        rim_row(wide_b, 3, False, [right[2], none, none])
        split_halves(wide_a, 0, a_hi, a_lo)
        split_halves(wide_b, 0, b_hi, b_lo)


def pair_tile(own, rim, depth, nb, b):
    def row(k):
        if 0 <= k < nb:
            return own[k * BLOCK : (k + 1) * BLOCK, :]
        k = k + depth if k < 0 else depth + k - nb
        return rim[k * BLOCK : (k + 1) * BLOCK, :]

    return jnp.concatenate([row(b), row(b + 1)], axis=0)


def product(x, w, dims):
    o = lax.dot_general(x, w, dims, preferred_element_type=F32)
    return (o[ROWS:, 128:] + o[ROWS:, :128] + o[:ROWS, 128:]) + o[:ROWS, :128]


def push(v, tiles):
    x = jnp.concatenate(split2(v), axis=0)
    outs = []
    for i, (hi, lo) in enumerate(tiles):
        outs.append(product(x[:, i * 128 : i * 128 + 256], jnp.concatenate([hi, lo], axis=0), NT))
    return jnp.concatenate(outs, axis=1)


def pull(v, tiles):
    x = jnp.concatenate(split2(v), axis=0)
    outs = []
    for i in range(len(tiles) - 1):
        parts = [
            jnp.concatenate([tiles[i][s][:, 128:], tiles[i + 1][s][:, :128]], axis=0) for s in range(2)
        ]
        outs.append(product(x[:, i * 128 : i * 128 + 256], jnp.concatenate(parts, axis=1), NN))
    return jnp.concatenate(outs, axis=1)


def tiles_of(refs, depth, nb, first, last):
    own_hi, own_lo, rim_hi, rim_lo = refs
    return [
        (pair_tile(own_hi, rim_hi, depth, nb, b), pair_tile(own_lo, rim_lo, depth, nb, b))
        for b in range(first, last, 2)
    ]


def gram(u):
    high, low = split2(u)
    o = lax.dot_general(
        jnp.concatenate([low, high], axis=0),
        jnp.concatenate([low] * 4 + [high] * 4, axis=0),
        NT,
        preferred_element_type=F32,
    )
    total = (o[:ROWS, :128] + o[:ROWS, 128:] + o[ROWS:, :128]) + o[ROWS:, 128:]
    panel = lax.rem(iota((COLS, 128), 1), ROWS) // COLS
    out = jnp.zeros((COLS, 128), F32)
    for p in range(PANELS):
        out = out + jnp.where(panel == p, total[p * COLS : (p + 1) * COLS], 0.0)
    return out


def noted(g, e, slot, new_g, new_e):
    mine = (iota((COLS, 128), 1) // ROWS) == slot
    return jnp.where(mine, new_g, g), jnp.where(mine, new_e, e)


def by_side(e_a, e_b):
    even = parity() == 0
    return jnp.where(even, e_b, e_a), jnp.where(even, e_a, e_b)


def aside_kernel(edge, *refs):
    out = refs[-1]
    width, wanted = edge.shape[1], out.shape[1]
    if width == wanted:
        out[...] = edge[...]
        return
    none = jnp.zeros((ROWS, wanted - width), F32)
    left = jnp.concatenate([none, edge[...]], axis=1)
    right = jnp.concatenate([edge[...], none], axis=1)
    out[...] = jnp.where(parity() == 0, left, right)


def push_kernel(nb, owner, edge_b, main, edge_a, near_b, near_a, a_hi, a_lo, b_hi, b_lo, out, out_b, out_a, wide):
    own = nb * BLOCK

    @pl.when(lax.axis_index("tm") == owner)
    def _():
        edge_rows(near_a, near_b, wide)
        rim_hi, rim_lo = split2(jnp.concatenate([wide[0], wide[1]], axis=1))
        left, right = by_side(edge_a[...], edge_b[...])
        v = jnp.concatenate([left, main[:, :own], right], axis=1)
        w = push(v, tiles_of((a_hi, a_lo, rim_hi, rim_lo), 1, nb, -1, nb))
        u = push(w, tiles_of((b_hi, b_lo, None, None), 0, nb, 0, nb))
        out[...] = u
        wide_b, wide_a = out_b.shape[1], out_a.shape[1]
        out_b[...] = by_side(u[:, :wide_b], u[:, own - wide_b :])[1]
        out_a[...] = by_side(u[:, own - wide_a :], u[:, :wide_a])[1]


def turn_kernel(nb, owner, slot, edge_b, main, edge_a, a_hi, a_lo, b_hi, b_lo, ra_hi, ra_lo, rb_hi, rb_lo,
                old, expand, first, out, out_b):
    own = nb * BLOCK
    end = own + 128

    @pl.when(lax.axis_index("tm") != owner)
    def _():
        out[: 2 * COLS, end:] = old[...]

    @pl.when(lax.axis_index("tm") == owner)
    def _():
        left, right = by_side(edge_a[...], edge_b[...])
        v = jnp.concatenate([left, main[:, :own], right], axis=1)
        tiles_a = tiles_of((a_hi, a_lo, ra_hi, ra_lo), RIM_A, nb, -RIM_A, nb + RIM_A)
        tiles_b = tiles_of((b_hi, b_lo, rb_hi, rb_lo), RIM_B, nb, -RIM_B, nb + RIM_B)
        u = push(push(v, tiles_a), tiles_b)
        u_own = u[:, 256 : 256 + own]
        first[...] = u_own
        back = pull(pull(u * DOWN, tiles_b), tiles_a[1:-1])
        back_own = back[:, 128 : 128 + own]
        out[:, :own] = back_own
        out[:, own:end] = by_side(back[:, end:], back[:, :128])[1]
        out_b[...] = by_side(back[:, 128:256], back[:, own:end])[1]
        g, e = noted(old[:COLS], old[COLS:], slot, gram(u_own), expand[:COLS])
        g, e = noted(g, e, slot + 1, gram(back_own), expand[COLS:] * (1.0 / DOWN))
        out[: 2 * COLS, end:] = jnp.concatenate([g, e], axis=0)


def pull_kernel(nb, owner, edge_b, main, edge_a, a_hi, a_lo, b_hi, b_lo, ra_hi, ra_lo, rb_hi, rb_lo, out):
    own = nb * BLOCK

    @pl.when(lax.axis_index("tm") == owner)
    def _():
        left, right = by_side(edge_a[...], edge_b[...])
        v = jnp.concatenate([left, main[:, :own], right], axis=1)
        y = pull(v, tiles_of((b_hi, b_lo, rb_hi, rb_lo), 2, nb, -2, nb + 2))
        out[...] = pull(y, tiles_of((a_hi, a_lo, ra_hi, ra_lo), 1, nb, -1, nb + 1))


def note_kernel(nb, owner, slot, forward, u, old, expand, out):
    @pl.when(lax.axis_index("tm") != owner)
    def _():
        out[...] = old[...]

    @pl.when(lax.axis_index("tm") == owner)
    def _():
        e = expand[:COLS] if forward else expand[COLS:]
        out[:COLS], out[COLS:] = noted(old[:COLS], old[COLS:], slot, gram(u[:, : nb * BLOCK]), e)


def exact(x, y):
    m = x.shape[0]
    o = lax.dot_general(
        jnp.concatenate(split3(x), axis=0), jnp.concatenate(split3(y), axis=1), NN, preferred_element_type=F32
    )
    piece = [[o[i * m : (i + 1) * m, j * 128 : (j + 1) * 128] for j in range(3)] for i in range(3)]
    small = (piece[0][2] + piece[2][0]) + piece[1][1]
    return (small + (piece[0][1] + piece[1][0])) + piece[0][0]


def scale_kernel(stages, boxes, grams, meta, *refs):
    panels, (out_f, out_a) = refs[: len(stages)], refs[len(stages) :]
    own = out_f.shape[1]
    parts = [grams[i] for i in range(grams.shape[0])]
    while len(parts) > 1:
        parts = [a + b for a, b in zip(parts[::2], parts[1::2])] + parts[len(parts) // 2 * 2 :]
    total = parts[0] * (1.0 / boxes)
    growth = meta[COLS:, :]
    row, lane = iota((ROWS, 128), 0), iota((ROWS, 128), 1)
    same = (row // COLS) == (lax.rem(lane, ROWS) // COLS)
    me = lax.axis_index("tm")

    def full(x, n):
        turns = [x if k == n else pltpu.roll(x, ((k - n) % 4) * ROWS, 1) for k in range(4)]
        group = lane[:COLS] // ROWS
        spread = turns[0]
        for k in range(1, 4):
            spread = jnp.where(group == k, turns[k], spread)
        return jnp.where(same, jnp.concatenate([spread] * PANELS, axis=0), 0.0)

    count = len(stages)
    h = full(growth, 0)
    stack = jnp.concatenate([h, exact(jnp.concatenate([full(total, n)[:, :ROWS] for n in range(count)], axis=0), h)])
    select = {True: None, False: None}
    for n, (owner, forward) in enumerate(stages):
        if n:
            stack = exact(stack[:, :ROWS], full(growth, n))
        square = jnp.sum(stack[:ROWS] * stack[ROWS : 2 * ROWS], axis=0, keepdims=True)
        scale = lax.rsqrt(jnp.maximum(square, 0.0) + 1e-06)
        later = [stack[2 * ROWS :]] if n + 1 < count else []
        stack = jnp.concatenate([stack[:ROWS]] + later, axis=0) * scale
        back, u = stack[:ROWS], panels[n][:, :own]
        old = select[forward]
        select[forward] = (back, u) if old is None else (
            jnp.where(me == owner, back, old[0]), jnp.where(me == owner, u, old[1])
        )
    for forward, out in ((True, out_f), (False, out_a)):
        if select[forward] is None:
            out[...] = jnp.zeros_like(out)
        else:
            back, u = select[forward]
            left = jnp.concatenate(split2(back[:, :ROWS].T), axis=0)
            o = lax.dot_general(left, jnp.concatenate(split2(u), axis=1), NN, preferred_element_type=F32)
            out[...] = (o[ROWS:, own:] + o[ROWS:, :own] + o[:ROWS, own:]) + o[:ROWS, :own]


def shards(panels_in, blocks, block_mask, mixing):
    owners, count = lax.axis_size("tm"), lax.axis_size("space")
    me, place = lax.axis_index("tm"), lax.axis_index("space")
    nb, own = blocks.shape[1], panels_in.shape[1]
    even = lax.rem(place, 2) == 0
    bf, f32 = (lambda *s: (s, BF)), (lambda *s: (s, F32))

    def partner_a(s):
        return s ^ 1

    def partner_b(s):
        t = s + 1 if s % 2 else s - 1
        return t if 0 <= t < count else s

    def beside(x, to, only=None):
        route = [(t * count + s, t * count + to(s)) for t in (only or range(owners)) for s in range(count)]
        return lax.ppermute(x, ("tm", "space"), route)

    def hop(x, t, o, to):
        pairs = [(t, o), (o, t)] if t != o else [(t, t)]
        return lax.ppermute(x, ("tm", "space"), [(i * count + s, k * count + to(s)) for i, k in pairs for s in range(count)])

    def edges_of(x, wide_b, wide_a):
        return (
            jnp.where(even, x[:, :wide_b], x[:, own - wide_b : own]),
            jnp.where(even, x[:, own - wide_a : own], x[:, :wide_a]),
        )

    rows, mask = blocks.transpose(0, 2, 1, 3), block_mask.transpose(2, 0, 1)
    vm = lambda *s: pltpu.VMEM(s, F32)
    turn = owners % GROUP != 0
    turning = owners - 1 if turn else owners
    begin = call(first_kernel, [f32(8, 128)], (), flops=10**9)
    sizes = [224, 96 * (RIM_A + RIM_B), 96 * (FAR_A + FAR_B)] if turn else [224, 224]
    edges = call(
        functools.partial(edge_kernel, nb, turning),
        [f32(n, 128) for n in sizes],
        (*begin, rows, mask, panels_in),
    )
    near_b, near_a = beside(edges[0], partner_b, range(turning)), beside(edges[1], partner_a)
    if turn:
        far_b = beside(edges[2], partner_b, [turning])
    rows, mask, mixing, _ = lax.optimization_barrier((rows, mask, mixing, edges))
    *own_tiles, expand = call(
        functools.partial(own_kernel, nb),
        [bf(own, 256)] * 4 + [f32(2 * COLS, 128)],
        (rows, mask, mixing),
        [vm(2 * RUN, own, 128)],
    )

    def rim_call(kernel, deep_a, deep_b, args):
        deep_a, deep_b = 2 * deep_a * BLOCK, 2 * deep_b * BLOCK
        outs, scratch = [bf(deep_a, 256)] * 2 + [bf(deep_b, 256)] * 2, [vm(2, deep_a, 128), vm(2, deep_b, 128)]
        return call(kernel, outs, args, scratch)

    pull_rims = rim_call(functools.partial(pull_rim_kernel, turning), 1, 2, (near_a, near_b))
    if turn:
        turn_rims = rim_call(functools.partial(rim_kernel, turning), RIM_A, RIM_B, (far_b, near_a))

    meta = jnp.zeros((2 * COLS, 128), F32)
    main, edge_a, edge_b = panels_in, near_a[96:128], near_b[96:128]
    stages = 2 * owners
    owner_of = [k if k < owners else stages - 1 - k for k in range(stages)]
    kept, result, k = [], None, 0
    while k < stages:
        owner, slot = owner_of[k], k % GROUP
        turns_here, turns_next = turn and k == owners - 1, turn and k + 1 == owners - 1
        if turns_here:
            first, main, send_b = call(
                functools.partial(turn_kernel, nb, owner, slot),
                [f32(ROWS, own), f32(ROWS, own + 256), f32(ROWS, 128)],
                (edge_b, main, edge_a, *own_tiles, *turn_rims, meta, expand),
            )
            kept += [first, main]
            meta = main[: 2 * COLS, own + 128 :]
            k += 2
        else:
            if k < owners:
                main, send_b, send_a = call(
                    functools.partial(push_kernel, nb, owner),
                    [f32(ROWS, own)] + [f32(ROWS, w) for w in ((256, 384) if turns_next else (128, 128))],
                    (edge_b, main, edge_a, near_b, near_a, *own_tiles),
                    [vm(2, 2 * BLOCK, 128)],
                    flops=PUSH,
                )
            else:
                (main,) = call(
                    functools.partial(pull_kernel, nb, owner),
                    [f32(ROWS, own)],
                    (edge_b, main, edge_a, *own_tiles, *pull_rims),
                )
                send_b, send_a = edges_of(main, 128, 128)
            (meta,) = call(
                functools.partial(note_kernel, nb, owner, slot, k < owners),
                [f32(2 * COLS, 128)],
                (main, meta, expand),
            )
            kept.append(main)
            k += 1
        share = not (turns_next and slot == 0)

        if k % GROUP == 0 or k == stages:
            todo = [(owner_of[i], i < owners) for i in range(k - len(kept), k)]
            every = jnp.broadcast_to(meta[None, :COLS], (count, COLS, 128))
            grams = lax.all_to_all(every, "space", 0, 0)
            pair = call(
                functools.partial(scale_kernel, todo, count * own), [f32(ROWS, own)] * 2, (grams, meta, *kept)
            )
            if result is None:
                result = pair
            else:
                live = [
                    functools.reduce(jnp.logical_or, [me == o for o, f in todo if f == way], jnp.bool_(False))
                    for way in (True, False)
                ]
                result = [jnp.where(c, new, old) for c, new, old in zip(live, pair, result)]
            main = pair[0 if k - 1 < owners else 1]
            send_b, send_a = edges_of(main, *((256, 384) if turn and k == owners - 1 else (128, 128)))
            meta, kept, share = jnp.zeros((2 * COLS, 128), F32), [], False
        if k == stages:
            break

        before, after = owner_of[k - 1], owner_of[k]
        if after != before:
            main = hop(main, before, after, lambda s: s)
        into_turn = turn and k == owners - 1
        (edge_b,) = call(
            aside_kernel,
            [f32(ROWS, 384 if into_turn else 128)],
            (hop(send_b, before, after, partner_b),) + ((turn_rims[0],) if into_turn else ()),
            flops=ASIDE_1 if into_turn else ASIDE_2,
        )
        if main.shape[1] > own:
            edge_a = main[:, own : own + 128]
            meta = meta + main[: 2 * COLS, own + 128 :]
        else:
            edge_a = hop(send_a, before, after, partner_a)
            if share and after != before:
                meta = meta + hop(meta, before, after, lambda s: s)
    return result[0][None], result[1][None]


def solution(mesh):
    return jax.shard_map(
        shards,
        mesh=mesh,
        in_specs=(
            P(None, "space"),
            P("tm", "space", None, None),
            P("tm", "space", None),
            P("tm", None, None, None),
        ),
        out_specs=(P("tm", None, "space"), P("tm", None, "space")),
        check_vma=False,
    )
```

```python
import functools

import jax
import jax.numpy as jnp
from jax import lax
from jax.experimental import pallas as pl
from jax.experimental.pallas import tpu as pltpu
from jax.sharding import PartitionSpec as P

BLOCK = 64
COLS = 8
PANELS = 4
ROWS = COLS * PANELS
RUN = 2
GROUP = 4
RIM_A, RIM_B = 5, 4
FAR_A, FAR_B = 3, 2
PUSH = 3 * 10**9
ASIDE_1, ASIDE_2 = 7 * 10**8, 5 * 10**8
DOWN = 2.0**-16
BF = jnp.bfloat16
F32 = jnp.float32
HIGH = lax.Precision.HIGHEST
NT = (((1,), (1,)), ((), ()))
NN = (((1,), (0,)), ((), ()))
TN = (((0,), (0,)), ((), ()))
VM = pl.BlockSpec(memory_space=pltpu.VMEM)


def call(kernel, outs, args, scratch=(), flops=10**6, far=0, limit=12):
    shapes = [jax.ShapeDtypeStruct(shape, dtype) for shape, dtype in outs]
    return pl.pallas_call(
        kernel,
        out_shape=shapes,
        in_specs=[pl.BlockSpec(memory_space=pltpu.HBM)] * far + [VM] * (len(args) - far),
        out_specs=[VM] * len(outs),
        scratch_shapes=list(scratch),
        compiler_params=pltpu.CompilerParams(vmem_limit_bytes=limit << 20),
        cost_estimate=pl.CostEstimate(flops=flops, bytes_accessed=10**5, transcendentals=0),
    )(*args)


def inside():
    place, last = lax.axis_index("space"), lax.axis_size("space") - 1
    return jnp.where((place == 0) | (place == last), 0.0, 1.0).astype(F32)


def parity():
    return lax.rem(lax.axis_index("space"), 2)


def iota(shape, dim):
    return lax.broadcasted_iota(jnp.int32, shape, dim)


def presence(mask, t, j, nb):
    place, last = lax.axis_index("space"), lax.axis_size("space") - 1
    here = jnp.broadcast_to(mask[j, t : t + 1, :], (nb, nb))
    diagonal = iota((nb, nb), 0) == iota((nb, nb), 1)
    column = jnp.sum(jnp.where(diagonal, here, 0), axis=1, keepdims=True).astype(F32)
    if j == 0:
        column = jnp.where((iota((nb, 1), 0) == 0) & (place == 0), 0.0, column)
    if j == 2:
        column = jnp.where((iota((nb, 1), 0) == nb - 1) & (place == last), 0.0, column)
    return column


def first_kernel(out):
    out[...] = jnp.zeros_like(out)


def edge_kernel(nb, turning, _, blocks, mask, panels, near_b, late_b, to_a, *far_b):
    width = panels.shape[1]
    turns = lax.axis_index("tm") == turning

    def near(dst, later, at, low_side, column, keep=1.0):
        edge = 0 if low_side else nb - 1
        inner = 1 if low_side else nb - 2
        rest = [(edge, 0), (edge, 1), (inner, 0)] if low_side else [(inner, 2), (edge, 1), (edge, 2)]
        slots = [(dst, 0, edge, j, j * 32) for j in range(3)]
        slots += [(later, 1, b, j, at + i * 32) for i, (b, j) in enumerate(rest)]
        for ref, t, b, j, start in slots:
            line = blocks[t, j, b : b + 1, :] * (column[t][j][b : b + 1, :] * keep)
            for r in range(32):
                ref[start + r : start + r + 1, :] = line[:, r * 128 : (r + 1) * 128]
        dst[96:128, :] = panels[:, :128] if low_side else panels[:, width - 128 :]

    for side in range(2):

        @pl.when((parity() == side) & jnp.logical_not(turns))
        def _():
            column = [[presence(mask, t, j, nb) for j in range(3)] for t in range(RUN)]
            near(near_b, late_b, 0, side == 0, column, inside())
            near(to_a, to_a, 128, side == 1, column)

    if not far_b:
        return

    @pl.when(turns)
    def _():
        even, odd = parity() == 0, parity() == 1
        keep = inside()
        for t, deep, start_a, wide, start_b in ((0, RIM_A, 0, FAR_A, 0), (1, RIM_B, 96 * RIM_A, FAR_B, 96 * FAR_A)):
            column = [jnp.broadcast_to(presence(mask, t, j, nb), (nb, 128)) for j in range(3)]
            for r in range(32):
                for j in range(3):
                    y = blocks[t, j, :, r * 128 : (r + 1) * 128] * column[j]
                    for dst, rows, start, tail_if in ((to_a, deep, start_a, even), (far_b[0], wide, start_b, odd)):
                        to = pl.ds(start + j * 32 + r, rows, stride=96)
                        dst[to, :] = jnp.where(tail_if, y[nb - rows :], y[:rows])
        far_b[0][...] = far_b[0][...] * keep


def banded(y, p):
    low = iota(y[0].shape, 1) < BLOCK
    zero = jnp.zeros_like(y[0])
    turned = [pltpu.roll(v, BLOCK, 1) for v in y]
    at_low, at_high = (y, turned) if p == 0 else (turned, y)
    first = (jnp.where(low, at_low[0], at_high[1]), jnp.where(low, at_low[2], zero))
    second = (jnp.where(low, zero, at_high[0]), jnp.where(low, at_low[1], at_high[2]))
    return first, second


def split2(x):
    high = x.astype(BF)
    return high, (x - high.astype(F32)).astype(BF)


def split3(x):
    first = x.astype(BF)
    x = x - first.astype(F32)
    second = x.astype(BF)
    return first, second, (x - second.astype(F32)).astype(BF)


def split_halves(wide, at, hi, lo):
    for half in range(2):
        lanes = slice(half * 128, half * 128 + 128)
        hi[:, lanes], lo[:, lanes] = split2(wide[at + half])


def own_kernel(nb, blocks, mask, mixing, a_hi, a_lo, b_hi, b_lo, expand, wide):
    for t, hi, lo in ((0, a_hi, a_lo), (1, b_hi, b_lo)):
        is_first = lax.rem(iota((nb, 128), 0), 2) == (1 - t)
        column = [jnp.broadcast_to(presence(mask, t, j, nb), (nb, 128)) for j in range(3)]
        for r in range(32):
            lanes = slice(r * 128, (r + 1) * 128)
            y = [blocks[t, j, :, lanes] * column[j] for j in range(3)]
            for p in range(2):
                first, second = banded(y, p)
                for half in range(2):
                    wide[2 * t + half, pl.ds(2 * r + p, nb, stride=BLOCK), :] = jnp.where(
                        is_first, first[half], second[half]
                    )
        split_halves(wide, 2 * t, hi, lo)
    pick = (lax.rem(iota((COLS, 128), 1), COLS) == iota((COLS, 128), 0)).astype(F32)
    row, lane = iota((ROWS, 128), 0), lax.rem(iota((ROWS, 128), 1), ROWS)
    same = (row // COLS) == (lane // COLS)
    step = []
    for t in range(RUN):
        m = mixing[t].reshape(ROWS, COLS)
        spread = lax.dot_general(m, pick, NN, precision=HIGH, preferred_element_type=F32)
        step.append((row == lane).astype(F32) - jnp.where(same, spread, 0.0))
    for i, (x, y) in enumerate(((step[0], step[1]), (step[1], step[0]))):
        e = lax.dot_general(x[:, :ROWS], y, NN, precision=HIGH, preferred_element_type=F32)
        expand[i * COLS : (i + 1) * COLS, :] = (
            e[0:COLS] + e[COLS : 2 * COLS] + e[2 * COLS : 3 * COLS] + e[3 * COLS :]
        )


def taken(from_a, from_b, left, at_a, at_b=None):
    use_b = (parity() == 0) == left
    at_b = at_a if at_b is None else at_b
    return jnp.where(use_b, from_b[at_b : at_b + 32, :], from_a[at_a : at_a + 32, :])


def rim_row(dst, index, first, y):
    for p in range(2):
        tiles = banded(y, p)[0 if first else 1]
        for half in range(2):
            dst[half, pl.ds(index * BLOCK + p, 32, stride=2), :] = tiles[half]


def edge_rows(near_a, near_b, dst):
    for left in (True, False):
        rim_row(dst, 1 - left, left, [taken(near_a, near_b, left, j * 32) for j in range(3)])


def rim_kernel(turning, far_b, far_a, a_hi, a_lo, b_hi, b_lo, wide_a, wide_b):
    none = jnp.zeros((32, 128), F32)

    @pl.when(lax.axis_index("tm") == turning)
    def _():
        for dst, deep, start_a, wide, start_b, odd in (
            (wide_a, RIM_A, 0, FAR_A, 0, 1),
            (wide_b, RIM_B, 96 * RIM_A, FAR_B, 96 * FAR_A, 0),
        ):
            for i in range(deep):
                for left in (True, False):
                    k = i - (deep - wide) if left else i
                    y = []
                    for j in range(3):
                        n, m = start_a + i * 96 + j * 32, start_b + k * 96 + j * 32
                        from_b = far_b[m : m + 32, :] if 0 <= k < wide else none
                        y.append(jnp.where((parity() == 0) == left, from_b, far_a[n : n + 32, :]))
                    place = i - deep if left else i
                    rim_row(dst, i if left else deep + i, place % 2 == odd, y)
        split_halves(wide_a, 0, a_hi, a_lo)
        split_halves(wide_b, 0, b_hi, b_lo)


def pull_rim_kernel(turning, near_a, near_b, late_b, a_hi, a_lo, b_hi, b_lo, wide_a, wide_b):
    @pl.when(lax.axis_index("tm") != turning)
    def _():
        edge_rows(near_a, near_b, wide_a)
        none = jnp.zeros((32, 128), F32)
        left = [taken(near_a, late_b, True, 128 + i * 32, i * 32) for i in range(3)]
        right = [taken(near_a, late_b, False, 128 + i * 32, i * 32) for i in range(3)]
        rim_row(wide_b, 0, True, [none, none, left[0]])
        rim_row(wide_b, 1, False, [none, left[1], left[2]])
        rim_row(wide_b, 2, True, [right[0], right[1], none])
        rim_row(wide_b, 3, False, [right[2], none, none])
        split_halves(wide_a, 0, a_hi, a_lo)
        split_halves(wide_b, 0, b_hi, b_lo)


def pair_tile(own, rim, depth, nb, b):
    def row(k):
        if 0 <= k < nb:
            return own[k * BLOCK : (k + 1) * BLOCK, :]
        k = k + depth if k < 0 else depth + k - nb
        return rim[k * BLOCK : (k + 1) * BLOCK, :]

    return jnp.concatenate([row(b), row(b + 1)], axis=0)


def product(x, w, dims):
    o = lax.dot_general(x, w, dims, preferred_element_type=F32)
    return (o[ROWS:, 128:] + o[ROWS:, :128] + o[:ROWS, 128:]) + o[:ROWS, :128]


def push(v, tiles):
    x = jnp.concatenate(split2(v), axis=0)
    outs = []
    for i, (hi, lo) in enumerate(tiles):
        outs.append(product(x[:, i * 128 : i * 128 + 256], jnp.concatenate([hi, lo], axis=0), NT))
    return jnp.concatenate(outs, axis=1)


def pull(v, tiles):
    x = jnp.concatenate(split2(v), axis=0)
    outs = []
    for i in range(len(tiles) - 1):
        parts = [
            jnp.concatenate([tiles[i][s][:, 128:], tiles[i + 1][s][:, :128]], axis=0) for s in range(2)
        ]
        outs.append(product(x[:, i * 128 : i * 128 + 256], jnp.concatenate(parts, axis=1), NN))
    return jnp.concatenate(outs, axis=1)


def tiles_of(refs, depth, nb, first, last):
    own_hi, own_lo, rim_hi, rim_lo = refs
    return [
        (pair_tile(own_hi, rim_hi, depth, nb, b), pair_tile(own_lo, rim_lo, depth, nb, b))
        for b in range(first, last, 2)
    ]


def gram(u):
    high, low = split2(u)
    o = lax.dot_general(
        jnp.concatenate([low, high], axis=0),
        jnp.concatenate([low] * 4 + [high] * 4, axis=0),
        NT,
        preferred_element_type=F32,
    )
    total = (o[:ROWS, :128] + o[:ROWS, 128:] + o[ROWS:, :128]) + o[ROWS:, 128:]
    panel = lax.rem(iota((COLS, 128), 1), ROWS) // COLS
    out = jnp.zeros((COLS, 128), F32)
    for p in range(PANELS):
        out = out + jnp.where(panel == p, total[p * COLS : (p + 1) * COLS], 0.0)
    return out


def noted(g, e, slot, new_g, new_e):
    mine = (iota((COLS, 128), 1) // ROWS) == slot
    return jnp.where(mine, new_g, g), jnp.where(mine, new_e, e)


def panels_of(ref, own):
    if ref.shape[0] == ROWS:
        return ref[:, :own]
    return jnp.concatenate([ref[i * ROWS : (i + 1) * ROWS, :] for i in range(own // 128)], axis=1)


def by_side(e_a, e_b):
    even = parity() == 0
    return jnp.where(even, e_b, e_a), jnp.where(even, e_a, e_b)


def aside_kernel(edge, *refs):
    out = refs[-1]
    width, wanted = edge.shape[1], out.shape[1]
    if width == wanted:
        out[...] = edge[...]
        return
    none = jnp.zeros((ROWS, wanted - width), F32)
    left = jnp.concatenate([none, edge[...]], axis=1)
    right = jnp.concatenate([edge[...], none], axis=1)
    out[...] = jnp.where(parity() == 0, left, right)


def push_kernel(nb, owner, edge_b, main, edge_a, near_b, near_a, a_hi, a_lo, b_hi, b_lo, out, out_b, out_a, wide):
    own = nb * BLOCK

    @pl.when(lax.axis_index("tm") == owner)
    def _():
        edge_rows(near_a, near_b, wide)
        rim_hi, rim_lo = split2(jnp.concatenate([wide[0], wide[1]], axis=1))
        left, right = by_side(edge_a[...], edge_b[...])
        v = jnp.concatenate([left, main[:, :own], right], axis=1)
        w = push(v, tiles_of((a_hi, a_lo, rim_hi, rim_lo), 1, nb, -1, nb))
        u = push(w, tiles_of((b_hi, b_lo, None, None), 0, nb, 0, nb))
        out[...] = u
        wide_b, wide_a = out_b.shape[1], out_a.shape[1]
        out_b[...] = by_side(u[:, :wide_b], u[:, own - wide_b :])[1]
        out_a[...] = by_side(u[:, own - wide_a :], u[:, :wide_a])[1]


def turn_kernel(nb, owner, slot, edge_b, main, edge_a, a_hi, a_lo, b_hi, b_lo, ra_hi, ra_lo, rb_hi, rb_lo,
                old, expand, first, out, out_b):
    own = nb * BLOCK
    end = own + 128
    pieces = own // 128
    record = slice((pieces + 1) * ROWS, (pieces + 1) * ROWS + 2 * COLS)

    @pl.when(lax.axis_index("tm") != owner)
    def _():
        out[record, :] = old[...]

    @pl.when(lax.axis_index("tm") == owner)
    def _():
        left, right = by_side(edge_a[...], edge_b[...])
        v = jnp.concatenate([left, main[:, :own], right], axis=1)
        tiles_a = tiles_of((a_hi, a_lo, ra_hi, ra_lo), RIM_A, nb, -RIM_A, nb + RIM_A)
        tiles_b = tiles_of((b_hi, b_lo, rb_hi, rb_lo), RIM_B, nb, -RIM_B, nb + RIM_B)
        u = push(push(v, tiles_a), tiles_b)
        u_own = u[:, 256 : 256 + own]
        first[...] = u_own
        back = pull(pull(u * DOWN, tiles_b), tiles_a[1:-1])
        back_own = back[:, 128 : 128 + own]
        for i in range(pieces):
            out[i * ROWS : (i + 1) * ROWS, :] = back_own[:, i * 128 : (i + 1) * 128]
        out[pieces * ROWS : (pieces + 1) * ROWS, :] = by_side(back[:, end:], back[:, :128])[1]
        out_b[...] = by_side(back[:, 128:256], back[:, own:end])[1]
        g, e = noted(old[:COLS], old[COLS:], slot, gram(u_own), expand[:COLS])
        g, e = noted(g, e, slot + 1, gram(back_own), expand[COLS:] * (1.0 / DOWN))
        out[record, :] = jnp.concatenate([g, e], axis=0)


def pull_kernel(nb, owner, edge_b, main, edge_a, a_hi, a_lo, b_hi, b_lo, ra_hi, ra_lo, rb_hi, rb_lo, out):
    own = nb * BLOCK

    @pl.when(lax.axis_index("tm") == owner)
    def _():
        left, right = by_side(edge_a[...], edge_b[...])
        v = jnp.concatenate([left, panels_of(main, own), right], axis=1)
        y = pull(v, tiles_of((b_hi, b_lo, rb_hi, rb_lo), 2, nb, -2, nb + 2))
        out[...] = pull(y, tiles_of((a_hi, a_lo, ra_hi, ra_lo), 1, nb, -1, nb + 1))


def note_kernel(nb, owner, slot, forward, u, old, expand, out):
    @pl.when(lax.axis_index("tm") != owner)
    def _():
        out[...] = old[...]

    @pl.when(lax.axis_index("tm") == owner)
    def _():
        e = expand[:COLS] if forward else expand[COLS:]
        out[:COLS], out[COLS:] = noted(old[:COLS], old[COLS:], slot, gram(u[:, : nb * BLOCK]), e)


def exact(x, y):
    m = x.shape[0]
    o = lax.dot_general(
        jnp.concatenate(split3(x), axis=0), jnp.concatenate(split3(y), axis=1), NN, preferred_element_type=F32
    )
    piece = [[o[i * m : (i + 1) * m, j * 128 : (j + 1) * 128] for j in range(3)] for i in range(3)]
    small = (piece[0][2] + piece[2][0]) + piece[1][1]
    return (small + (piece[0][1] + piece[1][0])) + piece[0][0]


def scale_kernel(stages, boxes, grams, meta, *refs):
    panels, (out_f, out_a) = refs[: len(stages)], refs[len(stages) :]
    own = out_f.shape[1]
    parts = [grams[i] for i in range(grams.shape[0])]
    while len(parts) > 1:
        parts = [a + b for a, b in zip(parts[::2], parts[1::2])] + parts[len(parts) // 2 * 2 :]
    total = parts[0] * (1.0 / boxes)
    growth = meta[COLS:, :]
    row, lane = iota((ROWS, 128), 0), iota((ROWS, 128), 1)
    same = (row // COLS) == (lax.rem(lane, ROWS) // COLS)
    me = lax.axis_index("tm")

    def full(x, n):
        turns = [x if k == n else pltpu.roll(x, ((k - n) % 4) * ROWS, 1) for k in range(4)]
        group = lane[:COLS] // ROWS
        spread = turns[0]
        for k in range(1, 4):
            spread = jnp.where(group == k, turns[k], spread)
        return jnp.where(same, jnp.concatenate([spread] * PANELS, axis=0), 0.0)

    count = len(stages)
    h = full(growth, 0)
    stack = jnp.concatenate([h, exact(jnp.concatenate([full(total, n)[:, :ROWS] for n in range(count)], axis=0), h)])
    select = {True: None, False: None}
    for n, (owner, forward) in enumerate(stages):
        if n:
            stack = exact(stack[:, :ROWS], full(growth, n))
        square = jnp.sum(stack[:ROWS] * stack[ROWS : 2 * ROWS], axis=0, keepdims=True)
        scale = lax.rsqrt(jnp.maximum(square, 0.0) + 1e-06)
        later = [stack[2 * ROWS :]] if n + 1 < count else []
        stack = jnp.concatenate([stack[:ROWS]] + later, axis=0) * scale
        back, u = stack[:ROWS], panels_of(panels[n], own)
        old = select[forward]
        select[forward] = (back, u) if old is None else (
            jnp.where(me == owner, back, old[0]), jnp.where(me == owner, u, old[1])
        )
    for forward, out in ((True, out_f), (False, out_a)):
        if select[forward] is None:
            out[...] = jnp.zeros_like(out)
        else:
            back, u = select[forward]
            left = jnp.concatenate(split2(back[:, :ROWS].T), axis=0)
            o = lax.dot_general(left, jnp.concatenate(split2(u), axis=1), NN, preferred_element_type=F32)
            out[...] = (o[ROWS:, own:] + o[ROWS:, :own] + o[:ROWS, own:]) + o[:ROWS, :own]


def shards(panels_in, blocks, block_mask, mixing):
    owners, count = lax.axis_size("tm"), lax.axis_size("space")
    me, place = lax.axis_index("tm"), lax.axis_index("space")
    nb, own = blocks.shape[1], panels_in.shape[1]
    even = lax.rem(place, 2) == 0
    bf, f32 = (lambda *s: (s, BF)), (lambda *s: (s, F32))

    def partner_a(s):
        return s ^ 1

    def partner_b(s):
        t = s + 1 if s % 2 else s - 1
        return t if 0 <= t < count else s

    def beside(x, to, only=None):
        route = [(t * count + s, t * count + to(s)) for t in (only or range(owners)) for s in range(count)]
        return lax.ppermute(x, ("tm", "space"), route)

    def hop(x, t, o, to):
        pairs = [(t, o), (o, t)] if t != o else [(t, t)]
        return lax.ppermute(x, ("tm", "space"), [(i * count + s, k * count + to(s)) for i, k in pairs for s in range(count)])

    def edges_of(x, wide_b, wide_a):
        return (
            jnp.where(even, x[:, :wide_b], x[:, own - wide_b : own]),
            jnp.where(even, x[:, own - wide_a : own], x[:, :wide_a]),
        )

    rows, mask = blocks.transpose(0, 2, 1, 3), block_mask.transpose(2, 0, 1)
    vm = lambda *s: pltpu.VMEM(s, F32)
    turn = owners % GROUP != 0
    turning = owners - 1 if turn else owners
    begin = call(first_kernel, [f32(8, 128)], (), flops=10**9)
    sizes = [128, 96] + ([96 * (RIM_A + RIM_B), 96 * (FAR_A + FAR_B)] if turn else [224])
    edges = call(
        functools.partial(edge_kernel, nb, turning),
        [f32(n, 128) for n in sizes],
        (*begin, rows, mask, panels_in),
    )
    near_b, near_a = beside(edges[0], partner_b, range(turning)), beside(edges[2], partner_a)
    if turn:
        far_b = beside(edges[3], partner_b, [turning])
    rows, mask, mixing, _ = lax.optimization_barrier((rows, mask, mixing, edges))
    *own_tiles, expand = call(
        functools.partial(own_kernel, nb),
        [bf(own, 256)] * 4 + [f32(2 * COLS, 128)],
        (rows, mask, mixing),
        [vm(2 * RUN, own, 128)],
    )

    def rim_call(kernel, deep_a, deep_b, args):
        deep_a, deep_b = 2 * deep_a * BLOCK, 2 * deep_b * BLOCK
        outs, scratch = [bf(deep_a, 256)] * 2 + [bf(deep_b, 256)] * 2, [vm(2, deep_a, 128), vm(2, deep_b, 128)]
        return call(kernel, outs, args, scratch)

    def late_rims(after):
        late, _ = lax.optimization_barrier((edges[1], after))
        args = (near_a, near_b, beside(late, partner_b, range(turning)))
        return rim_call(functools.partial(pull_rim_kernel, turning), 1, 2, args)

    pull_rims = None
    if turn:
        turn_rims = rim_call(functools.partial(rim_kernel, turning), RIM_A, RIM_B, (far_b, near_a))

    meta = jnp.zeros((2 * COLS, 128), F32)
    main, edge_a, edge_b = panels_in, near_a[96:128], near_b[96:128]
    stages = 2 * owners
    owner_of = [k if k < owners else stages - 1 - k for k in range(stages)]
    kept, result, k = [], None, 0
    record = ROWS * (own // 128 + 1)
    while k < stages:
        owner, slot, turned = owner_of[k], k % GROUP, False
        turns_here, turns_next = turn and k == owners - 1, turn and k + 1 == owners - 1
        if turns_here:
            first, main, send_b = call(
                functools.partial(turn_kernel, nb, owner, slot),
                [f32(ROWS, own), f32(record + 2 * COLS, 128), f32(ROWS, 128)],
                (edge_b, main, edge_a, *own_tiles, *turn_rims, meta, expand),
            )
            kept += [first, main]
            turned = True
            meta = main[record:]
            k += 2
        else:
            if k < owners:
                main, send_b, send_a = call(
                    functools.partial(push_kernel, nb, owner),
                    [f32(ROWS, own)] + [f32(ROWS, w) for w in ((256, 384) if turns_next else (128, 128))],
                    (edge_b, main, edge_a, near_b, near_a, *own_tiles),
                    [vm(2, 2 * BLOCK, 128)],
                    flops=PUSH,
                )
                if pull_rims is None:
                    pull_rims = late_rims(send_b)
            else:
                (main,) = call(
                    functools.partial(pull_kernel, nb, owner),
                    [f32(ROWS, own)],
                    (edge_b, main, edge_a, *own_tiles, *pull_rims),
                )
                send_b, send_a = edges_of(main, 128, 128)
            (meta,) = call(
                functools.partial(note_kernel, nb, owner, slot, k < owners),
                [f32(2 * COLS, 128)],
                (main, meta, expand),
            )
            kept.append(main)
            k += 1
        share = not (turns_next and slot == 0)

        if k % GROUP == 0 or k == stages:
            todo = [(owner_of[i], i < owners) for i in range(k - len(kept), k)]
            every = jnp.broadcast_to(meta[None, :COLS], (count, COLS, 128))
            grams = lax.all_to_all(every, "space", 0, 0)
            pair = call(
                functools.partial(scale_kernel, todo, count * own), [f32(ROWS, own)] * 2, (grams, meta, *kept)
            )
            if result is None:
                result = pair
            else:
                live = [
                    functools.reduce(jnp.logical_or, [me == o for o, f in todo if f == way], jnp.bool_(False))
                    for way in (True, False)
                ]
                result = [jnp.where(c, new, old) for c, new, old in zip(live, pair, result)]
            main = pair[0 if k - 1 < owners else 1]
            send_b, send_a = edges_of(main, *((256, 384) if turn and k == owners - 1 else (128, 128)))
            meta, kept, share, turned = jnp.zeros((2 * COLS, 128), F32), [], False, False
        if k == stages:
            break

        before, after = owner_of[k - 1], owner_of[k]
        if after != before:
            main = hop(main, before, after, lambda s: s)
        into_turn = turn and k == owners - 1
        wide_a = 384 if into_turn else 128
        (edge_b,) = call(
            aside_kernel,
            [f32(ROWS, wide_a)],
            (hop(send_b, before, after, partner_b),) + ((turn_rims[0],) if into_turn else ()),
            flops=ASIDE_1 if into_turn else ASIDE_2,
        )
        if turned:
            edge_a = main[record - ROWS : record]
            meta = meta + main[record:]
        else:
            edge_a = hop(send_a, before, after, partner_a)
            if share and after != before:
                meta = meta + hop(meta, before, after, lambda s: s)
    return result[0][None], result[1][None]


def solution(mesh):
    return jax.shard_map(
        shards,
        mesh=mesh,
        in_specs=(
            P(None, "space"),
            P("tm", "space", None, None),
            P("tm", "space", None),
            P("tm", None, None, None),
        ),
        out_specs=(P("tm", None, "space"), P("tm", None, "space")),
        check_vma=False,
    )
```

```python
import functools

import jax
import jax.numpy as jnp
from jax import lax
from jax.experimental import pallas as pl
from jax.experimental.pallas import tpu as pltpu
from jax.sharding import PartitionSpec as P

BLOCK = 64
COLS = 8
PANELS = 4
ROWS = COLS * PANELS
RUN = 2
GROUP = 4
RIM_A, RIM_B = 5, 4
FAR_A, FAR_B = 3, 2
PUSH = 3 * 10**9
ASIDE_0 = 10**10
ASIDE_1, ASIDE_2 = 7 * 10**8, 5 * 10**8
DOWN = 2.0**-16
BF = jnp.bfloat16
F32 = jnp.float32
HIGH = lax.Precision.HIGHEST
NT = (((1,), (1,)), ((), ()))
NN = (((1,), (0,)), ((), ()))
TN = (((0,), (0,)), ((), ()))
VM = pl.BlockSpec(memory_space=pltpu.VMEM)


def call(kernel, outs, args, scratch=(), flops=10**6, far=0, limit=12):
    shapes = [jax.ShapeDtypeStruct(shape, dtype) for shape, dtype in outs]
    return pl.pallas_call(
        kernel,
        out_shape=shapes,
        in_specs=[pl.BlockSpec(memory_space=pltpu.HBM)] * far + [VM] * (len(args) - far),
        out_specs=[VM] * len(outs),
        scratch_shapes=list(scratch),
        compiler_params=pltpu.CompilerParams(vmem_limit_bytes=limit << 20),
        cost_estimate=pl.CostEstimate(flops=flops, bytes_accessed=10**5, transcendentals=0),
    )(*args)


def inside():
    place, last = lax.axis_index("space"), lax.axis_size("space") - 1
    return jnp.where((place == 0) | (place == last), 0.0, 1.0).astype(F32)


def parity():
    return lax.rem(lax.axis_index("space"), 2)


def iota(shape, dim):
    return lax.broadcasted_iota(jnp.int32, shape, dim)


def presence(mask, t, j, nb):
    place, last = lax.axis_index("space"), lax.axis_size("space") - 1
    here = jnp.broadcast_to(mask[j, t : t + 1, :], (nb, nb))
    diagonal = iota((nb, nb), 0) == iota((nb, nb), 1)
    column = jnp.sum(jnp.where(diagonal, here, 0), axis=1, keepdims=True).astype(F32)
    if j == 0:
        column = jnp.where((iota((nb, 1), 0) == 0) & (place == 0), 0.0, column)
    if j == 2:
        column = jnp.where((iota((nb, 1), 0) == nb - 1) & (place == last), 0.0, column)
    return column


def first_kernel(out):
    out[...] = jnp.zeros_like(out)


def block_of(blocks, column, t, j, b, nb):
    return blocks[t, j, pl.ds(b, BLOCK // 2, stride=nb), :] * column[t][j][b : b + 1, :]


def edge_kernel(nb, turning, _, blocks, mask, panels, near_b, late_b, to_a, *far_b):
    width = panels.shape[1]
    turns = lax.axis_index("tm") == turning
    column = [[presence(mask, t, j, nb) for j in range(3)] for t in range(RUN)]

    def near(dst, later, at, low_side, keep=1.0):
        edge = 0 if low_side else nb - 1
        inner = 1 if low_side else nb - 2
        for j in range(3):
            dst[j * 32 : (j + 1) * 32, :] = block_of(blocks, column, 0, j, edge, nb) * keep
        dst[96:128, :] = panels[:, :128] if low_side else panels[:, width - 128 :]
        rest = [(edge, 0), (edge, 1), (inner, 0)] if low_side else [(inner, 2), (edge, 1), (edge, 2)]
        for i, (b, j) in enumerate(rest):
            later[at + i * 32 : at + (i + 1) * 32, :] = block_of(blocks, column, 1, j, b, nb) * keep

    def far(dst, deep_a, deep_b, low_side, keep=1.0):
        at = 0
        for t, deep in ((0, deep_a), (1, deep_b)):
            for b in range(deep) if low_side else range(nb - deep, nb):
                for j in range(3):
                    dst[at : at + 32, :] = block_of(blocks, column, t, j, b, nb) * keep
                    at += 32

    for side in range(2):

        @pl.when((parity() == side) & jnp.logical_not(turns))
        def _():
            near(near_b, late_b, 0, side == 0, inside())
            near(to_a, to_a, 128, side == 1)

        if far_b:

            @pl.when((parity() == side) & turns)
            def _():
                far(far_b[0], FAR_A, FAR_B, side == 0, inside())
                far(to_a, RIM_A, RIM_B, side == 1)


def banded(y, p):
    low = iota(y[0].shape, 1) < BLOCK
    zero = jnp.zeros_like(y[0])
    turned = [pltpu.roll(v, BLOCK, 1) for v in y]
    at_low, at_high = (y, turned) if p == 0 else (turned, y)
    first = (jnp.where(low, at_low[0], at_high[1]), jnp.where(low, at_low[2], zero))
    second = (jnp.where(low, zero, at_high[0]), jnp.where(low, at_low[1], at_high[2]))
    return first, second


def split2(x):
    high = x.astype(BF)
    return high, (x - high.astype(F32)).astype(BF)


def split3(x):
    first = x.astype(BF)
    x = x - first.astype(F32)
    second = x.astype(BF)
    return first, second, (x - second.astype(F32)).astype(BF)


def split_halves(wide, at, hi, lo):
    for half in range(2):
        lanes = slice(half * 128, half * 128 + 128)
        hi[:, lanes], lo[:, lanes] = split2(wide[at + half])


def own_kernel(nb, blocks, mask, mixing, a_hi, a_lo, b_hi, b_lo, expand, *wide):
    column = [[presence(mask, t, j, nb) for j in range(3)] for t in range(RUN)]
    for t, hi, lo in ((0, a_hi, a_lo), (1, b_hi, b_lo)):
        for b in range(nb):
            rim_row(wide[t], b, b % 2 == 1 - t, [block_of(blocks, column, t, j, b, nb) for j in range(3)])
        split_halves(wide[t], 0, hi, lo)
    pick = (lax.rem(iota((COLS, 128), 1), COLS) == iota((COLS, 128), 0)).astype(F32)
    row, lane = iota((ROWS, 128), 0), lax.rem(iota((ROWS, 128), 1), ROWS)
    same = (row // COLS) == (lane // COLS)
    step = []
    for t in range(RUN):
        m = mixing[t].reshape(ROWS, COLS)
        spread = lax.dot_general(m, pick, NN, precision=HIGH, preferred_element_type=F32)
        step.append((row == lane).astype(F32) - jnp.where(same, spread, 0.0))
    for i, (x, y) in enumerate(((step[0], step[1]), (step[1], step[0]))):
        e = lax.dot_general(x[:, :ROWS], y, NN, precision=HIGH, preferred_element_type=F32)
        expand[i * COLS : (i + 1) * COLS, :] = (
            e[0:COLS] + e[COLS : 2 * COLS] + e[2 * COLS : 3 * COLS] + e[3 * COLS :]
        )


def taken(from_a, from_b, left, at_a, at_b=None):
    use_b = (parity() == 0) == left
    at_b = at_a if at_b is None else at_b
    return jnp.where(use_b, from_b[at_b : at_b + 32, :], from_a[at_a : at_a + 32, :])


def rim_row(dst, index, first, y):
    for p in range(2):
        tiles = banded(y, p)[0 if first else 1]
        for half in range(2):
            dst[half, pl.ds(index * BLOCK + p, 32, stride=2), :] = tiles[half]


def edge_rows(near_a, near_b, dst):
    for left in (True, False):
        rim_row(dst, 1 - left, left, [taken(near_a, near_b, left, j * 32) for j in range(3)])


def rim_kernel(turning, far_b, far_a, a_hi, a_lo, b_hi, b_lo, wide_a, wide_b):
    none = jnp.zeros((32, 128), F32)

    @pl.when(lax.axis_index("tm") == turning)
    def _():
        for dst, deep, start_a, wide, start_b, odd in (
            (wide_a, RIM_A, 0, FAR_A, 0, 1),
            (wide_b, RIM_B, 96 * RIM_A, FAR_B, 96 * FAR_A, 0),
        ):
            for i in range(deep):
                for left in (True, False):
                    k = i - (deep - wide) if left else i
                    y = []
                    for j in range(3):
                        n, m = start_a + i * 96 + j * 32, start_b + k * 96 + j * 32
                        from_b = far_b[m : m + 32, :] if 0 <= k < wide else none
                        y.append(jnp.where((parity() == 0) == left, from_b, far_a[n : n + 32, :]))
                    place = i - deep if left else i
                    rim_row(dst, i if left else deep + i, place % 2 == odd, y)
        split_halves(wide_a, 0, a_hi, a_lo)
        split_halves(wide_b, 0, b_hi, b_lo)


def pull_rim_kernel(turning, near_a, near_b, late_b, a_hi, a_lo, b_hi, b_lo, wide_a, wide_b):
    @pl.when(lax.axis_index("tm") != turning)
    def _():
        edge_rows(near_a, near_b, wide_a)
        none = jnp.zeros((32, 128), F32)
        left = [taken(near_a, late_b, True, 128 + i * 32, i * 32) for i in range(3)]
        right = [taken(near_a, late_b, False, 128 + i * 32, i * 32) for i in range(3)]
        rim_row(wide_b, 0, True, [none, none, left[0]])
        rim_row(wide_b, 1, False, [none, left[1], left[2]])
        rim_row(wide_b, 2, True, [right[0], right[1], none])
        rim_row(wide_b, 3, False, [right[2], none, none])
        split_halves(wide_a, 0, a_hi, a_lo)
        split_halves(wide_b, 0, b_hi, b_lo)


def pair_tile(own, rim, depth, nb, b):
    def row(k):
        if 0 <= k < nb:
            return own[k * BLOCK : (k + 1) * BLOCK, :]
        k = k + depth if k < 0 else depth + k - nb
        return rim[k * BLOCK : (k + 1) * BLOCK, :]

    return jnp.concatenate([row(b), row(b + 1)], axis=0)


def product(x, w, dims):
    o = lax.dot_general(x, w, dims, preferred_element_type=F32)
    return (o[ROWS:, 128:] + o[ROWS:, :128] + o[:ROWS, 128:]) + o[:ROWS, :128]


def push(v, tiles):
    x = jnp.concatenate(split2(v), axis=0)
    outs = []
    for i, (hi, lo) in enumerate(tiles):
        outs.append(product(x[:, i * 128 : i * 128 + 256], jnp.concatenate([hi, lo], axis=0), NT))
    return jnp.concatenate(outs, axis=1)


def pull(v, tiles):
    x = jnp.concatenate(split2(v), axis=0)
    outs = []
    for i in range(len(tiles) - 1):
        parts = [
            jnp.concatenate([tiles[i][s][:, 128:], tiles[i + 1][s][:, :128]], axis=0) for s in range(2)
        ]
        outs.append(product(x[:, i * 128 : i * 128 + 256], jnp.concatenate(parts, axis=1), NN))
    return jnp.concatenate(outs, axis=1)


def tiles_of(refs, depth, nb, first, last):
    own_hi, own_lo, rim_hi, rim_lo = refs
    return [
        (pair_tile(own_hi, rim_hi, depth, nb, b), pair_tile(own_lo, rim_lo, depth, nb, b))
        for b in range(first, last, 2)
    ]


def gram(u):
    high, low = split2(u)
    o = lax.dot_general(
        jnp.concatenate([low, high], axis=0),
        jnp.concatenate([low] * 4 + [high] * 4, axis=0),
        NT,
        preferred_element_type=F32,
    )
    total = (o[:ROWS, :128] + o[:ROWS, 128:] + o[ROWS:, :128]) + o[ROWS:, 128:]
    panel = lax.rem(iota((COLS, 128), 1), ROWS) // COLS
    out = jnp.zeros((COLS, 128), F32)
    for p in range(PANELS):
        out = out + jnp.where(panel == p, total[p * COLS : (p + 1) * COLS], 0.0)
    return out


def noted(g, e, slot, new_g, new_e):
    mine = (iota((COLS, 128), 1) // ROWS) == slot
    return jnp.where(mine, new_g, g), jnp.where(mine, new_e, e)


def panels_of(ref, own):
    if ref.shape[0] == ROWS:
        return ref[:, :own]
    return jnp.concatenate([ref[i * ROWS : (i + 1) * ROWS, :] for i in range(own // 128)], axis=1)


def by_side(e_a, e_b):
    even = parity() == 0
    return jnp.where(even, e_b, e_a), jnp.where(even, e_a, e_b)


def aside_kernel(edge, *refs):
    out = refs[-1]
    width, wanted = edge.shape[1], out.shape[1]
    if width == wanted:
        out[...] = edge[...]
        return
    none = jnp.zeros((ROWS, wanted - width), F32)
    left = jnp.concatenate([none, edge[...]], axis=1)
    right = jnp.concatenate([edge[...], none], axis=1)
    out[...] = jnp.where(parity() == 0, left, right)


def push_kernel(nb, owner, edge_b, main, edge_a, near_b, near_a, a_hi, a_lo, b_hi, b_lo, out, out_b, out_a, wide):
    own = nb * BLOCK

    @pl.when(lax.axis_index("tm") == owner)
    def _():
        edge_rows(near_a, near_b, wide)
        rim_hi, rim_lo = split2(jnp.concatenate([wide[0], wide[1]], axis=1))
        left, right = by_side(edge_a[...], edge_b[...])
        v = jnp.concatenate([left, main[:, :own], right], axis=1)
        w = push(v, tiles_of((a_hi, a_lo, rim_hi, rim_lo), 1, nb, -1, nb))
        u = push(w, tiles_of((b_hi, b_lo, None, None), 0, nb, 0, nb))
        out[...] = u
        wide_b, wide_a = out_b.shape[1], out_a.shape[1]
        out_b[...] = by_side(u[:, :wide_b], u[:, own - wide_b :])[1]
        out_a[...] = by_side(u[:, own - wide_a :], u[:, :wide_a])[1]


def turn_kernel(nb, owner, slot, edge_b, main, edge_a, a_hi, a_lo, b_hi, b_lo, ra_hi, ra_lo, rb_hi, rb_lo,
                old, expand, first, out, out_b):
    own = nb * BLOCK
    end = own + 128
    pieces = own // 128
    record = slice((pieces + 1) * ROWS, (pieces + 1) * ROWS + 2 * COLS)

    @pl.when(lax.axis_index("tm") != owner)
    def _():
        out[record, :] = old[...]

    @pl.when(lax.axis_index("tm") == owner)
    def _():
        left, right = by_side(edge_a[...], edge_b[...])
        v = jnp.concatenate([left, main[:, :own], right], axis=1)
        tiles_a = tiles_of((a_hi, a_lo, ra_hi, ra_lo), RIM_A, nb, -RIM_A, nb + RIM_A)
        tiles_b = tiles_of((b_hi, b_lo, rb_hi, rb_lo), RIM_B, nb, -RIM_B, nb + RIM_B)
        u = push(push(v, tiles_a), tiles_b)
        u_own = u[:, 256 : 256 + own]
        first[...] = u_own
        back = pull(pull(u * DOWN, tiles_b), tiles_a[1:-1])
        back_own = back[:, 128 : 128 + own]
        for i in range(pieces):
            out[i * ROWS : (i + 1) * ROWS, :] = back_own[:, i * 128 : (i + 1) * 128]
        out[pieces * ROWS : (pieces + 1) * ROWS, :] = by_side(back[:, end:], back[:, :128])[1]
        out_b[...] = by_side(back[:, 128:256], back[:, own:end])[1]
        g, e = noted(old[:COLS], old[COLS:], slot, gram(u_own), expand[:COLS])
        g, e = noted(g, e, slot + 1, gram(back_own), expand[COLS:] * (1.0 / DOWN))
        out[record, :] = jnp.concatenate([g, e], axis=0)


def pull_kernel(nb, owner, slot, edge_b, main, edge_a, a_hi, a_lo, b_hi, b_lo, ra_hi, ra_lo, rb_hi, rb_lo,
                old, expand, out, record, *every):
    own = nb * BLOCK

    @pl.when(lax.axis_index("tm") != owner)
    def _():
        record[...] = old[...]

    @pl.when(lax.axis_index("tm") == owner)
    def _():
        left, right = by_side(edge_a[...], edge_b[...])
        v = jnp.concatenate([left, panels_of(main, own), right], axis=1)
        y = pull(v, tiles_of((b_hi, b_lo, rb_hi, rb_lo), 2, nb, -2, nb + 2))
        u = pull(y, tiles_of((a_hi, a_lo, ra_hi, ra_lo), 1, nb, -1, nb + 1))
        out[...] = u
        record[:COLS], record[COLS:] = noted(old[:COLS], old[COLS:], slot, gram(u), expand[COLS:])

    for ref in every:
        for i in range(ref.shape[0]):
            ref[i] = record[:COLS]


def note_kernel(nb, owner, slot, u, old, expand, out):
    @pl.when(lax.axis_index("tm") != owner)
    def _():
        out[...] = old[...]

    @pl.when(lax.axis_index("tm") == owner)
    def _():
        out[:COLS], out[COLS:] = noted(old[:COLS], old[COLS:], slot, gram(u[:, : nb * BLOCK]), expand[:COLS])


def exact(x, y):
    rows = x.shape[0]
    m = -(-rows // 16) * 16
    if m > rows:
        x = jnp.concatenate([x, jnp.zeros((m - rows, x.shape[1]), F32)], axis=0)
    o = lax.dot_general(
        jnp.concatenate(split3(x), axis=0), jnp.concatenate(split3(y), axis=1), NN, preferred_element_type=F32
    )
    piece = [[o[i * m : i * m + rows, j * 128 : (j + 1) * 128] for j in range(3)] for i in range(3)]
    small = (piece[0][2] + piece[2][0]) + piece[1][1]
    return (small + (piece[0][1] + piece[1][0])) + piece[0][0]


def scale_kernel(stages, boxes, grams, meta, *refs):
    panels, (out_f, out_a) = refs[: len(stages)], refs[len(stages) :]
    own = out_f.shape[1]
    parts = [grams[i] for i in range(grams.shape[0])]
    while len(parts) > 1:
        parts = [a + b for a, b in zip(parts[::2], parts[1::2])] + parts[len(parts) // 2 * 2 :]
    total = parts[0] * (1.0 / boxes)
    growth = meta[COLS:, :]
    row, lane = iota((ROWS, 128), 0), iota((ROWS, 128), 1)
    same = (row // COLS) == (lax.rem(lane, ROWS) // COLS)
    group = lane[:COLS] // ROWS
    me = lax.axis_index("tm")

    def spread(x, n):
        turns = [x if k == n else pltpu.roll(x, ((k - n) % 4) * ROWS, 1) for k in range(4)]
        out = turns[0]
        for k in range(1, 4):
            out = jnp.where(group == k, turns[k], out)
        return out

    def full(x):
        return jnp.where(same, jnp.concatenate([x] * PANELS, axis=0), 0.0)

    count = len(stages)
    grow = [spread(growth, n) for n in range(count)]
    products = jnp.concatenate([spread(total, n)[:, :ROWS] for n in range(count)], axis=0)
    stack = jnp.concatenate([grow[0], exact(products, full(grow[0]))], axis=0)
    select = {True: None, False: None}
    for n, (owner, forward) in enumerate(stages):
        if n:
            stack = exact(stack[:, :ROWS], full(grow[n]))
        square = jnp.sum(stack[:COLS] * stack[COLS : 2 * COLS], axis=0, keepdims=True)
        scale = lax.rsqrt(jnp.maximum(square, 0.0) + 1e-06)
        later = [stack[2 * COLS :]] if n + 1 < count else []
        stack = jnp.concatenate([stack[:COLS]] + later, axis=0) * scale
        back, u = stack[:COLS], panels_of(panels[n], own)
        old = select[forward]
        select[forward] = (back, u) if old is None else (
            jnp.where(me == owner, back, old[0]), jnp.where(me == owner, u, old[1])
        )
    for forward, out in ((True, out_f), (False, out_a)):
        if select[forward] is None:
            out[...] = jnp.zeros_like(out)
        else:
            back, u = select[forward]
            left = jnp.concatenate(split2(full(back)[:, :ROWS].T), axis=0)
            o = lax.dot_general(left, jnp.concatenate(split2(u), axis=1), NN, preferred_element_type=F32)
            out[...] = (o[ROWS:, own:] + o[ROWS:, :own] + o[:ROWS, own:]) + o[:ROWS, :own]


def shards(panels_in, blocks, block_mask, mixing):
    owners, count = lax.axis_size("tm"), lax.axis_size("space")
    me, place = lax.axis_index("tm"), lax.axis_index("space")
    nb, own = blocks.shape[1], panels_in.shape[1]
    even = lax.rem(place, 2) == 0
    bf, f32 = (lambda *s: (s, BF)), (lambda *s: (s, F32))

    def partner_a(s):
        return s ^ 1

    def partner_b(s):
        t = s + 1 if s % 2 else s - 1
        return t if 0 <= t < count else s

    def beside(x, to, only=None):
        route = [(t * count + s, t * count + to(s)) for t in (only or range(owners)) for s in range(count)]
        return lax.ppermute(x, ("tm", "space"), route)

    def hop(x, t, o, to):
        pairs = [(t, o), (o, t)] if t != o else [(t, t)]
        return lax.ppermute(x, ("tm", "space"), [(i * count + s, k * count + to(s)) for i, k in pairs for s in range(count)])

    def edges_of(x, wide_b, wide_a):
        return (
            jnp.where(even, x[:, :wide_b], x[:, own - wide_b : own]),
            jnp.where(even, x[:, own - wide_a : own], x[:, :wide_a]),
        )

    rows = blocks.reshape(RUN, nb, 3, BLOCK // 2, 2 * BLOCK).transpose(0, 2, 3, 1, 4)
    rows, mask = rows.reshape(RUN, 3, BLOCK // 2 * nb, 2 * BLOCK), block_mask.transpose(2, 0, 1)
    vm = lambda *s: pltpu.VMEM(s, F32)
    turn = owners % GROUP != 0
    turning = owners - 1 if turn else owners
    begin = call(first_kernel, [f32(8, 128)], (), flops=10**9)
    sizes = [128, 96] + ([96 * (RIM_A + RIM_B), 96 * (FAR_A + FAR_B)] if turn else [224])
    edges = call(
        functools.partial(edge_kernel, nb, turning),
        [f32(n, 128) for n in sizes],
        (*begin, rows, mask, panels_in),
    )
    near_b, near_a = beside(edges[0], partner_b, range(turning)), beside(edges[2], partner_a)
    (near_b,) = call(aside_kernel, [f32(*near_b.shape)], (near_b,), flops=ASIDE_0)
    if turn:
        far_b = beside(edges[3], partner_b, [turning])
    rows, mask, mixing, _ = lax.optimization_barrier((rows, mask, mixing, edges))
    *own_tiles, expand = call(
        functools.partial(own_kernel, nb),
        [bf(own, 256)] * 4 + [f32(2 * COLS, 128)],
        (rows, mask, mixing),
        [vm(2, own, 128)] * RUN,
    )

    def rim_call(kernel, deep_a, deep_b, args):
        deep_a, deep_b = 2 * deep_a * BLOCK, 2 * deep_b * BLOCK
        outs, scratch = [bf(deep_a, 256)] * 2 + [bf(deep_b, 256)] * 2, [vm(2, deep_a, 128), vm(2, deep_b, 128)]
        return call(kernel, outs, args, scratch)

    def late_rims(after):
        late, _ = lax.optimization_barrier((edges[1], after))
        args = (near_a, near_b, beside(late, partner_b, range(turning)))
        return rim_call(functools.partial(pull_rim_kernel, turning), 1, 2, args)

    pull_rims = None
    if turn:
        turn_rims = rim_call(functools.partial(rim_kernel, turning), RIM_A, RIM_B, (far_b, near_a))

    meta = jnp.zeros((2 * COLS, 128), F32)
    main, edge_a, edge_b = panels_in, near_a[96:128], near_b[96:128]
    stages = 2 * owners
    owner_of = [k if k < owners else stages - 1 - k for k in range(stages)]
    kept, result, k = [], None, 0
    record = ROWS * (own // 128 + 1)
    while k < stages:
        owner, slot, turned, sums = owner_of[k], k % GROUP, False, []
        turns_here, turns_next = turn and k == owners - 1, turn and k + 1 == owners - 1
        if turns_here:
            first, main, send_b = call(
                functools.partial(turn_kernel, nb, owner, slot),
                [f32(ROWS, own), f32(record + 2 * COLS, 128), f32(ROWS, 128)],
                (edge_b, main, edge_a, *own_tiles, *turn_rims, meta, expand),
            )
            kept += [first, main]
            turned = True
            meta = main[record:]
            k += 2
        else:
            if k < owners:
                main, send_b, send_a = call(
                    functools.partial(push_kernel, nb, owner),
                    [f32(ROWS, own)] + [f32(ROWS, w) for w in ((256, 384) if turns_next else (128, 128))],
                    (edge_b, main, edge_a, near_b, near_a, *own_tiles),
                    [vm(2, 2 * BLOCK, 128)],
                    flops=PUSH,
                )
                if pull_rims is None:
                    pull_rims = late_rims(send_b)
                (meta,) = call(
                    functools.partial(note_kernel, nb, owner, slot),
                    [f32(2 * COLS, 128)],
                    (main, meta, expand),
                )
            else:
                ends = (k + 1) % GROUP == 0 or k + 1 == stages
                main, meta, *sums = call(
                    functools.partial(pull_kernel, nb, owner, slot),
                    [f32(ROWS, own), f32(2 * COLS, 128)] + [f32(count, COLS, 128)] * ends,
                    (edge_b, main, edge_a, *own_tiles, *pull_rims, meta, expand),
                )
                send_b, send_a = edges_of(main, 128, 128)
            kept.append(main)
            k += 1
        share = not (turns_next and slot == 0)

        if k % GROUP == 0 or k == stages:
            todo = [(owner_of[i], i < owners) for i in range(k - len(kept), k)]
            every = sums[0] if sums else jnp.broadcast_to(meta[None, :COLS], (count, COLS, 128))
            grams = lax.all_to_all(every, "space", 0, 0)
            pair = call(
                functools.partial(scale_kernel, todo, count * own), [f32(ROWS, own)] * 2, (grams, meta, *kept)
            )
            if result is None:
                result = pair
            else:
                live = [
                    functools.reduce(jnp.logical_or, [me == o for o, f in todo if f == way], jnp.bool_(False))
                    for way in (True, False)
                ]
                result = [jnp.where(c, new, old) for c, new, old in zip(live, pair, result)]
            main = pair[0 if k - 1 < owners else 1]
            send_b, send_a = edges_of(main, *((256, 384) if turn and k == owners - 1 else (128, 128)))
            meta, kept, share, turned = jnp.zeros((2 * COLS, 128), F32), [], False, False
        if k == stages:
            break

        before, after = owner_of[k - 1], owner_of[k]
        if after != before:
            main = hop(main, before, after, lambda s: s)
        into_turn = turn and k == owners - 1
        wide_a = 384 if into_turn else 128
        (edge_b,) = call(
            aside_kernel,
            [f32(ROWS, wide_a)],
            (hop(send_b, before, after, partner_b),) + ((turn_rims[0],) if into_turn else ()),
            flops=ASIDE_1 if into_turn else ASIDE_2,
        )
        if turned:
            edge_a = main[record - ROWS : record]
            meta = meta + main[record:]
        else:
            edge_a = hop(send_a, before, after, partner_a)
            if share and after != before:
                meta = meta + hop(meta, before, after, lambda s: s)
    return result[0][None], result[1][None]


def solution(mesh):
    return jax.shard_map(
        shards,
        mesh=mesh,
        in_specs=(
            P(None, "space"),
            P("tm", "space", None, None),
            P("tm", "space", None),
            P("tm", None, None, None),
        ),
        out_specs=(P("tm", None, "space"), P("tm", None, "space")),
        check_vma=False,
    )
```

```python
import functools

import jax
import jax.numpy as jnp
from jax import lax
from jax.experimental import pallas as pl
from jax.experimental.pallas import tpu as pltpu
from jax.sharding import PartitionSpec as P

BLOCK = 64
COLS = 8
PANELS = 4
ROWS = COLS * PANELS
RUN = 2
GROUP = 4
RIM_A, RIM_B = 5, 4
FAR_A, FAR_B = 3, 2
PUSH = 3 * 10**9
ASIDE_0 = 10**10
ASIDE_1, ASIDE_2 = 7 * 10**8, 5 * 10**8
DOWN = 2.0**-16
BF = jnp.bfloat16
F32 = jnp.float32
HIGH = lax.Precision.HIGHEST
NT = (((1,), (1,)), ((), ()))
NN = (((1,), (0,)), ((), ()))
TN = (((0,), (0,)), ((), ()))
VM = pl.BlockSpec(memory_space=pltpu.VMEM)


def call(kernel, outs, args, scratch=(), flops=10**6, far=0, limit=12):
    shapes = [jax.ShapeDtypeStruct(shape, dtype) for shape, dtype in outs]
    return pl.pallas_call(
        kernel,
        out_shape=shapes,
        in_specs=[pl.BlockSpec(memory_space=pltpu.HBM)] * far + [VM] * (len(args) - far),
        out_specs=[VM] * len(outs),
        scratch_shapes=list(scratch),
        compiler_params=pltpu.CompilerParams(vmem_limit_bytes=limit << 20),
        cost_estimate=pl.CostEstimate(flops=flops, bytes_accessed=10**5, transcendentals=0),
    )(*args)


def inside():
    place, last = lax.axis_index("space"), lax.axis_size("space") - 1
    return jnp.where((place == 0) | (place == last), 0.0, 1.0).astype(F32)


def parity():
    return lax.rem(lax.axis_index("space"), 2)


def iota(shape, dim):
    return lax.broadcasted_iota(jnp.int32, shape, dim)


def presence(mask, t, j, nb):
    place, last = lax.axis_index("space"), lax.axis_size("space") - 1
    here = jnp.broadcast_to(mask[j, t : t + 1, :], (nb, nb))
    diagonal = iota((nb, nb), 0) == iota((nb, nb), 1)
    column = jnp.sum(jnp.where(diagonal, here, 0), axis=1, keepdims=True).astype(F32)
    if j == 0:
        column = jnp.where((iota((nb, 1), 0) == 0) & (place == 0), 0.0, column)
    if j == 2:
        column = jnp.where((iota((nb, 1), 0) == nb - 1) & (place == last), 0.0, column)
    return column


def first_kernel(out):
    out[...] = jnp.zeros_like(out)


def block_of(blocks, column, t, j, b, nb):
    return blocks[t, j, pl.ds(b, BLOCK // 2, stride=nb), :] * column[t][j][b : b + 1, :]


def edge_kernel(nb, turning, _, blocks, mask, panels, near_b, late_b, to_a, *far_b):
    width = panels.shape[1]
    turns = lax.axis_index("tm") == turning
    column = [[presence(mask, t, j, nb) for j in range(3)] for t in range(RUN)]

    def near(dst, later, at, low_side, keep=1.0):
        edge = 0 if low_side else nb - 1
        inner = 1 if low_side else nb - 2
        for j in range(3):
            dst[j * 32 : (j + 1) * 32, :] = block_of(blocks, column, 0, j, edge, nb) * keep
        dst[96:128, :] = panels[:, :128] if low_side else panels[:, width - 128 :]
        rest = [(edge, 0), (edge, 1), (inner, 0)] if low_side else [(inner, 2), (edge, 1), (edge, 2)]
        for i, (b, j) in enumerate(rest):
            later[at + i * 32 : at + (i + 1) * 32, :] = block_of(blocks, column, 1, j, b, nb) * keep

    def far(dst, deep_a, deep_b, low_side, keep=1.0):
        at = 0
        for t, deep in ((0, deep_a), (1, deep_b)):
            for b in range(deep) if low_side else range(nb - deep, nb):
                for j in range(3):
                    dst[at : at + 32, :] = block_of(blocks, column, t, j, b, nb) * keep
                    at += 32

    for side in range(2):

        @pl.when((parity() == side) & jnp.logical_not(turns))
        def _():
            near(near_b, late_b, 0, side == 0, inside())
            near(to_a, to_a, 128, side == 1)

        if far_b:

            @pl.when((parity() == side) & turns)
            def _():
                far(far_b[0], FAR_A, FAR_B, side == 0, inside())
                far(to_a, RIM_A, RIM_B, side == 1)


def banded(y, p):
    low = iota(y[0].shape, 1) < BLOCK
    zero = jnp.zeros_like(y[0])
    turned = [pltpu.roll(v, BLOCK, 1) for v in y]
    at_low, at_high = (y, turned) if p == 0 else (turned, y)
    first = (jnp.where(low, at_low[0], at_high[1]), jnp.where(low, at_low[2], zero))
    second = (jnp.where(low, zero, at_high[0]), jnp.where(low, at_low[1], at_high[2]))
    return first, second


def split2(x):
    high = x.astype(BF)
    return high, (x - high.astype(F32)).astype(BF)


def split_halves(wide, at, hi, lo):
    for half in range(2):
        lanes = slice(half * 128, half * 128 + 128)
        hi[:, lanes], lo[:, lanes] = split2(wide[at + half])


def own_kernel(nb, blocks, mask, mixing, a_hi, a_lo, b_hi, b_lo, expand, *wide):
    column = [[presence(mask, t, j, nb) for j in range(3)] for t in range(RUN)]
    for t, hi, lo in ((0, a_hi, a_lo), (1, b_hi, b_lo)):
        for b in range(nb):
            rim_row(wide[t], b, b % 2 == 1 - t, [block_of(blocks, column, t, j, b, nb) for j in range(3)])
        split_halves(wide[t], 0, hi, lo)
    pick = (lax.rem(iota((COLS, 128), 1), COLS) == iota((COLS, 128), 0)).astype(F32)
    row, lane = iota((ROWS, 128), 0), lax.rem(iota((ROWS, 128), 1), ROWS)
    same = (row // COLS) == (lane // COLS)
    step = []
    for t in range(RUN):
        m = mixing[t].reshape(ROWS, COLS)
        spread = lax.dot_general(m, pick, NN, precision=HIGH, preferred_element_type=F32)
        step.append((row == lane).astype(F32) - jnp.where(same, spread, 0.0))
    for i, (x, y) in enumerate(((step[0], step[1]), (step[1], step[0]))):
        e = lax.dot_general(x[:, :ROWS], y, NN, precision=HIGH, preferred_element_type=F32)
        expand[i * COLS : (i + 1) * COLS, :] = (
            e[0:COLS] + e[COLS : 2 * COLS] + e[2 * COLS : 3 * COLS] + e[3 * COLS :]
        )


def taken(from_a, from_b, left, at_a, at_b=None):
    use_b = (parity() == 0) == left
    at_b = at_a if at_b is None else at_b
    return jnp.where(use_b, from_b[at_b : at_b + 32, :], from_a[at_a : at_a + 32, :])


def rim_row(dst, index, first, y):
    for p in range(2):
        tiles = banded(y, p)[0 if first else 1]
        for half in range(2):
            dst[half, pl.ds(index * BLOCK + p, 32, stride=2), :] = tiles[half]


def edge_rows(near_a, near_b, dst):
    for left in (True, False):
        rim_row(dst, 1 - left, left, [taken(near_a, near_b, left, j * 32) for j in range(3)])


def rim_kernel(turning, far_b, far_a, a_hi, a_lo, b_hi, b_lo, wide_a, wide_b):
    none = jnp.zeros((32, 128), F32)

    @pl.when(lax.axis_index("tm") == turning)
    def _():
        for dst, deep, start_a, wide, start_b, odd in (
            (wide_a, RIM_A, 0, FAR_A, 0, 1),
            (wide_b, RIM_B, 96 * RIM_A, FAR_B, 96 * FAR_A, 0),
        ):
            for i in range(deep):
                for left in (True, False):
                    k = i - (deep - wide) if left else i
                    y = []
                    for j in range(3):
                        n, m = start_a + i * 96 + j * 32, start_b + k * 96 + j * 32
                        from_b = far_b[m : m + 32, :] if 0 <= k < wide else none
                        y.append(jnp.where((parity() == 0) == left, from_b, far_a[n : n + 32, :]))
                    place = i - deep if left else i
                    rim_row(dst, i if left else deep + i, place % 2 == odd, y)
        split_halves(wide_a, 0, a_hi, a_lo)
        split_halves(wide_b, 0, b_hi, b_lo)


def pull_rim_kernel(turning, near_a, near_b, late_b, a_hi, a_lo, b_hi, b_lo, wide_a, wide_b):
    @pl.when(lax.axis_index("tm") != turning)
    def _():
        edge_rows(near_a, near_b, wide_a)
        none = jnp.zeros((32, 128), F32)
        left = [taken(near_a, late_b, True, 128 + i * 32, i * 32) for i in range(3)]
        right = [taken(near_a, late_b, False, 128 + i * 32, i * 32) for i in range(3)]
        rim_row(wide_b, 0, True, [none, none, left[0]])
        rim_row(wide_b, 1, False, [none, left[1], left[2]])
        rim_row(wide_b, 2, True, [right[0], right[1], none])
        rim_row(wide_b, 3, False, [right[2], none, none])
        split_halves(wide_a, 0, a_hi, a_lo)
        split_halves(wide_b, 0, b_hi, b_lo)


def pair_tile(own, rim, depth, nb, b):
    def row(k):
        if 0 <= k < nb:
            return own[k * BLOCK : (k + 1) * BLOCK, :]
        k = k + depth if k < 0 else depth + k - nb
        return rim[k * BLOCK : (k + 1) * BLOCK, :]

    return jnp.concatenate([row(b), row(b + 1)], axis=0)


def product(x, w, dims):
    o = lax.dot_general(x, w, dims, preferred_element_type=F32)
    return (o[ROWS:, 128:] + o[ROWS:, :128] + o[:ROWS, 128:]) + o[:ROWS, :128]


def push(v, tiles):
    x = jnp.concatenate(split2(v), axis=0)
    outs = []
    for i, (hi, lo) in enumerate(tiles):
        outs.append(product(x[:, i * 128 : i * 128 + 256], jnp.concatenate([hi, lo], axis=0), NT))
    return jnp.concatenate(outs, axis=1)


def pull(v, tiles):
    x = jnp.concatenate(split2(v), axis=0)
    outs = []
    for i in range(len(tiles) - 1):
        parts = [
            jnp.concatenate([tiles[i][s][:, 128:], tiles[i + 1][s][:, :128]], axis=0) for s in range(2)
        ]
        outs.append(product(x[:, i * 128 : i * 128 + 256], jnp.concatenate(parts, axis=1), NN))
    return jnp.concatenate(outs, axis=1)


def tiles_of(refs, depth, nb, first, last):
    own_hi, own_lo, rim_hi, rim_lo = refs
    return [
        (pair_tile(own_hi, rim_hi, depth, nb, b), pair_tile(own_lo, rim_lo, depth, nb, b))
        for b in range(first, last, 2)
    ]


def gram(u):
    high, low = split2(u)
    o = lax.dot_general(
        jnp.concatenate([low, high], axis=0),
        jnp.concatenate([low] * 4 + [high] * 4, axis=0),
        NT,
        preferred_element_type=F32,
    )
    total = (o[:ROWS, :128] + o[:ROWS, 128:] + o[ROWS:, :128]) + o[ROWS:, 128:]
    panel = lax.rem(iota((COLS, 128), 1), ROWS) // COLS
    out = jnp.zeros((COLS, 128), F32)
    for p in range(PANELS):
        out = out + jnp.where(panel == p, total[p * COLS : (p + 1) * COLS], 0.0)
    return out


def noted(g, e, slot, new_g, new_e):
    mine = (iota((COLS, 128), 1) // ROWS) == slot
    return jnp.where(mine, new_g, g), jnp.where(mine, new_e, e)


def panels_of(ref, own):
    if ref.shape[0] == ROWS:
        return ref[:, :own]
    return jnp.concatenate([ref[i * ROWS : (i + 1) * ROWS, :] for i in range(own // 128)], axis=1)


def by_side(e_a, e_b):
    even = parity() == 0
    return jnp.where(even, e_b, e_a), jnp.where(even, e_a, e_b)


def aside_kernel(edge, *refs):
    refs[-1][...] = edge[...]


def push_kernel(nb, owner, edge_b, main, edge_a, near_b, near_a, a_hi, a_lo, b_hi, b_lo, out, out_b, out_a, wide):
    own = nb * BLOCK

    @pl.when(lax.axis_index("tm") == owner)
    def _():
        edge_rows(near_a, near_b, wide)
        rim_hi, rim_lo = split2(jnp.concatenate([wide[0], wide[1]], axis=1))
        left, right = by_side(edge_a[...], edge_b[...])
        v = jnp.concatenate([left, main[:, :own], right], axis=1)
        w = push(v, tiles_of((a_hi, a_lo, rim_hi, rim_lo), 1, nb, -1, nb))
        u = push(w, tiles_of((b_hi, b_lo, None, None), 0, nb, 0, nb))
        out[...] = u
        wide_b, wide_a = out_b.shape[1], out_a.shape[1]
        out_b[...] = by_side(u[:, :wide_b], u[:, own - wide_b :])[1]
        out_a[...] = by_side(u[:, own - wide_a :], u[:, :wide_a])[1]


def turn_kernel(nb, owner, slot, edge_b, main, edge_a, a_hi, a_lo, b_hi, b_lo, ra_hi, ra_lo, rb_hi, rb_lo,
                old, expand, first, out, out_b):
    own = nb * BLOCK
    pieces = own // 128
    record = slice((pieces + 1) * ROWS, (pieces + 1) * ROWS + 2 * COLS)

    @pl.when(lax.axis_index("tm") != owner)
    def _():
        out[record, :] = old[...]

    def turn(low, edges):
        a0, a1 = (RIM_A, FAR_A) if low else (FAR_A, RIM_A)
        b0, b1 = (RIM_B, FAR_B) if low else (FAR_B, RIM_B)
        v = jnp.concatenate([edges[0], main[:, :own], edges[1]], axis=1)
        tiles_a = tiles_of((a_hi, a_lo, ra_hi, ra_lo), RIM_A, nb, -a0, nb + a1)
        tiles_b = tiles_of((b_hi, b_lo, rb_hi, rb_lo), RIM_B, nb, -b0, nb + b1)
        u = push(push(v, tiles_a), tiles_b)
        u_own = u[:, b0 * BLOCK : b0 * BLOCK + own]
        first[...] = u_own
        back = pull(pull(u * DOWN, tiles_b), tiles_a[1:-1])
        back_own, beyond = (back[:, 128:], back[:, :128]) if low else (back[:, :own], back[:, own:])
        for i in range(pieces):
            out[i * ROWS : (i + 1) * ROWS, :] = back_own[:, i * 128 : (i + 1) * 128]
        out[pieces * ROWS : (pieces + 1) * ROWS, :] = beyond
        out_b[...] = back_own[:, own - 128 :] if low else back_own[:, :128]
        g, e = noted(old[:COLS], old[COLS:], slot, gram(u_own), expand[:COLS])
        g, e = noted(g, e, slot + 1, gram(back_own), expand[COLS:] * (1.0 / DOWN))
        out[record, :] = jnp.concatenate([g, e], axis=0)

    mine = lax.axis_index("tm") == owner
    pl.when(mine & (parity() == 0))(lambda: turn(False, (edge_b[...], edge_a[...])))
    pl.when(mine & (parity() == 1))(lambda: turn(True, (edge_a[...], edge_b[...])))


def pull_kernel(nb, owner, slot, edge_b, main, edge_a, a_hi, a_lo, b_hi, b_lo, ra_hi, ra_lo, rb_hi, rb_lo,
                old, expand, out, record, *every):
    own = nb * BLOCK

    @pl.when(lax.axis_index("tm") != owner)
    def _():
        record[...] = old[...]

    @pl.when(lax.axis_index("tm") == owner)
    def _():
        left, right = by_side(edge_a[...], edge_b[...])
        v = jnp.concatenate([left, panels_of(main, own), right], axis=1)
        y = pull(v, tiles_of((b_hi, b_lo, rb_hi, rb_lo), 2, nb, -2, nb + 2))
        u = pull(y, tiles_of((a_hi, a_lo, ra_hi, ra_lo), 1, nb, -1, nb + 1))
        out[...] = u
        record[:COLS], record[COLS:] = noted(old[:COLS], old[COLS:], slot, gram(u), expand[COLS:])

    for ref in every:
        for i in range(ref.shape[0]):
            ref[i] = record[:COLS]


def note_kernel(nb, owner, slot, u, old, expand, out):
    @pl.when(lax.axis_index("tm") != owner)
    def _():
        out[...] = old[...]

    @pl.when(lax.axis_index("tm") == owner)
    def _():
        out[:COLS], out[COLS:] = noted(old[:COLS], old[COLS:], slot, gram(u[:, : nb * BLOCK]), expand[:COLS])


def exact(x, y):
    rows = x.shape[0]
    m = -(-rows // 16) * 16
    if m > rows:
        x = jnp.concatenate([x, jnp.zeros((m - rows, x.shape[1]), F32)], axis=0)
    o = lax.dot_general(
        jnp.concatenate(split2(x), axis=0), jnp.concatenate(split2(y), axis=1), NN, preferred_element_type=F32
    )
    o = (o[m:, 128:] + o[m:, :128] + o[:m, 128:]) + o[:m, :128]
    return o[:rows]


def scale_kernel(stages, boxes, grams, meta, *refs):
    panels, (out_f, out_a) = refs[: len(stages)], refs[len(stages) :]
    own = out_f.shape[1]
    parts = [grams[i] for i in range(grams.shape[0])]
    while len(parts) > 1:
        parts = [a + b for a, b in zip(parts[::2], parts[1::2])] + parts[len(parts) // 2 * 2 :]
    total = parts[0] * (1.0 / boxes)
    growth = meta[COLS:, :]
    row, lane = iota((ROWS, 128), 0), iota((ROWS, 128), 1)
    same = (row // COLS) == (lax.rem(lane, ROWS) // COLS)
    group = lane[:COLS] // ROWS
    me = lax.axis_index("tm")

    def spread(x, n):
        turns = [x if k == n else pltpu.roll(x, ((k - n) % 4) * ROWS, 1) for k in range(4)]
        out = turns[0]
        for k in range(1, 4):
            out = jnp.where(group == k, turns[k], out)
        return out

    def full(x):
        return jnp.where(same, jnp.concatenate([x] * PANELS, axis=0), 0.0)

    count = len(stages)
    grow = [spread(growth, n) for n in range(count)]
    products = jnp.concatenate([spread(total, n)[:, :ROWS] for n in range(count)], axis=0)
    stack = jnp.concatenate([grow[0], exact(products, full(grow[0]))], axis=0)
    select = {True: None, False: None}
    for n, (owner, forward) in enumerate(stages):
        if n:
            stack = exact(stack[:, :ROWS], full(grow[n]))
        square = jnp.sum(stack[:COLS] * stack[COLS : 2 * COLS], axis=0, keepdims=True)
        scale = lax.rsqrt(jnp.maximum(square, 0.0) + 1e-06)
        later = [stack[2 * COLS :]] if n + 1 < count else []
        stack = jnp.concatenate([stack[:COLS]] + later, axis=0) * scale
        back, u = stack[:COLS], panels_of(panels[n], own)
        old = select[forward]
        select[forward] = (back, u) if old is None else (
            jnp.where(me == owner, back, old[0]), jnp.where(me == owner, u, old[1])
        )
    for forward, out in ((True, out_f), (False, out_a)):
        if select[forward] is None:
            out[...] = jnp.zeros_like(out)
        else:
            back, u = select[forward]
            left = jnp.concatenate(split2(full(back)[:, :ROWS].T), axis=0)
            o = lax.dot_general(left, jnp.concatenate(split2(u), axis=1), NN, preferred_element_type=F32)
            out[...] = (o[ROWS:, own:] + o[ROWS:, :own] + o[:ROWS, own:]) + o[:ROWS, :own]


def shards(panels_in, blocks, block_mask, mixing):
    owners, count = lax.axis_size("tm"), lax.axis_size("space")
    me, place = lax.axis_index("tm"), lax.axis_index("space")
    nb, own = blocks.shape[1], panels_in.shape[1]
    even = lax.rem(place, 2) == 0
    bf, f32 = (lambda *s: (s, BF)), (lambda *s: (s, F32))

    def partner_a(s):
        return s ^ 1

    def partner_b(s):
        t = s + 1 if s % 2 else s - 1
        return t if 0 <= t < count else s

    def beside(x, to, only=None):
        route = [(t * count + s, t * count + to(s)) for t in (only or range(owners)) for s in range(count)]
        return lax.ppermute(x, ("tm", "space"), route)

    def hop(x, t, o, to):
        pairs = [(t, o), (o, t)] if t != o else [(t, t)]
        return lax.ppermute(x, ("tm", "space"), [(i * count + s, k * count + to(s)) for i, k in pairs for s in range(count)])

    def edges_of(x, wide_b, wide_a):
        return (
            jnp.where(even, x[:, :wide_b], x[:, own - wide_b : own]),
            jnp.where(even, x[:, own - wide_a : own], x[:, :wide_a]),
        )

    rows = blocks.reshape(RUN, nb, 3, BLOCK // 2, 2 * BLOCK).transpose(0, 2, 3, 1, 4)
    rows, mask = rows.reshape(RUN, 3, BLOCK // 2 * nb, 2 * BLOCK), block_mask.transpose(2, 0, 1)
    vm = lambda *s: pltpu.VMEM(s, F32)
    turn = owners % GROUP != 0
    turning = owners - 1 if turn else owners
    begin = call(first_kernel, [f32(8, 128)], (), flops=10**9)
    sizes = [128, 96] + ([96 * (RIM_A + RIM_B), 96 * (FAR_A + FAR_B)] if turn else [224])
    edges = call(
        functools.partial(edge_kernel, nb, turning),
        [f32(n, 128) for n in sizes],
        (*begin, rows, mask, panels_in),
    )
    near_b, near_a = beside(edges[0], partner_b, range(turning)), beside(edges[2], partner_a)
    (near_b,) = call(aside_kernel, [f32(*near_b.shape)], (near_b,), flops=ASIDE_0)
    if turn:
        far_b = beside(edges[3], partner_b, [turning])
    rows, mask, mixing, _ = lax.optimization_barrier((rows, mask, mixing, edges))
    *own_tiles, expand = call(
        functools.partial(own_kernel, nb),
        [bf(own, 256)] * 4 + [f32(2 * COLS, 128)],
        (rows, mask, mixing),
        [vm(2, own, 128)] * RUN,
    )

    def rim_call(kernel, deep_a, deep_b, args):
        deep_a, deep_b = 2 * deep_a * BLOCK, 2 * deep_b * BLOCK
        outs, scratch = [bf(deep_a, 256)] * 2 + [bf(deep_b, 256)] * 2, [vm(2, deep_a, 128), vm(2, deep_b, 128)]
        return call(kernel, outs, args, scratch)

    def late_rims(after):
        late, _ = lax.optimization_barrier((edges[1], after))
        args = (near_a, near_b, beside(late, partner_b, range(turning)))
        return rim_call(functools.partial(pull_rim_kernel, turning), 1, 2, args)

    pull_rims = None
    if turn:
        turn_rims = rim_call(functools.partial(rim_kernel, turning), RIM_A, RIM_B, (far_b, near_a))

    meta = jnp.zeros((2 * COLS, 128), F32)
    main, edge_a, edge_b = panels_in, near_a[96:128], near_b[96:128]
    stages = 2 * owners
    owner_of = [k if k < owners else stages - 1 - k for k in range(stages)]
    kept, result, k = [], None, 0
    record = ROWS * (own // 128 + 1)
    while k < stages:
        owner, slot, turned, sums = owner_of[k], k % GROUP, False, []
        turns_here, turns_next = turn and k == owners - 1, turn and k + 1 == owners - 1
        if turns_here:
            first, main, send_b = call(
                functools.partial(turn_kernel, nb, owner, slot),
                [f32(ROWS, own), f32(record + 2 * COLS, 128), f32(ROWS, 128)],
                (edge_b, main, edge_a, *own_tiles, *turn_rims, meta, expand),
            )
            kept += [first, main]
            turned = True
            meta = main[record:]
            k += 2
        else:
            if k < owners:
                main, send_b, send_a = call(
                    functools.partial(push_kernel, nb, owner),
                    [f32(ROWS, own)] + [f32(ROWS, w) for w in ((256, 384) if turns_next else (128, 128))],
                    (edge_b, main, edge_a, near_b, near_a, *own_tiles),
                    [vm(2, 2 * BLOCK, 128)],
                    flops=PUSH,
                )
                if pull_rims is None:
                    pull_rims = late_rims(send_b)
                (meta,) = call(
                    functools.partial(note_kernel, nb, owner, slot),
                    [f32(2 * COLS, 128)],
                    (main, meta, expand),
                )
            else:
                ends = (k + 1) % GROUP == 0 or k + 1 == stages
                main, meta, *sums = call(
                    functools.partial(pull_kernel, nb, owner, slot),
                    [f32(ROWS, own), f32(2 * COLS, 128)] + [f32(count, COLS, 128)] * ends,
                    (edge_b, main, edge_a, *own_tiles, *pull_rims, meta, expand),
                )
                send_b, send_a = edges_of(main, 128, 128)
            kept.append(main)
            k += 1
        share = not (turns_next and slot == 0)

        if k % GROUP == 0 or k == stages:
            todo = [(owner_of[i], i < owners) for i in range(k - len(kept), k)]
            every = sums[0] if sums else jnp.broadcast_to(meta[None, :COLS], (count, COLS, 128))
            grams = lax.all_to_all(every, "space", 0, 0)
            pair = call(
                functools.partial(scale_kernel, todo, count * own), [f32(ROWS, own)] * 2, (grams, meta, *kept)
            )
            if result is None:
                result = pair
            else:
                live = [
                    functools.reduce(jnp.logical_or, [me == o for o, f in todo if f == way], jnp.bool_(False))
                    for way in (True, False)
                ]
                result = [jnp.where(c, new, old) for c, new, old in zip(live, pair, result)]
            main = pair[0 if k - 1 < owners else 1]
            send_b, send_a = edges_of(main, *((256, 384) if turn and k == owners - 1 else (128, 128)))
            meta, kept, share, turned = jnp.zeros((2 * COLS, 128), F32), [], False, False
        if k == stages:
            break

        before, after = owner_of[k - 1], owner_of[k]
        if after != before:
            main = hop(main, before, after, lambda s: s)
        into_turn = turn and k == owners - 1
        (edge_b,) = call(
            aside_kernel,
            [f32(*send_b.shape)],
            (hop(send_b, before, after, partner_b),) + ((turn_rims[0],) if into_turn else ()),
            flops=ASIDE_1 if into_turn else ASIDE_2,
        )
        if turned:
            edge_a = main[record - ROWS : record]
            meta = meta + main[record:]
        else:
            edge_a = hop(send_a, before, after, partner_a)
            if share and after != before:
                meta = meta + hop(meta, before, after, lambda s: s)
    return result[0][None], result[1][None]


def solution(mesh):
    return jax.shard_map(
        shards,
        mesh=mesh,
        in_specs=(
            P(None, "space"),
            P("tm", "space", None, None),
            P("tm", "space", None),
            P("tm", None, None, None),
        ),
        out_specs=(P("tm", None, "space"), P("tm", None, "space")),
        check_vma=False,
    )
```

```python
import functools

import jax
import jax.numpy as jnp
from jax import lax
from jax.experimental import pallas as pl
from jax.experimental.pallas import tpu as pltpu
from jax.sharding import PartitionSpec as P

BLOCK = 64
COLS = 8
PANELS = 4
ROWS = COLS * PANELS
RUN = 2
GROUP = 4
RIM_A, RIM_B = 5, 4
FAR_A, FAR_B = 3, 2
PUSH = 3 * 10**9
ASIDE_0 = 10**10
ASIDE_1, ASIDE_2 = 7 * 10**8, 5 * 10**8
DOWN = 2.0**-16
BF = jnp.bfloat16
F32 = jnp.float32
HIGH = lax.Precision.HIGHEST
NT = (((1,), (1,)), ((), ()))
NN = (((1,), (0,)), ((), ()))
TN = (((0,), (0,)), ((), ()))
VM = pl.BlockSpec(memory_space=pltpu.VMEM)


def call(kernel, outs, args, scratch=(), flops=10**6, far=0, limit=12):
    shapes = [jax.ShapeDtypeStruct(shape, dtype) for shape, dtype in outs]
    return pl.pallas_call(
        kernel,
        out_shape=shapes,
        in_specs=[pl.BlockSpec(memory_space=pltpu.HBM)] * far + [VM] * (len(args) - far),
        out_specs=[VM] * len(outs),
        scratch_shapes=list(scratch),
        compiler_params=pltpu.CompilerParams(vmem_limit_bytes=limit << 20),
        cost_estimate=pl.CostEstimate(flops=flops, bytes_accessed=10**5, transcendentals=0),
    )(*args)


def inside():
    place, last = lax.axis_index("space"), lax.axis_size("space") - 1
    return jnp.where((place == 0) | (place == last), 0.0, 1.0).astype(F32)


def parity():
    return lax.rem(lax.axis_index("space"), 2)


def iota(shape, dim):
    return lax.broadcasted_iota(jnp.int32, shape, dim)


def presence(mask, t, j, nb):
    place, last = lax.axis_index("space"), lax.axis_size("space") - 1
    here = jnp.broadcast_to(mask[j, t : t + 1, :], (nb, nb))
    diagonal = iota((nb, nb), 0) == iota((nb, nb), 1)
    column = jnp.sum(jnp.where(diagonal, here, 0), axis=1, keepdims=True).astype(F32)
    if j == 0:
        column = jnp.where((iota((nb, 1), 0) == 0) & (place == 0), 0.0, column)
    if j == 2:
        column = jnp.where((iota((nb, 1), 0) == nb - 1) & (place == last), 0.0, column)
    return column


def first_kernel(out):
    out[...] = jnp.zeros_like(out)


def block_of(blocks, column, t, j, b, nb):
    return blocks[t, j, pl.ds(b, BLOCK // 2, stride=nb), :] * column[t][j][b : b + 1, :]


def edge_kernel(nb, turning, _, blocks, mask, panels, near_b, late_b, to_a, *far_b):
    width = panels.shape[1]
    turns = lax.axis_index("tm") == turning
    column = [[presence(mask, t, j, nb) for j in range(3)] for t in range(RUN)]

    def near(dst, later, at, low_side, keep=1.0):
        edge = 0 if low_side else nb - 1
        inner = 1 if low_side else nb - 2
        for j in range(3):
            dst[j * 32 : (j + 1) * 32, :] = block_of(blocks, column, 0, j, edge, nb) * keep
        dst[96:128, :] = panels[:, :128] if low_side else panels[:, width - 128 :]
        rest = [(edge, 0), (edge, 1), (inner, 0)] if low_side else [(inner, 2), (edge, 1), (edge, 2)]
        for i, (b, j) in enumerate(rest):
            later[at + i * 32 : at + (i + 1) * 32, :] = block_of(blocks, column, 1, j, b, nb) * keep

    def far(dst, deep_a, deep_b, low_side, keep=1.0):
        at = 0
        for t, deep in ((0, deep_a), (1, deep_b)):
            for b in range(deep) if low_side else range(nb - deep, nb):
                for j in range(3):
                    dst[at : at + 32, :] = block_of(blocks, column, t, j, b, nb) * keep
                    at += 32

    for side in range(2):

        @pl.when((parity() == side) & jnp.logical_not(turns))
        def _():
            near(near_b, late_b, 0, side == 0, inside())
            near(to_a, to_a, 128, side == 1)

        if far_b:

            @pl.when((parity() == side) & turns)
            def _():
                far(far_b[0], FAR_A, FAR_B, side == 0, inside())
                far(to_a, RIM_A, RIM_B, side == 1)


def banded(y, p):
    low = iota(y[0].shape, 1) < BLOCK
    zero = jnp.zeros_like(y[0])
    turned = [pltpu.roll(v, BLOCK, 1) for v in y]
    at_low, at_high = (y, turned) if p == 0 else (turned, y)
    first = (jnp.where(low, at_low[0], at_high[1]), jnp.where(low, at_low[2], zero))
    second = (jnp.where(low, zero, at_high[0]), jnp.where(low, at_low[1], at_high[2]))
    return first, second


def split2(x):
    high = x.astype(BF)
    return high, (x - high.astype(F32)).astype(BF)


def split3(x):
    first = x.astype(BF)
    x = x - first.astype(F32)
    second = x.astype(BF)
    return first, second, (x - second.astype(F32)).astype(BF)


def split_halves(wide, at, hi, lo):
    for half in range(2):
        lanes = slice(half * 128, half * 128 + 128)
        hi[:, lanes], lo[:, lanes] = split2(wide[at + half])


def own_kernel(nb, blocks, mask, mixing, a_hi, a_lo, b_hi, b_lo, expand, *wide):
    column = [[presence(mask, t, j, nb) for j in range(3)] for t in range(RUN)]
    for t, hi, lo in ((0, a_hi, a_lo), (1, b_hi, b_lo)):
        for b in range(nb):
            rim_row(wide[t], b, b % 2 == 1 - t, [block_of(blocks, column, t, j, b, nb) for j in range(3)])
        split_halves(wide[t], 0, hi, lo)
    pick = (lax.rem(iota((COLS, 128), 1), COLS) == iota((COLS, 128), 0)).astype(F32)
    row, lane = iota((ROWS, 128), 0), lax.rem(iota((ROWS, 128), 1), ROWS)
    same = (row // COLS) == (lane // COLS)
    step = []
    for t in range(RUN):
        m = mixing[t].reshape(ROWS, COLS)
        spread = lax.dot_general(m, pick, NN, precision=HIGH, preferred_element_type=F32)
        step.append((row == lane).astype(F32) - jnp.where(same, spread, 0.0))
    for i, (x, y) in enumerate(((step[0], step[1]), (step[1], step[0]))):
        e = lax.dot_general(x[:, :ROWS], y, NN, precision=HIGH, preferred_element_type=F32)
        expand[i * COLS : (i + 1) * COLS, :] = (
            e[0:COLS] + e[COLS : 2 * COLS] + e[2 * COLS : 3 * COLS] + e[3 * COLS :]
        )


def taken(from_a, from_b, left, at_a, at_b=None):
    use_b = (parity() == 0) == left
    at_b = at_a if at_b is None else at_b
    return jnp.where(use_b, from_b[at_b : at_b + 32, :], from_a[at_a : at_a + 32, :])


def rim_row(dst, index, first, y):
    for p in range(2):
        tiles = banded(y, p)[0 if first else 1]
        for half in range(2):
            dst[half, pl.ds(index * BLOCK + p, 32, stride=2), :] = tiles[half]


def edge_rows(near_a, near_b, dst):
    for left in (True, False):
        rim_row(dst, 1 - left, left, [taken(near_a, near_b, left, j * 32) for j in range(3)])


def rim_kernel(turning, far_b, far_a, a_hi, a_lo, b_hi, b_lo, wide_a, wide_b):
    none = jnp.zeros((32, 128), F32)

    @pl.when(lax.axis_index("tm") == turning)
    def _():
        for dst, deep, start_a, wide, start_b, odd in (
            (wide_a, RIM_A, 0, FAR_A, 0, 1),
            (wide_b, RIM_B, 96 * RIM_A, FAR_B, 96 * FAR_A, 0),
        ):
            for i in range(deep):
                for left in (True, False):
                    k = i - (deep - wide) if left else i
                    y = []
                    for j in range(3):
                        n, m = start_a + i * 96 + j * 32, start_b + k * 96 + j * 32
                        from_b = far_b[m : m + 32, :] if 0 <= k < wide else none
                        y.append(jnp.where((parity() == 0) == left, from_b, far_a[n : n + 32, :]))
                    place = i - deep if left else i
                    rim_row(dst, i if left else deep + i, place % 2 == odd, y)
        split_halves(wide_a, 0, a_hi, a_lo)
        split_halves(wide_b, 0, b_hi, b_lo)


def pull_rim_kernel(turning, near_a, near_b, late_b, a_hi, a_lo, b_hi, b_lo, wide_a, wide_b):
    @pl.when(lax.axis_index("tm") != turning)
    def _():
        edge_rows(near_a, near_b, wide_a)
        none = jnp.zeros((32, 128), F32)
        left = [taken(near_a, late_b, True, 128 + i * 32, i * 32) for i in range(3)]
        right = [taken(near_a, late_b, False, 128 + i * 32, i * 32) for i in range(3)]
        rim_row(wide_b, 0, True, [none, none, left[0]])
        rim_row(wide_b, 1, False, [none, left[1], left[2]])
        rim_row(wide_b, 2, True, [right[0], right[1], none])
        rim_row(wide_b, 3, False, [right[2], none, none])
        split_halves(wide_a, 0, a_hi, a_lo)
        split_halves(wide_b, 0, b_hi, b_lo)


def pair_tile(own, rim, depth, nb, b):
    def row(k):
        if 0 <= k < nb:
            return own[k * BLOCK : (k + 1) * BLOCK, :]
        k = k + depth if k < 0 else depth + k - nb
        return rim[k * BLOCK : (k + 1) * BLOCK, :]

    return jnp.concatenate([row(b), row(b + 1)], axis=0)


def pieces_sum(o, m, n, skip=0):
    rows, cols = o.shape[0] // m, o.shape[1] // n
    order = sorted(((i, j) for i in range(rows) for j in range(cols)), key=lambda p: -sum(p))
    total = None
    for i, j in order[skip:]:
        piece = o[i * m : (i + 1) * m, j * n : (j + 1) * n]
        total = piece if total is None else total + piece
    return total


def product(x, w, dims):
    o = lax.dot_general(x, w, dims, preferred_element_type=F32)
    return pieces_sum(o, ROWS, 128)


def push(v, tiles):
    x = jnp.concatenate(split3(v), axis=0)
    outs = []
    for i, (hi, lo) in enumerate(tiles):
        outs.append(product(x[:, i * 128 : i * 128 + 256], jnp.concatenate([hi, lo], axis=0), NT))
    return jnp.concatenate(outs, axis=1)


def pull(v, tiles):
    x = jnp.concatenate(split3(v), axis=0)
    outs = []
    for i in range(len(tiles) - 1):
        parts = [
            jnp.concatenate([tiles[i][s][:, 128:], tiles[i + 1][s][:, :128]], axis=0) for s in range(2)
        ]
        outs.append(product(x[:, i * 128 : i * 128 + 256], jnp.concatenate(parts, axis=1), NN))
    return jnp.concatenate(outs, axis=1)


def tiles_of(refs, depth, nb, first, last):
    own_hi, own_lo, rim_hi, rim_lo = refs
    return [
        (pair_tile(own_hi, rim_hi, depth, nb, b), pair_tile(own_lo, rim_lo, depth, nb, b))
        for b in range(first, last, 2)
    ]


def gram(u):
    first = lax.rem(iota(u.shape, 0), COLS) == 0
    parts = split3(u - jnp.where(first, 0.0, pltpu.roll(u, 1, 0)))
    wide = jnp.concatenate([x for x in parts for _ in range(4)], axis=0)
    o = lax.dot_general(jnp.concatenate(parts, axis=0), wide, NT, preferred_element_type=F32)
    total = pieces_sum(o, ROWS, 128)
    panel = lax.rem(iota((COLS, 128), 1), ROWS) // COLS
    out = jnp.zeros((COLS, 128), F32)
    for p in range(PANELS):
        out = out + jnp.where(panel == p, total[p * COLS : (p + 1) * COLS], 0.0)
    return out


def noted(g, e, slot, new_g, new_e):
    mine = (iota((COLS, 128), 1) // ROWS) == slot
    return jnp.where(mine, new_g, g), jnp.where(mine, new_e, e)


def panels_of(ref, own):
    if ref.shape[0] == ROWS:
        return ref[:, :own]
    return jnp.concatenate([ref[i * ROWS : (i + 1) * ROWS, :] for i in range(own // 128)], axis=1)


def by_side(e_a, e_b):
    even = parity() == 0
    return jnp.where(even, e_b, e_a), jnp.where(even, e_a, e_b)


def aside_kernel(edge, *refs):
    refs[-1][...] = edge[...]


def push_kernel(nb, owner, edge_b, main, edge_a, near_b, near_a, a_hi, a_lo, b_hi, b_lo, out, out_b, out_a, wide):
    own = nb * BLOCK

    @pl.when(lax.axis_index("tm") == owner)
    def _():
        edge_rows(near_a, near_b, wide)
        rim_hi, rim_lo = split2(jnp.concatenate([wide[0], wide[1]], axis=1))
        left, right = by_side(edge_a[...], edge_b[...])
        v = jnp.concatenate([left, main[:, :own], right], axis=1)
        w = push(v, tiles_of((a_hi, a_lo, rim_hi, rim_lo), 1, nb, -1, nb))
        u = push(w, tiles_of((b_hi, b_lo, None, None), 0, nb, 0, nb))
        out[...] = u
        wide_b, wide_a = out_b.shape[1], out_a.shape[1]
        out_b[...] = by_side(u[:, :wide_b], u[:, own - wide_b :])[1]
        out_a[...] = by_side(u[:, own - wide_a :], u[:, :wide_a])[1]


def turn_kernel(nb, owner, slot, edge_b, main, edge_a, a_hi, a_lo, b_hi, b_lo, ra_hi, ra_lo, rb_hi, rb_lo,
                old, expand, first, out, out_b):
    own = nb * BLOCK
    pieces = own // 128
    record = slice((pieces + 1) * ROWS, (pieces + 1) * ROWS + 2 * COLS)

    @pl.when(lax.axis_index("tm") != owner)
    def _():
        out[record, :] = old[...]

    def turn(low, edges):
        a0, a1 = (RIM_A, FAR_A) if low else (FAR_A, RIM_A)
        b0, b1 = (RIM_B, FAR_B) if low else (FAR_B, RIM_B)
        v = jnp.concatenate([edges[0], main[:, :own], edges[1]], axis=1)
        tiles_a = tiles_of((a_hi, a_lo, ra_hi, ra_lo), RIM_A, nb, -a0, nb + a1)
        tiles_b = tiles_of((b_hi, b_lo, rb_hi, rb_lo), RIM_B, nb, -b0, nb + b1)
        u = push(push(v, tiles_a), tiles_b)
        u_own = u[:, b0 * BLOCK : b0 * BLOCK + own]
        first[...] = u_own
        back = pull(pull(u * DOWN, tiles_b), tiles_a[1:-1])
        back_own, beyond = (back[:, 128:], back[:, :128]) if low else (back[:, :own], back[:, own:])
        for i in range(pieces):
            out[i * ROWS : (i + 1) * ROWS, :] = back_own[:, i * 128 : (i + 1) * 128]
        out[pieces * ROWS : (pieces + 1) * ROWS, :] = beyond
        out_b[...] = back_own[:, own - 128 :] if low else back_own[:, :128]
        g, e = noted(old[:COLS], old[COLS:], slot, gram(u_own), expand[:COLS])
        g, e = noted(g, e, slot + 1, gram(back_own), expand[COLS:] * (1.0 / DOWN))
        out[record, :] = jnp.concatenate([g, e], axis=0)

    mine = lax.axis_index("tm") == owner
    pl.when(mine & (parity() == 0))(lambda: turn(False, (edge_b[...], edge_a[...])))
    pl.when(mine & (parity() == 1))(lambda: turn(True, (edge_a[...], edge_b[...])))


def pull_kernel(nb, owner, slot, edge_b, main, edge_a, a_hi, a_lo, b_hi, b_lo, ra_hi, ra_lo, rb_hi, rb_lo,
                old, expand, out, record, *every):
    own = nb * BLOCK

    @pl.when(lax.axis_index("tm") != owner)
    def _():
        record[...] = old[...]

    @pl.when(lax.axis_index("tm") == owner)
    def _():
        left, right = by_side(edge_a[...], edge_b[...])
        v = jnp.concatenate([left, panels_of(main, own), right], axis=1)
        y = pull(v, tiles_of((b_hi, b_lo, rb_hi, rb_lo), 2, nb, -2, nb + 2))
        u = pull(y, tiles_of((a_hi, a_lo, ra_hi, ra_lo), 1, nb, -1, nb + 1))
        out[...] = u
        record[:COLS], record[COLS:] = noted(old[:COLS], old[COLS:], slot, gram(u), expand[COLS:])

    for ref in every:
        for i in range(ref.shape[0]):
            ref[i] = record[:COLS]


def note_kernel(nb, owner, slot, u, old, expand, out):
    @pl.when(lax.axis_index("tm") != owner)
    def _():
        out[...] = old[...]

    @pl.when(lax.axis_index("tm") == owner)
    def _():
        out[:COLS], out[COLS:] = noted(old[:COLS], old[COLS:], slot, gram(u[:, : nb * BLOCK]), expand[:COLS])


def exact(x, y):
    rows = x.shape[0]
    m = -(-rows // 16) * 16
    if m > rows:
        x = jnp.concatenate([x, jnp.zeros((m - rows, x.shape[1]), F32)], axis=0)
    o = lax.dot_general(
        jnp.concatenate(split3(x), axis=0), jnp.concatenate(split3(y), axis=1), NN, preferred_element_type=F32
    )
    return pieces_sum(o, m, 128, 3)[:rows]


def scale_kernel(stages, boxes, grams, meta, *refs):
    panels, (out_f, out_a) = refs[: len(stages)], refs[len(stages) :]
    own = out_f.shape[1]
    parts = [grams[i] for i in range(grams.shape[0])]
    while len(parts) > 1:
        parts = [a + b for a, b in zip(parts[::2], parts[1::2])] + parts[len(parts) // 2 * 2 :]
    total = parts[0] * (1.0 / boxes)
    growth = meta[COLS:, :]
    row, lane = iota((ROWS, 128), 0), iota((ROWS, 128), 1)
    same = (row // COLS) == (lax.rem(lane, ROWS) // COLS)
    group = lane[:COLS] // ROWS
    me = lax.axis_index("tm")

    def spread(x, n):
        turns = [x if k == n else pltpu.roll(x, ((k - n) % 4) * ROWS, 1) for k in range(4)]
        out = turns[0]
        for k in range(1, 4):
            out = jnp.where(group == k, turns[k], out)
        return out

    def full(x):
        return jnp.where(same, jnp.concatenate([x] * PANELS, axis=0), 0.0)

    count = len(stages)
    grow = [spread(growth, n) for n in range(count)]
    sums = [grow[0][COLS - 1 :]]
    for i in range(COLS - 2, -1, -1):
        sums.insert(0, sums[0] + grow[0][i : i + 1])
    sums = jnp.concatenate(sums, axis=0)
    products = jnp.concatenate([spread(total, n)[:, :ROWS] for n in range(count)], axis=0)
    stack = jnp.concatenate([grow[0], sums, exact(products, full(sums))], axis=0)
    select = {True: None, False: None}
    for n, (owner, forward) in enumerate(stages):
        if n:
            stack = exact(stack[:, :ROWS], full(grow[n]))
        square = jnp.sum(stack[COLS : 2 * COLS] * stack[2 * COLS : 3 * COLS], axis=0, keepdims=True)
        scale = lax.rsqrt(jnp.maximum(square, 0.0) + 1e-06)
        later = [stack[3 * COLS :]] if n + 1 < count else []
        stack = jnp.concatenate([stack[: 2 * COLS]] + later, axis=0) * scale
        back, u = stack[:COLS], panels_of(panels[n], own)
        old = select[forward]
        select[forward] = (back, u) if old is None else (
            jnp.where(me == owner, back, old[0]), jnp.where(me == owner, u, old[1])
        )
    for forward, out in ((True, out_f), (False, out_a)):
        if select[forward] is None:
            out[...] = jnp.zeros_like(out)
        else:
            back, u = select[forward]
            left = jnp.concatenate(split3(full(back)[:, :ROWS].T), axis=0)
            o = lax.dot_general(left, jnp.concatenate(split3(u), axis=1), NN, preferred_element_type=F32)
            out[...] = pieces_sum(o, ROWS, own, 3)


def shards(panels_in, blocks, block_mask, mixing):
    owners, count = lax.axis_size("tm"), lax.axis_size("space")
    me, place = lax.axis_index("tm"), lax.axis_index("space")
    nb, own = blocks.shape[1], panels_in.shape[1]
    even = lax.rem(place, 2) == 0
    bf, f32 = (lambda *s: (s, BF)), (lambda *s: (s, F32))

    def partner_a(s):
        return s ^ 1

    def partner_b(s):
        t = s + 1 if s % 2 else s - 1
        return t if 0 <= t < count else s

    def beside(x, to, only=None):
        route = [(t * count + s, t * count + to(s)) for t in (only or range(owners)) for s in range(count)]
        return lax.ppermute(x, ("tm", "space"), route)

    def hop(x, t, o, to):
        pairs = [(t, o), (o, t)] if t != o else [(t, t)]
        return lax.ppermute(x, ("tm", "space"), [(i * count + s, k * count + to(s)) for i, k in pairs for s in range(count)])

    def edges_of(x, wide_b, wide_a):
        return (
            jnp.where(even, x[:, :wide_b], x[:, own - wide_b : own]),
            jnp.where(even, x[:, own - wide_a : own], x[:, :wide_a]),
        )

    rows = blocks.reshape(RUN, nb, 3, BLOCK // 2, 2 * BLOCK).transpose(0, 2, 3, 1, 4)
    rows, mask = rows.reshape(RUN, 3, BLOCK // 2 * nb, 2 * BLOCK), block_mask.transpose(2, 0, 1)
    vm = lambda *s: pltpu.VMEM(s, F32)
    turn = owners % GROUP != 0
    turning = owners - 1 if turn else owners
    begin = call(first_kernel, [f32(8, 128)], (), flops=10**9)
    sizes = [128, 96] + ([96 * (RIM_A + RIM_B), 96 * (FAR_A + FAR_B)] if turn else [224])
    edges = call(
        functools.partial(edge_kernel, nb, turning),
        [f32(n, 128) for n in sizes],
        (*begin, rows, mask, panels_in),
    )
    near_b, near_a = beside(edges[0], partner_b, range(turning)), beside(edges[2], partner_a)
    (near_b,) = call(aside_kernel, [f32(*near_b.shape)], (near_b,), flops=ASIDE_0)
    if turn:
        far_b = beside(edges[3], partner_b, [turning])
    rows, mask, mixing, _ = lax.optimization_barrier((rows, mask, mixing, edges))
    *own_tiles, expand = call(
        functools.partial(own_kernel, nb),
        [bf(own, 256)] * 4 + [f32(2 * COLS, 128)],
        (rows, mask, mixing),
        [vm(2, own, 128)] * RUN,
    )

    def rim_call(kernel, deep_a, deep_b, args):
        deep_a, deep_b = 2 * deep_a * BLOCK, 2 * deep_b * BLOCK
        outs, scratch = [bf(deep_a, 256)] * 2 + [bf(deep_b, 256)] * 2, [vm(2, deep_a, 128), vm(2, deep_b, 128)]
        return call(kernel, outs, args, scratch)

    def late_rims(after):
        late, _ = lax.optimization_barrier((edges[1], after))
        args = (near_a, near_b, beside(late, partner_b, range(turning)))
        return rim_call(functools.partial(pull_rim_kernel, turning), 1, 2, args)

    pull_rims = None
    if turn:
        turn_rims = rim_call(functools.partial(rim_kernel, turning), RIM_A, RIM_B, (far_b, near_a))

    meta = jnp.zeros((2 * COLS, 128), F32)
    main, edge_a, edge_b = panels_in, near_a[96:128], near_b[96:128]
    stages = 2 * owners
    owner_of = [k if k < owners else stages - 1 - k for k in range(stages)]
    kept, result, k = [], None, 0
    record = ROWS * (own // 128 + 1)
    while k < stages:
        owner, slot, turned, sums = owner_of[k], k % GROUP, False, []
        turns_here, turns_next = turn and k == owners - 1, turn and k + 1 == owners - 1
        if turns_here:
            first, main, send_b = call(
                functools.partial(turn_kernel, nb, owner, slot),
                [f32(ROWS, own), f32(record + 2 * COLS, 128), f32(ROWS, 128)],
                (edge_b, main, edge_a, *own_tiles, *turn_rims, meta, expand),
            )
            kept += [first, main]
            turned = True
            meta = main[record:]
            k += 2
        else:
            if k < owners:
                main, send_b, send_a = call(
                    functools.partial(push_kernel, nb, owner),
                    [f32(ROWS, own)] + [f32(ROWS, w) for w in ((256, 384) if turns_next else (128, 128))],
                    (edge_b, main, edge_a, near_b, near_a, *own_tiles),
                    [vm(2, 2 * BLOCK, 128)],
                    flops=PUSH,
                )
                if pull_rims is None:
                    pull_rims = late_rims(send_b)
                (meta,) = call(
                    functools.partial(note_kernel, nb, owner, slot),
                    [f32(2 * COLS, 128)],
                    (main, meta, expand),
                )
            else:
                ends = (k + 1) % GROUP == 0 or k + 1 == stages
                main, meta, *sums = call(
                    functools.partial(pull_kernel, nb, owner, slot),
                    [f32(ROWS, own), f32(2 * COLS, 128)] + [f32(count, COLS, 128)] * ends,
                    (edge_b, main, edge_a, *own_tiles, *pull_rims, meta, expand),
                )
                send_b, send_a = edges_of(main, 128, 128)
            kept.append(main)
            k += 1
        share = not (turns_next and slot == 0)

        if k % GROUP == 0 or k == stages:
            todo = [(owner_of[i], i < owners) for i in range(k - len(kept), k)]
            every = sums[0] if sums else jnp.broadcast_to(meta[None, :COLS], (count, COLS, 128))
            grams = lax.all_to_all(every, "space", 0, 0)
            pair = call(
                functools.partial(scale_kernel, todo, count * own), [f32(ROWS, own)] * 2, (grams, meta, *kept)
            )
            if result is None:
                result = pair
            else:
                live = [
                    functools.reduce(jnp.logical_or, [me == o for o, f in todo if f == way], jnp.bool_(False))
                    for way in (True, False)
                ]
                result = [jnp.where(c, new, old) for c, new, old in zip(live, pair, result)]
            main = pair[0 if k - 1 < owners else 1]
            send_b, send_a = edges_of(main, *((256, 384) if turn and k == owners - 1 else (128, 128)))
            meta, kept, share, turned = jnp.zeros((2 * COLS, 128), F32), [], False, False
        if k == stages:
            break

        before, after = owner_of[k - 1], owner_of[k]
        if after != before:
            main = hop(main, before, after, lambda s: s)
        into_turn = turn and k == owners - 1
        (edge_b,) = call(
            aside_kernel,
            [f32(*send_b.shape)],
            (hop(send_b, before, after, partner_b),) + ((turn_rims[0],) if into_turn else ()),
            flops=ASIDE_1 if into_turn else ASIDE_2,
        )
        if turned:
            edge_a = main[record - ROWS : record]
            meta = meta + main[record:]
        else:
            edge_a = hop(send_a, before, after, partner_a)
            if share and after != before:
                meta = meta + hop(meta, before, after, lambda s: s)
    return result[0][None], result[1][None]


def solution(mesh):
    return jax.shard_map(
        shards,
        mesh=mesh,
        in_specs=(
            P(None, "space"),
            P("tm", "space", None, None),
            P("tm", "space", None),
            P("tm", None, None, None),
        ),
        out_specs=(P("tm", None, "space"), P("tm", None, "space")),
        check_vma=False,
    )
```

```python
import functools

import jax
import jax.numpy as jnp
from jax import lax
from jax.experimental import pallas as pl
from jax.experimental.pallas import tpu as pltpu
from jax.sharding import PartitionSpec as P

BLOCK = 64
COLS = 8
PANELS = 4
ROWS = COLS * PANELS
RUN = 2
GROUP = 4
RIM_A, RIM_B = 5, 4
FAR_A, FAR_B = 3, 2
PUSH = 3 * 10**9
ASIDE_0 = 10**10
ASIDE_1, ASIDE_2 = 7 * 10**8, 5 * 10**8
DOWN = 2.0**-16
BF = jnp.bfloat16
F32 = jnp.float32
HIGH = lax.Precision.HIGHEST
NT = (((1,), (1,)), ((), ()))
NN = (((1,), (0,)), ((), ()))
TN = (((0,), (0,)), ((), ()))
VM = pl.BlockSpec(memory_space=pltpu.VMEM)


def call(kernel, outs, args, scratch=(), flops=10**6, far=0, limit=12):
    shapes = [jax.ShapeDtypeStruct(shape, dtype) for shape, dtype in outs]
    return pl.pallas_call(
        kernel,
        out_shape=shapes,
        in_specs=[pl.BlockSpec(memory_space=pltpu.HBM)] * far + [VM] * (len(args) - far),
        out_specs=[VM] * len(outs),
        scratch_shapes=list(scratch),
        compiler_params=pltpu.CompilerParams(vmem_limit_bytes=limit << 20),
        cost_estimate=pl.CostEstimate(flops=flops, bytes_accessed=10**5, transcendentals=0),
    )(*args)


def inside():
    place, last = lax.axis_index("space"), lax.axis_size("space") - 1
    return jnp.where((place == 0) | (place == last), 0.0, 1.0).astype(F32)


def parity():
    return lax.rem(lax.axis_index("space"), 2)


def iota(shape, dim):
    return lax.broadcasted_iota(jnp.int32, shape, dim)


def presence(mask, t, j, nb):
    place, last = lax.axis_index("space"), lax.axis_size("space") - 1
    here = jnp.broadcast_to(mask[j, t : t + 1, :], (nb, nb))
    diagonal = iota((nb, nb), 0) == iota((nb, nb), 1)
    column = jnp.sum(jnp.where(diagonal, here, 0), axis=1, keepdims=True).astype(F32)
    if j == 0:
        column = jnp.where((iota((nb, 1), 0) == 0) & (place == 0), 0.0, column)
    if j == 2:
        column = jnp.where((iota((nb, 1), 0) == nb - 1) & (place == last), 0.0, column)
    return column


def first_kernel(out):
    out[...] = jnp.zeros_like(out)


def block_of(blocks, column, t, j, b, nb):
    return blocks[t, j, pl.ds(b, BLOCK // 2, stride=nb), :] * column[t][j][b : b + 1, :]


def edge_kernel(nb, turning, _, blocks, mask, panels, to_b, late_b, to_a, *refs):
    width = panels.shape[1]
    far_b, tile = refs[:-1], refs[-1]
    turns = lax.axis_index("tm") == turning
    column = [[presence(mask, t, j, nb) for j in range(3)] for t in range(RUN)]

    def near_a(dst, low_side):
        edge = 0 if low_side else nb - 1
        for j in range(3):
            dst[j * 32 : (j + 1) * 32, :] = block_of(blocks, column, 0, j, edge, nb)
        dst[96:128, :] = panels[:, :128] if low_side else panels[:, width - 128 :]
        later(dst, 128, low_side, False, 1.0)

    def near_b(dst, rest, low_side):
        keep = inside()
        edge = 0 if low_side else nb - 1
        y = [block_of(blocks, column, 0, j, edge, nb) for j in range(3)]
        dst[:32, :] = (y[0] if low_side else y[2]) * keep
        for p in range(2):
            first, second = banded(y, p)
            tile[pl.ds(p, 32, stride=2), :] = second[1] if low_side else first[0]
        group = panels[:, :128] if low_side else panels[:, width - 128 :]
        x, w = jnp.concatenate(split3(group), axis=0), jnp.concatenate(split2(tile[...]), axis=0)
        o = lax.dot_general(x, w, NT, preferred_element_type=F32)
        o = (o[2 * ROWS :] + o[ROWS : 2 * ROWS]) + o[:ROWS]
        share = (o + pltpu.roll(o, BLOCK, 1)) * keep
        low = iota((ROWS, 128), 1) < BLOCK
        dst[32:64, :] = jnp.where(low, group, share) if low_side else jnp.where(low, share, group)
        later(rest, 0, low_side, rest.shape[0] > 96, keep)

    def later(dst, at, low_side, more, keep):
        edge = 0 if low_side else nb - 1
        inner = 1 if low_side else nb - 2
        rest = [(1, edge, 0), (1, edge, 1), (1, inner, 0)] if low_side else [(1, inner, 2), (1, edge, 1), (1, edge, 2)]
        if more:
            rest += [(0, edge, 1), (0, edge, 2)] if low_side else [(0, edge, 0), (0, edge, 1)]
        for i, (t, b, j) in enumerate(rest):
            dst[at + i * 32 : at + (i + 1) * 32, :] = block_of(blocks, column, t, j, b, nb) * keep

    def far(dst, deep_a, deep_b, low_side, keep=1.0):
        at = 0
        for t, deep in ((0, deep_a), (1, deep_b)):
            for b in range(deep) if low_side else range(nb - deep, nb):
                for j in range(3):
                    dst[at : at + 32, :] = block_of(blocks, column, t, j, b, nb) * keep
                    at += 32

    for side in range(2):

        @pl.when((parity() == side) & jnp.logical_not(turns))
        def _():
            near_b(to_b, late_b, side == 0)
            near_a(to_a, side == 1)

        if far_b:

            @pl.when((parity() == side) & turns)
            def _():
                far(far_b[0], FAR_A, FAR_B, side == 0, inside())
                far(to_a, RIM_A, RIM_B, side == 1)


def banded(y, p):
    low = iota(y[0].shape, 1) < BLOCK
    zero = jnp.zeros_like(y[0])
    turned = [pltpu.roll(v, BLOCK, 1) for v in y]
    at_low, at_high = (y, turned) if p == 0 else (turned, y)
    first = (jnp.where(low, at_low[0], at_high[1]), jnp.where(low, at_low[2], zero))
    second = (jnp.where(low, zero, at_high[0]), jnp.where(low, at_low[1], at_high[2]))
    return first, second


def split2(x):
    high = x.astype(BF)
    return high, (x - high.astype(F32)).astype(BF)


def split3(x):
    first = x.astype(BF)
    x = x - first.astype(F32)
    second = x.astype(BF)
    return first, second, (x - second.astype(F32)).astype(BF)


def split_halves(wide, at, hi, lo):
    for half in range(2):
        lanes = slice(half * 128, half * 128 + 128)
        hi[:, lanes], lo[:, lanes] = split2(wide[at + half])


def own_kernel(nb, blocks, mask, mixing, a_hi, a_lo, b_hi, b_lo, expand, *wide):
    column = [[presence(mask, t, j, nb) for j in range(3)] for t in range(RUN)]
    for t, hi, lo in ((0, a_hi, a_lo), (1, b_hi, b_lo)):
        for b in range(nb):
            rim_row(wide[t], b, b % 2 == 1 - t, [block_of(blocks, column, t, j, b, nb) for j in range(3)])
        split_halves(wide[t], 0, hi, lo)
    pick = (lax.rem(iota((COLS, 128), 1), COLS) == iota((COLS, 128), 0)).astype(F32)
    row, lane = iota((ROWS, 128), 0), lax.rem(iota((ROWS, 128), 1), ROWS)
    same = (row // COLS) == (lane // COLS)
    step = []
    for t in range(RUN):
        m = mixing[t].reshape(ROWS, COLS)
        spread = lax.dot_general(m, pick, NN, precision=HIGH, preferred_element_type=F32)
        step.append((row == lane).astype(F32) - jnp.where(same, spread, 0.0))
    for i, (x, y) in enumerate(((step[0], step[1]), (step[1], step[0]))):
        e = lax.dot_general(x[:, :ROWS], y, NN, precision=HIGH, preferred_element_type=F32)
        expand[i * COLS : (i + 1) * COLS, :] = (
            e[0:COLS] + e[COLS : 2 * COLS] + e[2 * COLS : 3 * COLS] + e[3 * COLS :]
        )


def taken(from_a, from_b, left, at_a, at_b=None):
    use_b = (parity() == 0) == left
    at_b = at_a if at_b is None else at_b
    return jnp.where(use_b, from_b[at_b : at_b + 32, :], from_a[at_a : at_a + 32, :])


def rim_row(dst, index, first, y):
    for p in range(2):
        tiles = banded(y, p)[0 if first else 1]
        for half in range(2):
            dst[half, pl.ds(index * BLOCK + p, 32, stride=2), :] = tiles[half]


def edge_rows(near_a, near_b, dst, rest=None):
    even = parity() == 0
    block, none = near_b[:32, :], jnp.zeros((32, 128), F32)
    others = [none, none] if rest is None else [rest[96:128, :], rest[128:160, :]]
    for left in (True, False):
        from_b = others + [block] if left else [block] + others
        y = [jnp.where(even == left, from_b[j], near_a[j * 32 : (j + 1) * 32, :]) for j in range(3)]
        rim_row(dst, 1 - left, left, y)


def rim_kernel(turning, far_b, far_a, a_hi, a_lo, b_hi, b_lo, wide_a, wide_b):
    none = jnp.zeros((32, 128), F32)

    @pl.when(lax.axis_index("tm") == turning)
    def _():
        for dst, deep, start_a, wide, start_b, odd in (
            (wide_a, RIM_A, 0, FAR_A, 0, 1),
            (wide_b, RIM_B, 96 * RIM_A, FAR_B, 96 * FAR_A, 0),
        ):
            for i in range(deep):
                for left in (True, False):
                    k = i - (deep - wide) if left else i
                    y = []
                    for j in range(3):
                        n, m = start_a + i * 96 + j * 32, start_b + k * 96 + j * 32
                        from_b = far_b[m : m + 32, :] if 0 <= k < wide else none
                        y.append(jnp.where((parity() == 0) == left, from_b, far_a[n : n + 32, :]))
                    place = i - deep if left else i
                    rim_row(dst, i if left else deep + i, place % 2 == odd, y)
        split_halves(wide_a, 0, a_hi, a_lo)
        split_halves(wide_b, 0, b_hi, b_lo)


def pull_rim_kernel(turning, near_a, near_b, late_b, a_hi, a_lo, b_hi, b_lo, wide_a, wide_b):
    @pl.when(lax.axis_index("tm") != turning)
    def _():
        edge_rows(near_a, near_b, wide_a)
        none = jnp.zeros((32, 128), F32)
        left = [taken(near_a, late_b, True, 128 + i * 32, i * 32) for i in range(3)]
        right = [taken(near_a, late_b, False, 128 + i * 32, i * 32) for i in range(3)]
        rim_row(wide_b, 0, True, [none, none, left[0]])
        rim_row(wide_b, 1, False, [none, left[1], left[2]])
        rim_row(wide_b, 2, True, [right[0], right[1], none])
        rim_row(wide_b, 3, False, [right[2], none, none])
        split_halves(wide_a, 0, a_hi, a_lo)
        split_halves(wide_b, 0, b_hi, b_lo)


def pair_tile(own, rim, depth, nb, b):
    def row(k):
        if 0 <= k < nb:
            return own[k * BLOCK : (k + 1) * BLOCK, :]
        k = k + depth if k < 0 else depth + k - nb
        return rim[k * BLOCK : (k + 1) * BLOCK, :]

    return jnp.concatenate([row(b), row(b + 1)], axis=0)


def pieces_sum(o, m, n, skip=0):
    rows, cols = o.shape[0] // m, o.shape[1] // n
    order = sorted(((i, j) for i in range(rows) for j in range(cols)), key=lambda p: -sum(p))
    total = None
    for i, j in order[skip:]:
        piece = o[i * m : (i + 1) * m, j * n : (j + 1) * n]
        total = piece if total is None else total + piece
    return total


def product(x, w, dims):
    o = lax.dot_general(x, w, dims, preferred_element_type=F32)
    return pieces_sum(o, ROWS, 128)


def push(v, tiles):
    x = jnp.concatenate(split3(v), axis=0)
    outs = []
    for i, (hi, lo) in enumerate(tiles):
        outs.append(product(x[:, i * 128 : i * 128 + 256], jnp.concatenate([hi, lo], axis=0), NT))
    return jnp.concatenate(outs, axis=1)


def pull(v, tiles):
    x = jnp.concatenate(split3(v), axis=0)
    outs = []
    for i in range(len(tiles) - 1):
        parts = [
            jnp.concatenate([tiles[i][s][:, 128:], tiles[i + 1][s][:, :128]], axis=0) for s in range(2)
        ]
        outs.append(product(x[:, i * 128 : i * 128 + 256], jnp.concatenate(parts, axis=1), NN))
    return jnp.concatenate(outs, axis=1)


def tiles_of(refs, depth, nb, first, last):
    own_hi, own_lo, rim_hi, rim_lo = refs
    return [
        (pair_tile(own_hi, rim_hi, depth, nb, b), pair_tile(own_lo, rim_lo, depth, nb, b))
        for b in range(first, last, 2)
    ]


def gram(u):
    first = lax.rem(iota(u.shape, 0), COLS) == 0
    parts = split3(u - jnp.where(first, 0.0, pltpu.roll(u, 1, 0)))
    wide = jnp.concatenate([x for x in parts for _ in range(4)], axis=0)
    o = lax.dot_general(jnp.concatenate(parts, axis=0), wide, NT, preferred_element_type=F32)
    total = pieces_sum(o, ROWS, 128)
    panel = lax.rem(iota((COLS, 128), 1), ROWS) // COLS
    out = jnp.zeros((COLS, 128), F32)
    for p in range(PANELS):
        out = out + jnp.where(panel == p, total[p * COLS : (p + 1) * COLS], 0.0)
    return out


def noted(g, e, slot, new_g, new_e):
    mine = (iota((COLS, 128), 1) // ROWS) == slot
    return jnp.where(mine, new_g, g), jnp.where(mine, new_e, e)


def panels_of(ref, own):
    if ref.shape[0] == ROWS:
        return ref[:, :own]
    return jnp.concatenate([ref[i * ROWS : (i + 1) * ROWS, :] for i in range(own // 128)], axis=1)


def by_side(e_a, e_b):
    even = parity() == 0
    return jnp.where(even, e_b, e_a), jnp.where(even, e_a, e_b)


def aside_kernel(edge, *refs):
    refs[-1][...] = edge[...]


def push_kernel(nb, owner, edge_b, main, edge_a, near_b, near_a, a_hi, a_lo, b_hi, b_lo, *refs):
    own = nb * BLOCK
    *late, out, out_b, out_a, wide = refs

    @pl.when(lax.axis_index("tm") == owner)
    def _():
        edge_rows(near_a, near_b, wide, *late)
        rim_hi, rim_lo = split2(jnp.concatenate([wide[0], wide[1]], axis=1))
        left, right = by_side(edge_a[...], edge_b[...])
        v = jnp.concatenate([left, main[:, :own], right], axis=1)
        w = push(v, tiles_of((a_hi, a_lo, rim_hi, rim_lo), 1, nb, -1, nb))
        if not late:
            low, even = iota((ROWS, 128), 1) < BLOCK, parity() == 0
            at_left = jnp.where(low & even, edge_b[...], 0.0)
            at_right = jnp.where(low | even, 0.0, edge_b[...])
            w = jnp.concatenate([w[:, :128] + at_left, w[:, 128:own], w[:, own:] + at_right], axis=1)
        u = push(w, tiles_of((b_hi, b_lo, None, None), 0, nb, 0, nb))
        out[...] = u
        wide_b, wide_a = out_b.shape[1], out_a.shape[1]
        out_b[...] = by_side(u[:, :wide_b], u[:, own - wide_b :])[1]
        out_a[...] = by_side(u[:, own - wide_a :], u[:, :wide_a])[1]


def turn_kernel(nb, owner, slot, edge_b, main, edge_a, a_hi, a_lo, b_hi, b_lo, ra_hi, ra_lo, rb_hi, rb_lo,
                old, expand, first, out, out_b):
    own = nb * BLOCK
    pieces = own // 128
    record = slice((pieces + 1) * ROWS, (pieces + 1) * ROWS + 2 * COLS)

    @pl.when(lax.axis_index("tm") != owner)
    def _():
        out[record, :] = old[...]

    def turn(low, edges):
        a0, a1 = (RIM_A, FAR_A) if low else (FAR_A, RIM_A)
        b0, b1 = (RIM_B, FAR_B) if low else (FAR_B, RIM_B)
        v = jnp.concatenate([edges[0], main[:, :own], edges[1]], axis=1)
        tiles_a = tiles_of((a_hi, a_lo, ra_hi, ra_lo), RIM_A, nb, -a0, nb + a1)
        tiles_b = tiles_of((b_hi, b_lo, rb_hi, rb_lo), RIM_B, nb, -b0, nb + b1)
        u = push(push(v, tiles_a), tiles_b)
        u_own = u[:, b0 * BLOCK : b0 * BLOCK + own]
        first[...] = u_own
        back = pull(pull(u * DOWN, tiles_b), tiles_a[1:-1])
        back_own, beyond = (back[:, 128:], back[:, :128]) if low else (back[:, :own], back[:, own:])
        for i in range(pieces):
            out[i * ROWS : (i + 1) * ROWS, :] = back_own[:, i * 128 : (i + 1) * 128]
        out[pieces * ROWS : (pieces + 1) * ROWS, :] = beyond
        out_b[...] = back_own[:, own - 128 :] if low else back_own[:, :128]
        g, e = noted(old[:COLS], old[COLS:], slot, gram(u_own), expand[:COLS])
        g, e = noted(g, e, slot + 1, gram(back_own), expand[COLS:] * (1.0 / DOWN))
        out[record, :] = jnp.concatenate([g, e], axis=0)

    mine = lax.axis_index("tm") == owner
    pl.when(mine & (parity() == 0))(lambda: turn(False, (edge_b[...], edge_a[...])))
    pl.when(mine & (parity() == 1))(lambda: turn(True, (edge_a[...], edge_b[...])))


def pull_kernel(nb, owner, slot, edge_b, main, edge_a, a_hi, a_lo, b_hi, b_lo, ra_hi, ra_lo, rb_hi, rb_lo,
                old, expand, out, record, *every):
    own = nb * BLOCK

    @pl.when(lax.axis_index("tm") != owner)
    def _():
        record[...] = old[...]

    @pl.when(lax.axis_index("tm") == owner)
    def _():
        left, right = by_side(edge_a[...], edge_b[...])
        v = jnp.concatenate([left, panels_of(main, own), right], axis=1)
        y = pull(v, tiles_of((b_hi, b_lo, rb_hi, rb_lo), 2, nb, -2, nb + 2))
        u = pull(y, tiles_of((a_hi, a_lo, ra_hi, ra_lo), 1, nb, -1, nb + 1))
        out[...] = u
        record[:COLS], record[COLS:] = noted(old[:COLS], old[COLS:], slot, gram(u), expand[COLS:])

    for ref in every:
        for i in range(ref.shape[0]):
            ref[i] = record[:COLS]


def note_kernel(nb, owner, slot, u, old, expand, out):
    @pl.when(lax.axis_index("tm") != owner)
    def _():
        out[...] = old[...]

    @pl.when(lax.axis_index("tm") == owner)
    def _():
        out[:COLS], out[COLS:] = noted(old[:COLS], old[COLS:], slot, gram(u[:, : nb * BLOCK]), expand[:COLS])


def exact(x, y):
    rows = x.shape[0]
    m = -(-rows // 16) * 16
    if m > rows:
        x = jnp.concatenate([x, jnp.zeros((m - rows, x.shape[1]), F32)], axis=0)
    o = lax.dot_general(
        jnp.concatenate(split3(x), axis=0), jnp.concatenate(split3(y), axis=1), NN, preferred_element_type=F32
    )
    return pieces_sum(o, m, 128, 3)[:rows]


def scale_kernel(stages, boxes, grams, meta, *refs):
    panels, (out_f, out_a) = refs[: len(stages)], refs[len(stages) :]
    own = out_f.shape[1]
    parts = [grams[i] for i in range(grams.shape[0])]
    while len(parts) > 1:
        parts = [a + b for a, b in zip(parts[::2], parts[1::2])] + parts[len(parts) // 2 * 2 :]
    total = parts[0] * (1.0 / boxes)
    growth = meta[COLS:, :]
    row, lane = iota((ROWS, 128), 0), iota((ROWS, 128), 1)
    same = (row // COLS) == (lax.rem(lane, ROWS) // COLS)
    group = lane[:COLS] // ROWS
    me = lax.axis_index("tm")

    def spread(x, n):
        turns = [x if k == n else pltpu.roll(x, ((k - n) % 4) * ROWS, 1) for k in range(4)]
        out = turns[0]
        for k in range(1, 4):
            out = jnp.where(group == k, turns[k], out)
        return out

    def full(x):
        return jnp.where(same, jnp.concatenate([x] * PANELS, axis=0), 0.0)

    count = len(stages)
    grow = [spread(growth, n) for n in range(count)]
    sums = [grow[0][COLS - 1 :]]
    for i in range(COLS - 2, -1, -1):
        sums.insert(0, sums[0] + grow[0][i : i + 1])
    sums = jnp.concatenate(sums, axis=0)
    products = jnp.concatenate([spread(total, n)[:, :ROWS] for n in range(count)], axis=0)
    stack = jnp.concatenate([grow[0], sums, exact(products, full(sums))], axis=0)
    select = {True: None, False: None}
    for n, (owner, forward) in enumerate(stages):
        if n:
            stack = exact(stack[:, :ROWS], full(grow[n]))
        square = jnp.sum(stack[COLS : 2 * COLS] * stack[2 * COLS : 3 * COLS], axis=0, keepdims=True)
        scale = lax.rsqrt(jnp.maximum(square, 0.0) + 1e-06)
        later = [stack[3 * COLS :]] if n + 1 < count else []
        stack = jnp.concatenate([stack[: 2 * COLS]] + later, axis=0) * scale
        back, u = stack[:COLS], panels_of(panels[n], own)
        old = select[forward]
        select[forward] = (back, u) if old is None else (
            jnp.where(me == owner, back, old[0]), jnp.where(me == owner, u, old[1])
        )
    for forward, out in ((True, out_f), (False, out_a)):
        if select[forward] is None:
            out[...] = jnp.zeros_like(out)
        else:
            back, u = select[forward]
            left = jnp.concatenate(split3(full(back)[:, :ROWS].T), axis=0)
            o = lax.dot_general(left, jnp.concatenate(split3(u), axis=1), NN, preferred_element_type=F32)
            out[...] = pieces_sum(o, ROWS, own, 3)


def shards(panels_in, blocks, block_mask, mixing):
    owners, count = lax.axis_size("tm"), lax.axis_size("space")
    me, place = lax.axis_index("tm"), lax.axis_index("space")
    nb, own = blocks.shape[1], panels_in.shape[1]
    even = lax.rem(place, 2) == 0
    bf, f32 = (lambda *s: (s, BF)), (lambda *s: (s, F32))

    def partner_a(s):
        return s ^ 1

    def partner_b(s):
        t = s + 1 if s % 2 else s - 1
        return t if 0 <= t < count else s

    def beside(x, to, only=None):
        route = [(t * count + s, t * count + to(s)) for t in (only or range(owners)) for s in range(count)]
        return lax.ppermute(x, ("tm", "space"), route)

    def hop(x, t, o, to):
        pairs = [(t, o), (o, t)] if t != o else [(t, t)]
        return lax.ppermute(x, ("tm", "space"), [(i * count + s, k * count + to(s)) for i, k in pairs for s in range(count)])

    def edges_of(x, wide_b, wide_a):
        return (
            jnp.where(even, x[:, :wide_b], x[:, own - wide_b : own]),
            jnp.where(even, x[:, own - wide_a : own], x[:, :wide_a]),
        )

    rows = blocks.reshape(RUN, nb, 3, BLOCK // 2, 2 * BLOCK).transpose(0, 2, 3, 1, 4)
    rows, mask = rows.reshape(RUN, 3, BLOCK // 2 * nb, 2 * BLOCK), block_mask.transpose(2, 0, 1)
    vm = lambda *s: pltpu.VMEM(s, F32)
    turn = owners % GROUP != 0
    turning = owners - 1 if turn else owners
    begin = call(first_kernel, [f32(8, 128)], (), flops=10**9)
    sizes = [64, 96 if owners == 2 else 160] + ([96 * (RIM_A + RIM_B), 96 * (FAR_A + FAR_B)] if turn else [224])
    edges = call(
        functools.partial(edge_kernel, nb, turning),
        [f32(n, 128) for n in sizes],
        (*begin, rows, mask, panels_in),
        [vm(BLOCK, 128)],
    )
    near_b, near_a = beside(edges[0], partner_b, range(turning)), beside(edges[2], partner_a)
    (near_b,) = call(aside_kernel, [f32(*near_b.shape)], (near_b,), flops=ASIDE_0)
    if turn:
        far_b = beside(edges[3], partner_b, [turning])
    rows, mask, mixing, _ = lax.optimization_barrier((rows, mask, mixing, edges))
    *own_tiles, expand = call(
        functools.partial(own_kernel, nb),
        [bf(own, 256)] * 4 + [f32(2 * COLS, 128)],
        (rows, mask, mixing),
        [vm(2, own, 128)] * RUN,
    )

    def rim_call(kernel, deep_a, deep_b, args):
        deep_a, deep_b = 2 * deep_a * BLOCK, 2 * deep_b * BLOCK
        outs, scratch = [bf(deep_a, 256)] * 2 + [bf(deep_b, 256)] * 2, [vm(2, deep_a, 128), vm(2, deep_b, 128)]
        return call(kernel, outs, args, scratch)

    def late_rims(after):
        late, _ = lax.optimization_barrier((edges[1], after))
        late = beside(late, partner_b, range(turning))
        args = (near_a, near_b, late)
        return late, rim_call(functools.partial(pull_rim_kernel, turning), 1, 2, args)

    pull_rims = None
    if turn:
        turn_rims = rim_call(functools.partial(rim_kernel, turning), RIM_A, RIM_B, (far_b, near_a))

    meta = jnp.zeros((2 * COLS, 128), F32)
    main, edge_a, edge_b = panels_in, near_a[96:128], near_b[32:64]
    stages = 2 * owners
    owner_of = [k if k < owners else stages - 1 - k for k in range(stages)]
    kept, result, k = [], None, 0
    record = ROWS * (own // 128 + 1)
    while k < stages:
        owner, slot, turned, sums = owner_of[k], k % GROUP, False, []
        turns_here, turns_next = turn and k == owners - 1, turn and k + 1 == owners - 1
        if turns_here:
            first, main, send_b = call(
                functools.partial(turn_kernel, nb, owner, slot),
                [f32(ROWS, own), f32(record + 2 * COLS, 128), f32(ROWS, 128)],
                (edge_b, main, edge_a, *own_tiles, *turn_rims, meta, expand),
            )
            kept += [first, main]
            turned = True
            meta = main[record:]
            k += 2
        else:
            if k < owners:
                main, send_b, send_a = call(
                    functools.partial(push_kernel, nb, owner),
                    [f32(ROWS, own)] + [f32(ROWS, w) for w in ((256, 384) if turns_next else (128, 128))],
                    (edge_b, main, edge_a, near_b, near_a, *own_tiles, *([late_b] if k else [])),
                    [vm(2, 2 * BLOCK, 128)],
                    flops=PUSH,
                )
                if pull_rims is None:
                    late_b, pull_rims = late_rims(send_b)
                (meta,) = call(
                    functools.partial(note_kernel, nb, owner, slot),
                    [f32(2 * COLS, 128)],
                    (main, meta, expand),
                )
            else:
                ends = (k + 1) % GROUP == 0 or k + 1 == stages
                main, meta, *sums = call(
                    functools.partial(pull_kernel, nb, owner, slot),
                    [f32(ROWS, own), f32(2 * COLS, 128)] + [f32(count, COLS, 128)] * ends,
                    (edge_b, main, edge_a, *own_tiles, *pull_rims, meta, expand),
                )
                send_b, send_a = edges_of(main, 128, 128)
            kept.append(main)
            k += 1
        share = not (turns_next and slot == 0)

        if k % GROUP == 0 or k == stages:
            todo = [(owner_of[i], i < owners) for i in range(k - len(kept), k)]
            every = sums[0] if sums else jnp.broadcast_to(meta[None, :COLS], (count, COLS, 128))
            grams = lax.all_to_all(every, "space", 0, 0)
            pair = call(
                functools.partial(scale_kernel, todo, count * own), [f32(ROWS, own)] * 2, (grams, meta, *kept)
            )
            if result is None:
                result = pair
            else:
                live = [
                    functools.reduce(jnp.logical_or, [me == o for o, f in todo if f == way], jnp.bool_(False))
                    for way in (True, False)
                ]
                result = [jnp.where(c, new, old) for c, new, old in zip(live, pair, result)]
            main = pair[0 if k - 1 < owners else 1]
            send_b, send_a = edges_of(main, *((256, 384) if turn and k == owners - 1 else (128, 128)))
            meta, kept, share, turned = jnp.zeros((2 * COLS, 128), F32), [], False, False
        if k == stages:
            break

        before, after = owner_of[k - 1], owner_of[k]
        if after != before:
            main = hop(main, before, after, lambda s: s)
        into_turn = turn and k == owners - 1
        (edge_b,) = call(
            aside_kernel,
            [f32(*send_b.shape)],
            (hop(send_b, before, after, partner_b),) + ((turn_rims[0],) if into_turn else ()),
            flops=ASIDE_1 if into_turn else ASIDE_2,
        )
        if turned:
            edge_a = main[record - ROWS : record]
            meta = meta + main[record:]
        else:
            edge_a = hop(send_a, before, after, partner_a)
            if share and after != before:
                meta = meta + hop(meta, before, after, lambda s: s)
    return result[0][None], result[1][None]


def solution(mesh):
    return jax.shard_map(
        shards,
        mesh=mesh,
        in_specs=(
            P(None, "space"),
            P("tm", "space", None, None),
            P("tm", "space", None),
            P("tm", None, None, None),
        ),
        out_specs=(P("tm", None, "space"), P("tm", None, "space")),
        check_vma=False,
    )
```

```python
import functools

import jax
import jax.numpy as jnp
from jax import lax
from jax.experimental import pallas as pl
from jax.experimental.pallas import tpu as pltpu
from jax.sharding import PartitionSpec as P

BLOCK = 64
COLS = 8
PANELS = 4
ROWS = COLS * PANELS
RUN = 2
GROUP = 4
RIM_A, RIM_B = 5, 4
FAR_A, FAR_B = 3, 2
PUSH = 3 * 10**9
ASIDE_0 = 10**10
ASIDE_1, ASIDE_2 = 7 * 10**8, 5 * 10**8
DOWN = 2.0**-16
BF = jnp.bfloat16
F32 = jnp.float32
HIGH = lax.Precision.HIGHEST
NT = (((1,), (1,)), ((), ()))
NN = (((1,), (0,)), ((), ()))
TN = (((0,), (0,)), ((), ()))
VM = pl.BlockSpec(memory_space=pltpu.VMEM)


def call(kernel, outs, args, scratch=(), flops=10**6, far=0, limit=12):
    shapes = [jax.ShapeDtypeStruct(shape, dtype) for shape, dtype in outs]
    return pl.pallas_call(
        kernel,
        out_shape=shapes,
        in_specs=[pl.BlockSpec(memory_space=pltpu.HBM)] * far + [VM] * (len(args) - far),
        out_specs=[VM] * len(outs),
        scratch_shapes=list(scratch),
        compiler_params=pltpu.CompilerParams(vmem_limit_bytes=limit << 20),
        cost_estimate=pl.CostEstimate(flops=flops, bytes_accessed=10**5, transcendentals=0),
    )(*args)


def inside():
    place, last = lax.axis_index("space"), lax.axis_size("space") - 1
    return jnp.where((place == 0) | (place == last), 0.0, 1.0).astype(F32)


def parity():
    return lax.rem(lax.axis_index("space"), 2)


def iota(shape, dim):
    return lax.broadcasted_iota(jnp.int32, shape, dim)


def presence(mask, t, j, nb):
    place, last = lax.axis_index("space"), lax.axis_size("space") - 1
    here = jnp.broadcast_to(mask[j, t : t + 1, :], (nb, nb))
    diagonal = iota((nb, nb), 0) == iota((nb, nb), 1)
    column = jnp.sum(jnp.where(diagonal, here, 0), axis=1, keepdims=True).astype(F32)
    if j == 0:
        column = jnp.where((iota((nb, 1), 0) == 0) & (place == 0), 0.0, column)
    if j == 2:
        column = jnp.where((iota((nb, 1), 0) == nb - 1) & (place == last), 0.0, column)
    return column


def first_kernel(out):
    out[...] = jnp.zeros_like(out)


def block_of(blocks, column, t, j, b, nb):
    return blocks[t, j, pl.ds(b, BLOCK // 2, stride=nb), :] * column[t][j][b : b + 1, :]


def edge_kernel(nb, turning, parts, _, blocks, mask, panels, *refs):
    width = panels.shape[1]
    to_b, tile = refs if parts == "first" else (None, None)
    late_b, to_a, *far_b = (None, None) if parts == "first" else refs
    turns = lax.axis_index("tm") == turning
    column = [[presence(mask, t, j, nb) for j in range(3)] for t in range(RUN)]

    def near_a(dst, low_side):
        edge = 0 if low_side else nb - 1
        for j in range(3):
            dst[j * 32 : (j + 1) * 32, :] = block_of(blocks, column, 0, j, edge, nb)
        dst[96:128, :] = panels[:, :128] if low_side else panels[:, width - 128 :]
        later(dst, 128, low_side, False, 1.0)

    def near_b(dst, low_side):
        keep = inside()
        edge = 0 if low_side else nb - 1
        y = [block_of(blocks, column, 0, j, edge, nb) for j in range(3)]
        dst[:32, :] = (y[0] if low_side else y[2]) * keep
        for p in range(2):
            first, second = banded(y, p)
            tile[pl.ds(p, 32, stride=2), :] = second[1] if low_side else first[0]
        group = panels[:, :128] if low_side else panels[:, width - 128 :]
        x, w = jnp.concatenate(split3(group), axis=0), jnp.concatenate(split2(tile[...]), axis=0)
        o = lax.dot_general(x, w, NT, preferred_element_type=F32)
        o = (o[2 * ROWS :] + o[ROWS : 2 * ROWS]) + o[:ROWS]
        share = (o + pltpu.roll(o, BLOCK, 1)) * keep
        low = iota((ROWS, 128), 1) < BLOCK
        dst[32:64, :] = jnp.where(low, group, share) if low_side else jnp.where(low, share, group)

    def later(dst, at, low_side, more, keep):
        edge = 0 if low_side else nb - 1
        inner = 1 if low_side else nb - 2
        rest = [(1, edge, 0), (1, edge, 1), (1, inner, 0)] if low_side else [(1, inner, 2), (1, edge, 1), (1, edge, 2)]
        if more:
            rest += [(0, edge, 1), (0, edge, 2)] if low_side else [(0, edge, 0), (0, edge, 1)]
        for i, (t, b, j) in enumerate(rest):
            dst[at + i * 32 : at + (i + 1) * 32, :] = block_of(blocks, column, t, j, b, nb) * keep

    def far(dst, deep_a, deep_b, low_side, keep=1.0):
        at = 0
        for t, deep in ((0, deep_a), (1, deep_b)):
            for b in range(deep) if low_side else range(nb - deep, nb):
                for j in range(3):
                    dst[at : at + 32, :] = block_of(blocks, column, t, j, b, nb) * keep
                    at += 32

    for side in range(2):

        @pl.when((parity() == side) & jnp.logical_not(turns))
        def _():
            if parts == "first":
                near_b(to_b, side == 0)
            else:
                later(late_b, 0, side == 0, late_b.shape[0] > 96, inside())
                near_a(to_a, side == 1)

        if far_b:

            @pl.when((parity() == side) & turns)
            def _():
                far(far_b[0], FAR_A, FAR_B, side == 0, inside())
                far(to_a, RIM_A, RIM_B, side == 1)


def banded(y, p):
    low = iota(y[0].shape, 1) < BLOCK
    zero = jnp.zeros_like(y[0])
    turned = [pltpu.roll(v, BLOCK, 1) for v in y]
    at_low, at_high = (y, turned) if p == 0 else (turned, y)
    first = (jnp.where(low, at_low[0], at_high[1]), jnp.where(low, at_low[2], zero))
    second = (jnp.where(low, zero, at_high[0]), jnp.where(low, at_low[1], at_high[2]))
    return first, second


def split2(x):
    high = x.astype(BF)
    return high, (x - high.astype(F32)).astype(BF)


def split3(x):
    first = x.astype(BF)
    x = x - first.astype(F32)
    second = x.astype(BF)
    return first, second, (x - second.astype(F32)).astype(BF)


def split_halves(wide, at, hi, lo):
    for half in range(2):
        lanes = slice(half * 128, half * 128 + 128)
        hi[:, lanes], lo[:, lanes] = split2(wide[at + half])


def own_kernel(nb, blocks, mask, mixing, a_hi, a_lo, b_hi, b_lo, expand, *wide):
    column = [[presence(mask, t, j, nb) for j in range(3)] for t in range(RUN)]
    for t, hi, lo in ((0, a_hi, a_lo), (1, b_hi, b_lo)):
        for b in range(nb):
            rim_row(wide[t], b, b % 2 == 1 - t, [block_of(blocks, column, t, j, b, nb) for j in range(3)])
        split_halves(wide[t], 0, hi, lo)
    pick = (lax.rem(iota((COLS, 128), 1), COLS) == iota((COLS, 128), 0)).astype(F32)
    row, lane = iota((ROWS, 128), 0), lax.rem(iota((ROWS, 128), 1), ROWS)
    same = (row // COLS) == (lane // COLS)
    step = []
    for t in range(RUN):
        m = mixing[t].reshape(ROWS, COLS)
        spread = lax.dot_general(m, pick, NN, precision=HIGH, preferred_element_type=F32)
        step.append((row == lane).astype(F32) - jnp.where(same, spread, 0.0))
    for i, (x, y) in enumerate(((step[0], step[1]), (step[1], step[0]))):
        e = lax.dot_general(x[:, :ROWS], y, NN, precision=HIGH, preferred_element_type=F32)
        expand[i * COLS : (i + 1) * COLS, :] = (
            e[0:COLS] + e[COLS : 2 * COLS] + e[2 * COLS : 3 * COLS] + e[3 * COLS :]
        )


def taken(from_a, from_b, left, at_a, at_b=None):
    use_b = (parity() == 0) == left
    at_b = at_a if at_b is None else at_b
    return jnp.where(use_b, from_b[at_b : at_b + 32, :], from_a[at_a : at_a + 32, :])


def rim_row(dst, index, first, y):
    for p in range(2):
        tiles = banded(y, p)[0 if first else 1]
        for half in range(2):
            dst[half, pl.ds(index * BLOCK + p, 32, stride=2), :] = tiles[half]


def edge_rows(near_a, near_b, dst, rest=None):
    even = parity() == 0
    block, none = near_b[:32, :], jnp.zeros((32, 128), F32)
    others = [none, none] if rest is None else [rest[96:128, :], rest[128:160, :]]
    for left in (True, False):
        from_b = others + [block] if left else [block] + others
        y = [jnp.where(even == left, from_b[j], near_a[j * 32 : (j + 1) * 32, :]) for j in range(3)]
        rim_row(dst, 1 - left, left, y)


def rim_kernel(turning, far_b, far_a, a_hi, a_lo, b_hi, b_lo, wide_a, wide_b):
    none = jnp.zeros((32, 128), F32)

    @pl.when(lax.axis_index("tm") == turning)
    def _():
        for dst, deep, start_a, wide, start_b, odd in (
            (wide_a, RIM_A, 0, FAR_A, 0, 1),
            (wide_b, RIM_B, 96 * RIM_A, FAR_B, 96 * FAR_A, 0),
        ):
            for i in range(deep):
                for left in (True, False):
                    k = i - (deep - wide) if left else i
                    y = []
                    for j in range(3):
                        n, m = start_a + i * 96 + j * 32, start_b + k * 96 + j * 32
                        from_b = far_b[m : m + 32, :] if 0 <= k < wide else none
                        y.append(jnp.where((parity() == 0) == left, from_b, far_a[n : n + 32, :]))
                    place = i - deep if left else i
                    rim_row(dst, i if left else deep + i, place % 2 == odd, y)
        split_halves(wide_a, 0, a_hi, a_lo)
        split_halves(wide_b, 0, b_hi, b_lo)


def pull_rim_kernel(turning, near_a, near_b, late_b, a_hi, a_lo, b_hi, b_lo, wide_a, wide_b):
    @pl.when(lax.axis_index("tm") != turning)
    def _():
        edge_rows(near_a, near_b, wide_a)
        none = jnp.zeros((32, 128), F32)
        left = [taken(near_a, late_b, True, 128 + i * 32, i * 32) for i in range(3)]
        right = [taken(near_a, late_b, False, 128 + i * 32, i * 32) for i in range(3)]
        rim_row(wide_b, 0, True, [none, none, left[0]])
        rim_row(wide_b, 1, False, [none, left[1], left[2]])
        rim_row(wide_b, 2, True, [right[0], right[1], none])
        rim_row(wide_b, 3, False, [right[2], none, none])
        split_halves(wide_a, 0, a_hi, a_lo)
        split_halves(wide_b, 0, b_hi, b_lo)


def pair_tile(own, rim, depth, nb, b):
    def row(k):
        if 0 <= k < nb:
            return own[k * BLOCK : (k + 1) * BLOCK, :]
        k = k + depth if k < 0 else depth + k - nb
        return rim[k * BLOCK : (k + 1) * BLOCK, :]

    return jnp.concatenate([row(b), row(b + 1)], axis=0)


def pieces_sum(o, m, n, skip=0):
    rows, cols = o.shape[0] // m, o.shape[1] // n
    order = sorted(((i, j) for i in range(rows) for j in range(cols)), key=lambda p: -sum(p))
    total = None
    for i, j in order[skip:]:
        piece = o[i * m : (i + 1) * m, j * n : (j + 1) * n]
        total = piece if total is None else total + piece
    return total


def product(x, w, dims):
    o = lax.dot_general(x, w, dims, preferred_element_type=F32)
    return pieces_sum(o, ROWS, 128)


def push(v, tiles):
    x = jnp.concatenate(split3(v), axis=0)
    outs = []
    for i, (hi, lo) in enumerate(tiles):
        outs.append(product(x[:, i * 128 : i * 128 + 256], jnp.concatenate([hi, lo], axis=0), NT))
    return jnp.concatenate(outs, axis=1)


def pull(v, tiles):
    x = jnp.concatenate(split3(v), axis=0)
    outs = []
    for i in range(len(tiles) - 1):
        parts = [
            jnp.concatenate([tiles[i][s][:, 128:], tiles[i + 1][s][:, :128]], axis=0) for s in range(2)
        ]
        outs.append(product(x[:, i * 128 : i * 128 + 256], jnp.concatenate(parts, axis=1), NN))
    return jnp.concatenate(outs, axis=1)


def tiles_of(refs, depth, nb, first, last):
    own_hi, own_lo, rim_hi, rim_lo = refs
    return [
        (pair_tile(own_hi, rim_hi, depth, nb, b), pair_tile(own_lo, rim_lo, depth, nb, b))
        for b in range(first, last, 2)
    ]


def gram(u):
    first = lax.rem(iota(u.shape, 0), COLS) == 0
    parts = split3(u - jnp.where(first, 0.0, pltpu.roll(u, 1, 0)))
    wide = jnp.concatenate([x for x in parts for _ in range(4)], axis=0)
    o = lax.dot_general(jnp.concatenate(parts, axis=0), wide, NT, preferred_element_type=F32)
    total = pieces_sum(o, ROWS, 128)
    panel = lax.rem(iota((COLS, 128), 1), ROWS) // COLS
    out = jnp.zeros((COLS, 128), F32)
    for p in range(PANELS):
        out = out + jnp.where(panel == p, total[p * COLS : (p + 1) * COLS], 0.0)
    return out


def noted(g, e, slot, new_g, new_e):
    mine = (iota((COLS, 128), 1) // ROWS) == slot
    return jnp.where(mine, new_g, g), jnp.where(mine, new_e, e)


def panels_of(ref, own):
    if ref.shape[0] == ROWS:
        return ref[:, :own]
    return jnp.concatenate([ref[i * ROWS : (i + 1) * ROWS, :] for i in range(own // 128)], axis=1)


def by_side(e_a, e_b):
    even = parity() == 0
    return jnp.where(even, e_b, e_a), jnp.where(even, e_a, e_b)


def aside_kernel(edge, *refs):
    refs[-1][...] = edge[...]


def push_kernel(nb, owner, edge_b, main, edge_a, near_b, near_a, a_hi, a_lo, b_hi, b_lo, *refs):
    own = nb * BLOCK
    *late, out, out_b, out_a, wide = refs

    @pl.when(lax.axis_index("tm") == owner)
    def _():
        edge_rows(near_a, near_b, wide, *late)
        rim_hi, rim_lo = split2(jnp.concatenate([wide[0], wide[1]], axis=1))
        left, right = by_side(edge_a[...], edge_b[...])
        v = jnp.concatenate([left, main[:, :own], right], axis=1)
        w = push(v, tiles_of((a_hi, a_lo, rim_hi, rim_lo), 1, nb, -1, nb))
        if not late:
            low, even = iota((ROWS, 128), 1) < BLOCK, parity() == 0
            at_left = jnp.where(low & even, edge_b[...], 0.0)
            at_right = jnp.where(low | even, 0.0, edge_b[...])
            w = jnp.concatenate([w[:, :128] + at_left, w[:, 128:own], w[:, own:] + at_right], axis=1)
        u = push(w, tiles_of((b_hi, b_lo, None, None), 0, nb, 0, nb))
        out[...] = u
        wide_b, wide_a = out_b.shape[1], out_a.shape[1]
        out_b[...] = by_side(u[:, :wide_b], u[:, own - wide_b :])[1]
        out_a[...] = by_side(u[:, own - wide_a :], u[:, :wide_a])[1]


def turn_kernel(nb, owner, slot, edge_b, main, edge_a, a_hi, a_lo, b_hi, b_lo, ra_hi, ra_lo, rb_hi, rb_lo,
                old, expand, first, out, out_b):
    own = nb * BLOCK
    pieces = own // 128
    record = slice((pieces + 1) * ROWS, (pieces + 1) * ROWS + 2 * COLS)

    @pl.when(lax.axis_index("tm") != owner)
    def _():
        out[record, :] = old[...]

    def turn(low, edges):
        a0, a1 = (RIM_A, FAR_A) if low else (FAR_A, RIM_A)
        b0, b1 = (RIM_B, FAR_B) if low else (FAR_B, RIM_B)
        v = jnp.concatenate([edges[0], main[:, :own], edges[1]], axis=1)
        tiles_a = tiles_of((a_hi, a_lo, ra_hi, ra_lo), RIM_A, nb, -a0, nb + a1)
        tiles_b = tiles_of((b_hi, b_lo, rb_hi, rb_lo), RIM_B, nb, -b0, nb + b1)
        u = push(push(v, tiles_a), tiles_b)
        u_own = u[:, b0 * BLOCK : b0 * BLOCK + own]
        first[...] = u_own
        back = pull(pull(u * DOWN, tiles_b), tiles_a[1:-1])
        back_own, beyond = (back[:, 128:], back[:, :128]) if low else (back[:, :own], back[:, own:])
        for i in range(pieces):
            out[i * ROWS : (i + 1) * ROWS, :] = back_own[:, i * 128 : (i + 1) * 128]
        out[pieces * ROWS : (pieces + 1) * ROWS, :] = beyond
        out_b[...] = back_own[:, own - 128 :] if low else back_own[:, :128]
        g, e = noted(old[:COLS], old[COLS:], slot, gram(u_own), expand[:COLS])
        g, e = noted(g, e, slot + 1, gram(back_own), expand[COLS:] * (1.0 / DOWN))
        out[record, :] = jnp.concatenate([g, e], axis=0)

    mine = lax.axis_index("tm") == owner
    pl.when(mine & (parity() == 0))(lambda: turn(False, (edge_b[...], edge_a[...])))
    pl.when(mine & (parity() == 1))(lambda: turn(True, (edge_a[...], edge_b[...])))


def pull_kernel(nb, owner, slot, edge_b, main, edge_a, a_hi, a_lo, b_hi, b_lo, ra_hi, ra_lo, rb_hi, rb_lo,
                old, expand, out, record, *every):
    own = nb * BLOCK

    @pl.when(lax.axis_index("tm") != owner)
    def _():
        record[...] = old[...]

    @pl.when(lax.axis_index("tm") == owner)
    def _():
        left, right = by_side(edge_a[...], edge_b[...])
        v = jnp.concatenate([left, panels_of(main, own), right], axis=1)
        y = pull(v, tiles_of((b_hi, b_lo, rb_hi, rb_lo), 2, nb, -2, nb + 2))
        u = pull(y, tiles_of((a_hi, a_lo, ra_hi, ra_lo), 1, nb, -1, nb + 1))
        out[...] = u
        record[:COLS], record[COLS:] = noted(old[:COLS], old[COLS:], slot, gram(u), expand[COLS:])

    for ref in every:
        for i in range(ref.shape[0]):
            ref[i] = record[:COLS]


def note_kernel(nb, owner, slot, u, old, expand, out):
    @pl.when(lax.axis_index("tm") != owner)
    def _():
        out[...] = old[...]

    @pl.when(lax.axis_index("tm") == owner)
    def _():
        out[:COLS], out[COLS:] = noted(old[:COLS], old[COLS:], slot, gram(u[:, : nb * BLOCK]), expand[:COLS])


def exact(x, y):
    rows = x.shape[0]
    m = -(-rows // 16) * 16
    if m > rows:
        x = jnp.concatenate([x, jnp.zeros((m - rows, x.shape[1]), F32)], axis=0)
    o = lax.dot_general(
        jnp.concatenate(split3(x), axis=0), jnp.concatenate(split3(y), axis=1), NN, preferred_element_type=F32
    )
    return pieces_sum(o, m, 128, 3)[:rows]


def scale_kernel(stages, boxes, grams, meta, *refs):
    panels, (out_f, out_a) = refs[: len(stages)], refs[len(stages) :]
    own = out_f.shape[1]
    parts = [grams[i] for i in range(grams.shape[0])]
    while len(parts) > 1:
        parts = [a + b for a, b in zip(parts[::2], parts[1::2])] + parts[len(parts) // 2 * 2 :]
    total = parts[0] * (1.0 / boxes)
    growth = meta[COLS:, :]
    row, lane = iota((ROWS, 128), 0), iota((ROWS, 128), 1)
    same = (row // COLS) == (lax.rem(lane, ROWS) // COLS)
    group = lane[:COLS] // ROWS
    me = lax.axis_index("tm")

    def spread(x, n):
        turns = [x if k == n else pltpu.roll(x, ((k - n) % 4) * ROWS, 1) for k in range(4)]
        out = turns[0]
        for k in range(1, 4):
            out = jnp.where(group == k, turns[k], out)
        return out

    def full(x):
        return jnp.where(same, jnp.concatenate([x] * PANELS, axis=0), 0.0)

    count = len(stages)
    grow = [spread(growth, n) for n in range(count)]
    sums = [grow[0][COLS - 1 :]]
    for i in range(COLS - 2, -1, -1):
        sums.insert(0, sums[0] + grow[0][i : i + 1])
    sums = jnp.concatenate(sums, axis=0)
    products = jnp.concatenate([spread(total, n)[:, :ROWS] for n in range(count)], axis=0)
    stack = jnp.concatenate([grow[0], sums, exact(products, full(sums))], axis=0)
    select = {True: None, False: None}
    for n, (owner, forward) in enumerate(stages):
        if n:
            stack = exact(stack[:, :ROWS], full(grow[n]))
        square = jnp.sum(stack[COLS : 2 * COLS] * stack[2 * COLS : 3 * COLS], axis=0, keepdims=True)
        scale = lax.rsqrt(jnp.maximum(square, 0.0) + 1e-06)
        later = [stack[3 * COLS :]] if n + 1 < count else []
        stack = jnp.concatenate([stack[: 2 * COLS]] + later, axis=0) * scale
        back, u = stack[:COLS], panels_of(panels[n], own)
        old = select[forward]
        select[forward] = (back, u) if old is None else (
            jnp.where(me == owner, back, old[0]), jnp.where(me == owner, u, old[1])
        )
    for forward, out in ((True, out_f), (False, out_a)):
        if select[forward] is None:
            out[...] = jnp.zeros_like(out)
        else:
            back, u = select[forward]
            left = jnp.concatenate(split3(full(back)[:, :ROWS].T), axis=0)
            o = lax.dot_general(left, jnp.concatenate(split3(u), axis=1), NN, preferred_element_type=F32)
            out[...] = pieces_sum(o, ROWS, own, 3)


def shards(panels_in, blocks, block_mask, mixing):
    owners, count = lax.axis_size("tm"), lax.axis_size("space")
    me, place = lax.axis_index("tm"), lax.axis_index("space")
    nb, own = blocks.shape[1], panels_in.shape[1]
    even = lax.rem(place, 2) == 0
    bf, f32 = (lambda *s: (s, BF)), (lambda *s: (s, F32))

    def partner_a(s):
        return s ^ 1

    def partner_b(s):
        t = s + 1 if s % 2 else s - 1
        return t if 0 <= t < count else s

    def beside(x, to, only=None):
        route = [(t * count + s, t * count + to(s)) for t in (only or range(owners)) for s in range(count)]
        return lax.ppermute(x, ("tm", "space"), route)

    def hop(x, t, o, to):
        pairs = [(t, o), (o, t)] if t != o else [(t, t)]
        return lax.ppermute(x, ("tm", "space"), [(i * count + s, k * count + to(s)) for i, k in pairs for s in range(count)])

    def edges_of(x, wide_b, wide_a):
        return (
            jnp.where(even, x[:, :wide_b], x[:, own - wide_b : own]),
            jnp.where(even, x[:, own - wide_a : own], x[:, :wide_a]),
        )

    rows = blocks.reshape(RUN, nb, 3, BLOCK // 2, 2 * BLOCK).transpose(0, 2, 3, 1, 4)
    rows, mask = rows.reshape(RUN, 3, BLOCK // 2 * nb, 2 * BLOCK), block_mask.transpose(2, 0, 1)
    vm = lambda *s: pltpu.VMEM(s, F32)
    turn = owners % GROUP != 0
    turning = owners - 1 if turn else owners
    begin = call(first_kernel, [f32(8, 128)], (), flops=10**9)
    (near,) = call(
        functools.partial(edge_kernel, nb, turning, "first"),
        [f32(64, 128)],
        (*begin, rows, mask, panels_in),
        [vm(BLOCK, 128)],
    )
    near_b = beside(near, partner_b, range(turning))
    begin, rows, mask, mixing, _ = lax.optimization_barrier((begin, rows, mask, mixing, near))
    sizes = [96 if owners == 2 else 160]
    sizes += [96 * (RIM_A + RIM_B), 96 * (FAR_A + FAR_B)] if turn else [224]
    edges = call(
        functools.partial(edge_kernel, nb, turning, "rest"),
        [f32(n, 128) for n in sizes],
        (*begin, rows, mask, panels_in),
    )
    near_a = beside(edges[1], partner_a)
    (near_b,) = call(aside_kernel, [f32(*near_b.shape)], (near_b,), flops=ASIDE_0)
    if turn:
        far_b = beside(edges[2], partner_b, [turning])
    *own_tiles, expand = call(
        functools.partial(own_kernel, nb),
        [bf(own, 256)] * 4 + [f32(2 * COLS, 128)],
        (rows, mask, mixing),
        [vm(2, own, 128)] * RUN,
    )

    def rim_call(kernel, deep_a, deep_b, args):
        deep_a, deep_b = 2 * deep_a * BLOCK, 2 * deep_b * BLOCK
        outs, scratch = [bf(deep_a, 256)] * 2 + [bf(deep_b, 256)] * 2, [vm(2, deep_a, 128), vm(2, deep_b, 128)]
        return call(kernel, outs, args, scratch)

    def late_rims(after):
        late, _ = lax.optimization_barrier((edges[0], after))
        late = beside(late, partner_b, range(turning))
        args = (near_a, near_b, late)
        return late, rim_call(functools.partial(pull_rim_kernel, turning), 1, 2, args)

    pull_rims = None
    if turn:
        turn_rims = rim_call(functools.partial(rim_kernel, turning), RIM_A, RIM_B, (far_b, near_a))

    meta = jnp.zeros((2 * COLS, 128), F32)
    main, edge_a, edge_b = panels_in, near_a[96:128], near_b[32:64]
    stages = 2 * owners
    owner_of = [k if k < owners else stages - 1 - k for k in range(stages)]
    kept, result, k = [], None, 0
    record = ROWS * (own // 128 + 1)
    while k < stages:
        owner, slot, turned, sums = owner_of[k], k % GROUP, False, []
        turns_here, turns_next = turn and k == owners - 1, turn and k + 1 == owners - 1
        if turns_here:
            first, main, send_b = call(
                functools.partial(turn_kernel, nb, owner, slot),
                [f32(ROWS, own), f32(record + 2 * COLS, 128), f32(ROWS, 128)],
                (edge_b, main, edge_a, *own_tiles, *turn_rims, meta, expand),
            )
            kept += [first, main]
            turned = True
            meta = main[record:]
            k += 2
        else:
            if k < owners:
                main, send_b, send_a = call(
                    functools.partial(push_kernel, nb, owner),
                    [f32(ROWS, own)] + [f32(ROWS, w) for w in ((256, 384) if turns_next else (128, 128))],
                    (edge_b, main, edge_a, near_b, near_a, *own_tiles, *([late_b] if k else [])),
                    [vm(2, 2 * BLOCK, 128)],
                    flops=PUSH,
                )
                if pull_rims is None:
                    late_b, pull_rims = late_rims(send_b)
                (meta,) = call(
                    functools.partial(note_kernel, nb, owner, slot),
                    [f32(2 * COLS, 128)],
                    (main, meta, expand),
                )
            else:
                ends = (k + 1) % GROUP == 0 or k + 1 == stages
                main, meta, *sums = call(
                    functools.partial(pull_kernel, nb, owner, slot),
                    [f32(ROWS, own), f32(2 * COLS, 128)] + [f32(count, COLS, 128)] * ends,
                    (edge_b, main, edge_a, *own_tiles, *pull_rims, meta, expand),
                )
                send_b, send_a = edges_of(main, 128, 128)
            kept.append(main)
            k += 1
        share = not (turns_next and slot == 0)

        if k % GROUP == 0 or k == stages:
            todo = [(owner_of[i], i < owners) for i in range(k - len(kept), k)]
            every = sums[0] if sums else jnp.broadcast_to(meta[None, :COLS], (count, COLS, 128))
            grams = lax.all_to_all(every, "space", 0, 0)
            pair = call(
                functools.partial(scale_kernel, todo, count * own), [f32(ROWS, own)] * 2, (grams, meta, *kept)
            )
            if result is None:
                result = pair
            else:
                live = [
                    functools.reduce(jnp.logical_or, [me == o for o, f in todo if f == way], jnp.bool_(False))
                    for way in (True, False)
                ]
                result = [jnp.where(c, new, old) for c, new, old in zip(live, pair, result)]
            main = pair[0 if k - 1 < owners else 1]
            send_b, send_a = edges_of(main, *((256, 384) if turn and k == owners - 1 else (128, 128)))
            meta, kept, share, turned = jnp.zeros((2 * COLS, 128), F32), [], False, False
        if k == stages:
            break

        before, after = owner_of[k - 1], owner_of[k]
        if after != before:
            main = hop(main, before, after, lambda s: s)
        into_turn = turn and k == owners - 1
        (edge_b,) = call(
            aside_kernel,
            [f32(*send_b.shape)],
            (hop(send_b, before, after, partner_b),) + ((turn_rims[0],) if into_turn else ()),
            flops=ASIDE_1 if into_turn else ASIDE_2,
        )
        if turned:
            edge_a = main[record - ROWS : record]
            meta = meta + main[record:]
        else:
            edge_a = hop(send_a, before, after, partner_a)
            if share and after != before:
                meta = meta + hop(meta, before, after, lambda s: s)
    return result[0][None], result[1][None]


def solution(mesh):
    return jax.shard_map(
        shards,
        mesh=mesh,
        in_specs=(
            P(None, "space"),
            P("tm", "space", None, None),
            P("tm", "space", None),
            P("tm", None, None, None),
        ),
        out_specs=(P("tm", None, "space"), P("tm", None, "space")),
        check_vma=False,
    )
```

```python
import functools

import jax
import jax.numpy as jnp
from jax import lax
from jax.experimental import pallas as pl
from jax.experimental.pallas import tpu as pltpu
from jax.sharding import PartitionSpec as P

BLOCK = 64
COLS = 8
PANELS = 4
ROWS = COLS * PANELS
RUN = 2
GROUP = 4
RIM_A, RIM_B = 5, 4
FAR_A, FAR_B = 3, 2
PUSH = 3 * 10**9
ASIDE_0 = 10**10
ASIDE_1, ASIDE_2 = 7 * 10**8, 5 * 10**8
DOWN = 2.0**-16
BF = jnp.bfloat16
F32 = jnp.float32
HIGH = lax.Precision.HIGHEST
NT = (((1,), (1,)), ((), ()))
NN = (((1,), (0,)), ((), ()))
TN = (((0,), (0,)), ((), ()))
VM = pl.BlockSpec(memory_space=pltpu.VMEM)


def call(kernel, outs, args, scratch=(), flops=10**6, far=0, limit=12):
    shapes = [jax.ShapeDtypeStruct(shape, dtype) for shape, dtype in outs]
    return pl.pallas_call(
        kernel,
        out_shape=shapes,
        in_specs=[pl.BlockSpec(memory_space=pltpu.HBM)] * far + [VM] * (len(args) - far),
        out_specs=[VM] * len(outs),
        scratch_shapes=list(scratch),
        compiler_params=pltpu.CompilerParams(vmem_limit_bytes=limit << 20),
        cost_estimate=pl.CostEstimate(flops=flops, bytes_accessed=10**5, transcendentals=0),
    )(*args)


def inside():
    place, last = lax.axis_index("space"), lax.axis_size("space") - 1
    return jnp.where((place == 0) | (place == last), 0.0, 1.0).astype(F32)


def parity():
    return lax.rem(lax.axis_index("space"), 2)


def iota(shape, dim):
    return lax.broadcasted_iota(jnp.int32, shape, dim)


def presence(mask, t, j, nb):
    place, last = lax.axis_index("space"), lax.axis_size("space") - 1
    here = jnp.broadcast_to(mask[j, t : t + 1, :], (nb, nb))
    diagonal = iota((nb, nb), 0) == iota((nb, nb), 1)
    column = jnp.sum(jnp.where(diagonal, here, 0), axis=1, keepdims=True).astype(F32)
    if j == 0:
        column = jnp.where((iota((nb, 1), 0) == 0) & (place == 0), 0.0, column)
    if j == 2:
        column = jnp.where((iota((nb, 1), 0) == nb - 1) & (place == last), 0.0, column)
    return column


def first_kernel(out):
    out[...] = jnp.zeros_like(out)


def block_of(blocks, column, t, j, b, nb):
    return blocks[t, j, pl.ds(b, BLOCK // 2, stride=nb), :] * column[t][j][b : b + 1, :]


def edge_kernel(nb, turning, _, blocks, mask, panels, near_b, late_b, to_a, *far_b):
    width = panels.shape[1]
    turns = lax.axis_index("tm") == turning
    column = [[presence(mask, t, j, nb) for j in range(3)] for t in range(RUN)]

    def near(dst, later, at, low_side, keep=1.0):
        edge = 0 if low_side else nb - 1
        inner = 1 if low_side else nb - 2
        for j in range(3):
            dst[j * 32 : (j + 1) * 32, :] = block_of(blocks, column, 0, j, edge, nb) * keep
        dst[96:128, :] = panels[:, :128] if low_side else panels[:, width - 128 :]
        rest = [(edge, 0), (edge, 1), (inner, 0)] if low_side else [(inner, 2), (edge, 1), (edge, 2)]
        for i, (b, j) in enumerate(rest):
            later[at + i * 32 : at + (i + 1) * 32, :] = block_of(blocks, column, 1, j, b, nb) * keep

    def far(dst, deep_a, deep_b, low_side, keep=1.0):
        at = 0
        for t, deep in ((0, deep_a), (1, deep_b)):
            for b in range(deep) if low_side else range(nb - deep, nb):
                for j in range(3):
                    dst[at : at + 32, :] = block_of(blocks, column, t, j, b, nb) * keep
                    at += 32

    for side in range(2):

        @pl.when((parity() == side) & jnp.logical_not(turns))
        def _():
            near(near_b, late_b, 0, side == 0, inside())
            near(to_a, to_a, 128, side == 1)

        if far_b:

            @pl.when((parity() == side) & turns)
            def _():
                far(far_b[0], FAR_A, FAR_B, side == 0, inside())
                far(to_a, RIM_A, RIM_B, side == 1)


def banded(y, p):
    low = iota(y[0].shape, 1) < BLOCK
    zero = jnp.zeros_like(y[0])
    turned = [pltpu.roll(v, BLOCK, 1) for v in y]
    at_low, at_high = (y, turned) if p == 0 else (turned, y)
    first = (jnp.where(low, at_low[0], at_high[1]), jnp.where(low, at_low[2], zero))
    second = (jnp.where(low, zero, at_high[0]), jnp.where(low, at_low[1], at_high[2]))
    return first, second


def split2(x):
    high = x.astype(BF)
    return high, (x - high.astype(F32)).astype(BF)


def split3(x):
    first = x.astype(BF)
    x = x - first.astype(F32)
    second = x.astype(BF)
    return first, second, (x - second.astype(F32)).astype(BF)


def split_halves(wide, at, hi, lo):
    for half in range(2):
        lanes = slice(half * 128, half * 128 + 128)
        hi[:, lanes], lo[:, lanes] = split2(wide[at + half])


def own_kernel(nb, blocks, mask, mixing, a_hi, a_lo, b_hi, b_lo, expand, *wide):
    column = [[presence(mask, t, j, nb) for j in range(3)] for t in range(RUN)]
    for t, hi, lo in ((0, a_hi, a_lo), (1, b_hi, b_lo)):
        for b in range(nb):
            rim_row(wide[t], b, b % 2 == 1 - t, [block_of(blocks, column, t, j, b, nb) for j in range(3)])
        split_halves(wide[t], 0, hi, lo)
    pick = (lax.rem(iota((COLS, 128), 1), COLS) == iota((COLS, 128), 0)).astype(F32)
    row, lane = iota((ROWS, 128), 0), lax.rem(iota((ROWS, 128), 1), ROWS)
    same = (row // COLS) == (lane // COLS)
    step = []
    for t in range(RUN):
        m = mixing[t].reshape(ROWS, COLS)
        spread = lax.dot_general(m, pick, NN, precision=HIGH, preferred_element_type=F32)
        step.append((row == lane).astype(F32) - jnp.where(same, spread, 0.0))
    for i, (x, y) in enumerate(((step[0], step[1]), (step[1], step[0]))):
        e = lax.dot_general(x[:, :ROWS], y, NN, precision=HIGH, preferred_element_type=F32)
        expand[i * COLS : (i + 1) * COLS, :] = (
            e[0:COLS] + e[COLS : 2 * COLS] + e[2 * COLS : 3 * COLS] + e[3 * COLS :]
        )


def taken(from_a, from_b, left, at_a, at_b=None):
    use_b = (parity() == 0) == left
    at_b = at_a if at_b is None else at_b
    return jnp.where(use_b, from_b[at_b : at_b + 32, :], from_a[at_a : at_a + 32, :])


def rim_row(dst, index, first, y):
    for p in range(2):
        tiles = banded(y, p)[0 if first else 1]
        for half in range(2):
            dst[half, pl.ds(index * BLOCK + p, 32, stride=2), :] = tiles[half]


def edge_rows(near_a, near_b, dst):
    for left in (True, False):
        rim_row(dst, 1 - left, left, [taken(near_a, near_b, left, j * 32) for j in range(3)])


def rim_kernel(turning, far_b, far_a, a_hi, a_lo, b_hi, b_lo, wide_a, wide_b):
    none = jnp.zeros((32, 128), F32)

    @pl.when(lax.axis_index("tm") == turning)
    def _():
        for dst, deep, start_a, wide, start_b, odd in (
            (wide_a, RIM_A, 0, FAR_A, 0, 1),
            (wide_b, RIM_B, 96 * RIM_A, FAR_B, 96 * FAR_A, 0),
        ):
            for i in range(deep):
                for left in (True, False):
                    k = i - (deep - wide) if left else i
                    y = []
                    for j in range(3):
                        n, m = start_a + i * 96 + j * 32, start_b + k * 96 + j * 32
                        from_b = far_b[m : m + 32, :] if 0 <= k < wide else none
                        y.append(jnp.where((parity() == 0) == left, from_b, far_a[n : n + 32, :]))
                    place = i - deep if left else i
                    rim_row(dst, i if left else deep + i, place % 2 == odd, y)
        split_halves(wide_a, 0, a_hi, a_lo)
        split_halves(wide_b, 0, b_hi, b_lo)


def pull_rim_kernel(turning, near_a, near_b, late_b, a_hi, a_lo, b_hi, b_lo, wide_a, wide_b):
    @pl.when(lax.axis_index("tm") != turning)
    def _():
        edge_rows(near_a, near_b, wide_a)
        none = jnp.zeros((32, 128), F32)
        left = [taken(near_a, late_b, True, 128 + i * 32, i * 32) for i in range(3)]
        right = [taken(near_a, late_b, False, 128 + i * 32, i * 32) for i in range(3)]
        rim_row(wide_b, 0, True, [none, none, left[0]])
        rim_row(wide_b, 1, False, [none, left[1], left[2]])
        rim_row(wide_b, 2, True, [right[0], right[1], none])
        rim_row(wide_b, 3, False, [right[2], none, none])
        split_halves(wide_a, 0, a_hi, a_lo)
        split_halves(wide_b, 0, b_hi, b_lo)


def pair_tile(own, rim, depth, nb, b):
    def row(k):
        if 0 <= k < nb:
            return own[k * BLOCK : (k + 1) * BLOCK, :]
        k = k + depth if k < 0 else depth + k - nb
        return rim[k * BLOCK : (k + 1) * BLOCK, :]

    return jnp.concatenate([row(b), row(b + 1)], axis=0)


def pieces_sum(o, m, n, skip=0):
    rows, cols = o.shape[0] // m, o.shape[1] // n
    order = sorted(((i, j) for i in range(rows) for j in range(cols)), key=lambda p: -sum(p))
    total = None
    for i, j in order[skip:]:
        piece = o[i * m : (i + 1) * m, j * n : (j + 1) * n]
        total = piece if total is None else total + piece
    return total


def product(x, w, dims):
    o = lax.dot_general(x, w, dims, preferred_element_type=F32)
    return pieces_sum(o, ROWS, 128)


def push(v, tiles):
    x = jnp.concatenate(split3(v), axis=0)
    outs = []
    for i, (hi, lo) in enumerate(tiles):
        outs.append(product(x[:, i * 128 : i * 128 + 256], jnp.concatenate([hi, lo], axis=0), NT))
    return jnp.concatenate(outs, axis=1)


def pull(v, tiles):
    x = jnp.concatenate(split3(v), axis=0)
    outs = []
    for i in range(len(tiles) - 1):
        parts = [
            jnp.concatenate([tiles[i][s][:, 128:], tiles[i + 1][s][:, :128]], axis=0) for s in range(2)
        ]
        outs.append(product(x[:, i * 128 : i * 128 + 256], jnp.concatenate(parts, axis=1), NN))
    return jnp.concatenate(outs, axis=1)


def tiles_of(refs, depth, nb, first, last):
    own_hi, own_lo, rim_hi, rim_lo = refs
    return [
        (pair_tile(own_hi, rim_hi, depth, nb, b), pair_tile(own_lo, rim_lo, depth, nb, b))
        for b in range(first, last, 2)
    ]


def gram(u):
    first = lax.rem(iota(u.shape, 0), COLS) == 0
    parts = split3(u - jnp.where(first, 0.0, pltpu.roll(u, 1, 0)))
    wide = jnp.concatenate([x for x in parts for _ in range(4)], axis=0)
    o = lax.dot_general(jnp.concatenate(parts, axis=0), wide, NT, preferred_element_type=F32)
    total = pieces_sum(o, ROWS, 128)
    panel = lax.rem(iota((COLS, 128), 1), ROWS) // COLS
    out = jnp.zeros((COLS, 128), F32)
    for p in range(PANELS):
        out = out + jnp.where(panel == p, total[p * COLS : (p + 1) * COLS], 0.0)
    return out


def noted(g, e, slot, new_g, new_e):
    mine = (iota((COLS, 128), 1) // ROWS) == slot
    return jnp.where(mine, new_g, g), jnp.where(mine, new_e, e)


def panels_of(ref, own):
    if ref.shape[0] == ROWS:
        return ref[:, :own]
    return jnp.concatenate([ref[i * ROWS : (i + 1) * ROWS, :] for i in range(own // 128)], axis=1)


def by_side(e_a, e_b):
    even = parity() == 0
    return jnp.where(even, e_b, e_a), jnp.where(even, e_a, e_b)


def aside_kernel(edge, *refs):
    refs[-1][...] = edge[...]


def push_kernel(nb, owner, edge_b, main, edge_a, near_b, near_a, a_hi, a_lo, b_hi, b_lo, out, out_b, out_a, wide):
    own = nb * BLOCK

    @pl.when(lax.axis_index("tm") == owner)
    def _():
        edge_rows(near_a, near_b, wide)
        rim_hi, rim_lo = split2(jnp.concatenate([wide[0], wide[1]], axis=1))
        left, right = by_side(edge_a[...], edge_b[...])
        v = jnp.concatenate([left, main[:, :own], right], axis=1)
        w = push(v, tiles_of((a_hi, a_lo, rim_hi, rim_lo), 1, nb, -1, nb))
        u = push(w, tiles_of((b_hi, b_lo, None, None), 0, nb, 0, nb))
        out[...] = u
        wide_b, wide_a = out_b.shape[1], out_a.shape[1]
        out_b[...] = by_side(u[:, :wide_b], u[:, own - wide_b :])[1]
        out_a[...] = by_side(u[:, own - wide_a :], u[:, :wide_a])[1]


def turn_kernel(nb, owner, slot, edge_b, main, edge_a, a_hi, a_lo, b_hi, b_lo, ra_hi, ra_lo, rb_hi, rb_lo,
                old, expand, first, out, out_b):
    own = nb * BLOCK
    pieces = own // 128
    record = slice((pieces + 1) * ROWS, (pieces + 1) * ROWS + 2 * COLS)

    @pl.when(lax.axis_index("tm") != owner)
    def _():
        out[record, :] = old[...]

    def turn(low, edges):
        a0, a1 = (RIM_A, FAR_A) if low else (FAR_A, RIM_A)
        b0, b1 = (RIM_B, FAR_B) if low else (FAR_B, RIM_B)
        v = jnp.concatenate([edges[0], main[:, :own], edges[1]], axis=1)
        tiles_a = tiles_of((a_hi, a_lo, ra_hi, ra_lo), RIM_A, nb, -a0, nb + a1)
        tiles_b = tiles_of((b_hi, b_lo, rb_hi, rb_lo), RIM_B, nb, -b0, nb + b1)
        u = push(push(v, tiles_a), tiles_b)
        u_own = u[:, b0 * BLOCK : b0 * BLOCK + own]
        first[...] = u_own
        back = pull(pull(u * DOWN, tiles_b), tiles_a[1:-1])
        back_own, beyond = (back[:, 128:], back[:, :128]) if low else (back[:, :own], back[:, own:])
        for i in range(pieces):
            out[i * ROWS : (i + 1) * ROWS, :] = back_own[:, i * 128 : (i + 1) * 128]
        out[pieces * ROWS : (pieces + 1) * ROWS, :] = beyond
        out_b[...] = back_own[:, own - 128 :] if low else back_own[:, :128]
        g, e = noted(old[:COLS], old[COLS:], slot, gram(u_own), expand[:COLS])
        g, e = noted(g, e, slot + 1, gram(back_own), expand[COLS:] * (1.0 / DOWN))
        out[record, :] = jnp.concatenate([g, e], axis=0)

    mine = lax.axis_index("tm") == owner
    pl.when(mine & (parity() == 0))(lambda: turn(False, (edge_b[...], edge_a[...])))
    pl.when(mine & (parity() == 1))(lambda: turn(True, (edge_a[...], edge_b[...])))


def pull_kernel(nb, owner, slot, edge_b, main, edge_a, a_hi, a_lo, b_hi, b_lo, ra_hi, ra_lo, rb_hi, rb_lo,
                old, expand, out, record, *every):
    own = nb * BLOCK

    @pl.when(lax.axis_index("tm") != owner)
    def _():
        record[...] = old[...]

    @pl.when(lax.axis_index("tm") == owner)
    def _():
        left, right = by_side(edge_a[...], edge_b[...])
        v = jnp.concatenate([left, panels_of(main, own), right], axis=1)
        y = pull(v, tiles_of((b_hi, b_lo, rb_hi, rb_lo), 2, nb, -2, nb + 2))
        u = pull(y, tiles_of((a_hi, a_lo, ra_hi, ra_lo), 1, nb, -1, nb + 1))
        out[...] = u
        record[:COLS], record[COLS:] = noted(old[:COLS], old[COLS:], slot, gram(u), expand[COLS:])

    for ref in every:
        for i in range(ref.shape[0]):
            ref[i] = record[:COLS]


def note_kernel(nb, owner, slot, u, old, expand, out):
    @pl.when(lax.axis_index("tm") != owner)
    def _():
        out[...] = old[...]

    @pl.when(lax.axis_index("tm") == owner)
    def _():
        out[:COLS], out[COLS:] = noted(old[:COLS], old[COLS:], slot, gram(u[:, : nb * BLOCK]), expand[:COLS])


def exact(x, y):
    rows = x.shape[0]
    m = -(-rows // 16) * 16
    if m > rows:
        x = jnp.concatenate([x, jnp.zeros((m - rows, x.shape[1]), F32)], axis=0)
    o = lax.dot_general(
        jnp.concatenate(split3(x), axis=0), jnp.concatenate(split3(y), axis=1), NN, preferred_element_type=F32
    )
    return pieces_sum(o, m, 128, 3)[:rows]


def scale_kernel(stages, boxes, grams, meta, *refs):
    panels, (out_f, out_a) = refs[: len(stages)], refs[len(stages) :]
    own = out_f.shape[1]
    parts = [grams[i] for i in range(grams.shape[0])]
    while len(parts) > 1:
        parts = [a + b for a, b in zip(parts[::2], parts[1::2])] + parts[len(parts) // 2 * 2 :]
    total = parts[0] * (1.0 / boxes)
    growth = meta[COLS:, :]
    row, lane = iota((ROWS, 128), 0), iota((ROWS, 128), 1)
    same = (row // COLS) == (lax.rem(lane, ROWS) // COLS)
    group = lane[:COLS] // ROWS
    me = lax.axis_index("tm")

    def spread(x, n):
        turns = [x if k == n else pltpu.roll(x, ((k - n) % 4) * ROWS, 1) for k in range(4)]
        out = turns[0]
        for k in range(1, 4):
            out = jnp.where(group == k, turns[k], out)
        return out

    def full(x):
        return jnp.where(same, jnp.concatenate([x] * PANELS, axis=0), 0.0)

    count = len(stages)
    grow = [spread(growth, n) for n in range(count)]
    sums = [grow[0][COLS - 1 :]]
    for i in range(COLS - 2, -1, -1):
        sums.insert(0, sums[0] + grow[0][i : i + 1])
    sums = jnp.concatenate(sums, axis=0)
    products = jnp.concatenate([spread(total, n)[:, :ROWS] for n in range(count)], axis=0)
    stack = jnp.concatenate([grow[0], sums, exact(products, full(sums))], axis=0)
    select = {True: None, False: None}
    for n, (owner, forward) in enumerate(stages):
        if n:
            stack = exact(stack[:, :ROWS], full(grow[n]))
        square = jnp.sum(stack[COLS : 2 * COLS] * stack[2 * COLS : 3 * COLS], axis=0, keepdims=True)
        scale = lax.rsqrt(jnp.maximum(square, 0.0) + 1e-06)
        later = [stack[3 * COLS :]] if n + 1 < count else []
        stack = jnp.concatenate([stack[: 2 * COLS]] + later, axis=0) * scale
        back, u = stack[:COLS], panels_of(panels[n], own)
        old = select[forward]
        select[forward] = (back, u) if old is None else (
            jnp.where(me == owner, back, old[0]), jnp.where(me == owner, u, old[1])
        )
    for forward, out in ((True, out_f), (False, out_a)):
        if select[forward] is None:
            out[...] = jnp.zeros_like(out)
        else:
            back, u = select[forward]
            left = jnp.concatenate(split3(full(back)[:, :ROWS].T), axis=0)
            total = None
            for i, part in reversed(list(enumerate(split3(u)))):
                o = lax.dot_general(left[: (3 - i) * ROWS], part, NN, preferred_element_type=F32)
                piece = pieces_sum(o, ROWS, own)
                total = piece if total is None else total + piece
            out[...] = total


def shards(panels_in, blocks, block_mask, mixing):
    owners, count = lax.axis_size("tm"), lax.axis_size("space")
    me, place = lax.axis_index("tm"), lax.axis_index("space")
    nb, own = blocks.shape[1], panels_in.shape[1]
    even = lax.rem(place, 2) == 0
    bf, f32 = (lambda *s: (s, BF)), (lambda *s: (s, F32))

    def partner_a(s):
        return s ^ 1

    def partner_b(s):
        t = s + 1 if s % 2 else s - 1
        return t if 0 <= t < count else s

    def beside(x, to, only=None):
        route = [(t * count + s, t * count + to(s)) for t in (only or range(owners)) for s in range(count)]
        return lax.ppermute(x, ("tm", "space"), route)

    def hop(x, t, o, to):
        pairs = [(t, o), (o, t)] if t != o else [(t, t)]
        return lax.ppermute(x, ("tm", "space"), [(i * count + s, k * count + to(s)) for i, k in pairs for s in range(count)])

    def edges_of(x, wide_b, wide_a):
        return (
            jnp.where(even, x[:, :wide_b], x[:, own - wide_b : own]),
            jnp.where(even, x[:, own - wide_a : own], x[:, :wide_a]),
        )

    rows = blocks.reshape(RUN, nb, 3, BLOCK // 2, 2 * BLOCK).transpose(0, 2, 3, 1, 4)
    rows, mask = rows.reshape(RUN, 3, BLOCK // 2 * nb, 2 * BLOCK), block_mask.transpose(2, 0, 1)
    vm = lambda *s: pltpu.VMEM(s, F32)
    turn = owners % GROUP != 0
    turning = owners - 1 if turn else owners
    begin = call(first_kernel, [f32(8, 128)], (), flops=10**9)
    sizes = [128, 96] + ([96 * (RIM_A + RIM_B), 96 * (FAR_A + FAR_B)] if turn else [224])
    edges = call(
        functools.partial(edge_kernel, nb, turning),
        [f32(n, 128) for n in sizes],
        (*begin, rows, mask, panels_in),
    )
    near_b, near_a = beside(edges[0], partner_b, range(turning)), beside(edges[2], partner_a)
    (near_b,) = call(aside_kernel, [f32(*near_b.shape)], (near_b,), flops=ASIDE_0)
    if turn:
        far_b = beside(edges[3], partner_b, [turning])
    rows, mask, mixing, _ = lax.optimization_barrier((rows, mask, mixing, edges))
    *own_tiles, expand = call(
        functools.partial(own_kernel, nb),
        [bf(own, 256)] * 4 + [f32(2 * COLS, 128)],
        (rows, mask, mixing),
        [vm(2, own, 128)] * RUN,
    )

    def rim_call(kernel, deep_a, deep_b, args):
        deep_a, deep_b = 2 * deep_a * BLOCK, 2 * deep_b * BLOCK
        outs, scratch = [bf(deep_a, 256)] * 2 + [bf(deep_b, 256)] * 2, [vm(2, deep_a, 128), vm(2, deep_b, 128)]
        return call(kernel, outs, args, scratch)

    def late_rims(after):
        late, _ = lax.optimization_barrier((edges[1], after))
        args = (near_a, near_b, beside(late, partner_b, range(turning)))
        return rim_call(functools.partial(pull_rim_kernel, turning), 1, 2, args)

    pull_rims = None
    if turn:
        turn_rims = rim_call(functools.partial(rim_kernel, turning), RIM_A, RIM_B, (far_b, near_a))

    meta = jnp.zeros((2 * COLS, 128), F32)
    main, edge_a, edge_b = panels_in, near_a[96:128], near_b[96:128]
    stages = 2 * owners
    owner_of = [k if k < owners else stages - 1 - k for k in range(stages)]
    kept, result, k = [], None, 0
    record = ROWS * (own // 128 + 1)
    while k < stages:
        owner, slot, turned, sums = owner_of[k], k % GROUP, False, []
        turns_here, turns_next = turn and k == owners - 1, turn and k + 1 == owners - 1
        if turns_here:
            first, main, send_b = call(
                functools.partial(turn_kernel, nb, owner, slot),
                [f32(ROWS, own), f32(record + 2 * COLS, 128), f32(ROWS, 128)],
                (edge_b, main, edge_a, *own_tiles, *turn_rims, meta, expand),
            )
            kept += [first, main]
            turned = True
            meta = main[record:]
            k += 2
        else:
            if k < owners:
                main, send_b, send_a = call(
                    functools.partial(push_kernel, nb, owner),
                    [f32(ROWS, own)] + [f32(ROWS, w) for w in ((256, 384) if turns_next else (128, 128))],
                    (edge_b, main, edge_a, near_b, near_a, *own_tiles),
                    [vm(2, 2 * BLOCK, 128)],
                    flops=PUSH,
                )
                if pull_rims is None:
                    pull_rims = late_rims(send_b)
                (meta,) = call(
                    functools.partial(note_kernel, nb, owner, slot),
                    [f32(2 * COLS, 128)],
                    (main, meta, expand),
                )
            else:
                ends = (k + 1) % GROUP == 0 or k + 1 == stages
                main, meta, *sums = call(
                    functools.partial(pull_kernel, nb, owner, slot),
                    [f32(ROWS, own), f32(2 * COLS, 128)] + [f32(count, COLS, 128)] * ends,
                    (edge_b, main, edge_a, *own_tiles, *pull_rims, meta, expand),
                )
                send_b, send_a = edges_of(main, 128, 128)
            kept.append(main)
            k += 1
        share = not (turns_next and slot == 0)

        if k % GROUP == 0 or k == stages:
            todo = [(owner_of[i], i < owners) for i in range(k - len(kept), k)]
            every = sums[0] if sums else jnp.broadcast_to(meta[None, :COLS], (count, COLS, 128))
            grams = lax.all_to_all(every, "space", 0, 0)
            pair = call(
                functools.partial(scale_kernel, todo, count * own), [f32(ROWS, own)] * 2, (grams, meta, *kept)
            )
            if result is None:
                result = pair
            else:
                live = [
                    functools.reduce(jnp.logical_or, [me == o for o, f in todo if f == way], jnp.bool_(False))
                    for way in (True, False)
                ]
                result = [jnp.where(c, new, old) for c, new, old in zip(live, pair, result)]
            main = pair[0 if k - 1 < owners else 1]
            send_b, send_a = edges_of(main, *((256, 384) if turn and k == owners - 1 else (128, 128)))
            meta, kept, share, turned = jnp.zeros((2 * COLS, 128), F32), [], False, False
        if k == stages:
            break

        before, after = owner_of[k - 1], owner_of[k]
        if after != before:
            main = hop(main, before, after, lambda s: s)
        into_turn = turn and k == owners - 1
        (edge_b,) = call(
            aside_kernel,
            [f32(*send_b.shape)],
            (hop(send_b, before, after, partner_b),) + ((turn_rims[0],) if into_turn else ()),
            flops=ASIDE_1 if into_turn else ASIDE_2,
        )
        if turned:
            edge_a = main[record - ROWS : record]
            meta = meta + main[record:]
        else:
            edge_a = hop(send_a, before, after, partner_a)
            if share and after != before:
                meta = meta + hop(meta, before, after, lambda s: s)
    return result[0][None], result[1][None]


def solution(mesh):
    return jax.shard_map(
        shards,
        mesh=mesh,
        in_specs=(
            P(None, "space"),
            P("tm", "space", None, None),
            P("tm", "space", None),
            P("tm", None, None, None),
        ),
        out_specs=(P("tm", None, "space"), P("tm", None, "space")),
        check_vma=False,
    )
```
